128 devices in a mesh: gx: 4 (over y), gy: 4 (over x), gz: 8 (over z, core).
Axes of the slice: x: 4, y: 4, z: 4, core: 2. Of those that a mesh axis runs over, the one named last changes fastest.
Arguments:
- image: float32 [64, 256, 1024], P('gx', 'gy', 'gz'), may hold values from 0 to 1
- labels: int32 [64, 256, 1024], P('gx', 'gy', 'gz'), may hold values from 0 to 2, as said below
Outputs:
- potential: float32 [64, 256, 1024], P('gx', 'gy', 'gz')
The draws below stay inside these ranges and needn't reach their ends.
Inputs may be any that keep to these rules, and one draw needn't show every extreme that they name: `labels`: 0 marks a background seed, 1 a foreground seed, 2 an unlabeled voxel.
All inputs are finite; a program needn't handle non-finite values.
Results may differ from the reference program's by a relative error of at most 0.0001.
Values sent between devices are 32-bit elements; how exact they have to be, the bound alone decides.
A program may use at most 128 MiB of HBM per device.

```python
import jax
import jax.numpy as jnp
from jax import lax

SMOOTH_STEPS = 3
COARSE_STEPS = 6
NX = 64
NY = 256
NZ = 1024


def draw_labels(key, part):
    key = jax.random.fold_in(key, 7)
    score = jax.random.randint(key, (NX, NY, NZ), 0, 1000)
    return jnp.where(score < 5, 1, jnp.where(score < 10, 0, 2)).astype(jnp.int32)


def levels(own_key, extent, shards, low, largest):
    def one(dim, parts):
        heights = jax.random.uniform(jax.random.fold_in(jax.random.fold_in(own_key, 6), dim), (parts,), jnp.float32, low / len(shards), largest / len(shards))
        return jnp.repeat(jnp.exp(heights), extent[dim] // parts).reshape((-1,) + (1,) * (len(extent) - dim - 1))

    level = one(*shards[0])
    for cut in shards[1:]:
        level = level * one(*cut)
    return level


def setup_inputs(seed: int = 0) -> dict:
    seeds = jax.random.split(jax.random.key(seed), 3)
    image = jnp.clip(1.0 * jax.random.uniform(seeds[0], (NX, NY, NZ), jnp.float32) ** levels(seeds[0], (NX, NY, NZ), ((0, 4), (1, 4), (2, 8)), -0.2, 0.2), 0.0, 1.0)
    labels = draw_labels(jax.random.fold_in(seeds[2], 71), 0)
    return dict(image=image, labels=labels)


HEAT_CONSTANT = 0.25
CONTRAST = 0.5
SCREENING = 0.002
SEED_WEIGHT = 1.0
THETA = 1.1
DELTA = 0.9


def soft_gradient(padded):
    central_voxel = padded[1:-1, 1:-1, 1:-1]
    beside_all = [padded[:-2, 1:-1, 1:-1], padded[2:, 1:-1, 1:-1], padded[1:-1, :-2, 1:-1],
              padded[1:-1, 2:, 1:-1], padded[1:-1, 1:-1, :-2], padded[1:-1, 1:-1, 2:]]
    expand_region = jnp.exp(central_voxel / HEAT_CONSTANT)
    contract_region = jnp.exp(-central_voxel / HEAT_CONSTANT)
    for remaining_part in beside_all:
        expand_region = expand_region + jnp.exp(remaining_part / HEAT_CONSTANT)
        contract_region = contract_region + jnp.exp(-remaining_part / HEAT_CONSTANT)
    return HEAT_CONSTANT * jnp.log(expand_region) + HEAT_CONSTANT * jnp.log(contract_region)


def face_weights(grad):
    medium_level = grad[1:-1, 1:-1, 1:-1]
    return (jnp.exp(-CONTRAST * (medium_level + grad[:-2, 1:-1, 1:-1])),
            jnp.exp(-CONTRAST * (medium_level + grad[2:, 1:-1, 1:-1])),
            jnp.exp(-CONTRAST * (medium_level + grad[1:-1, :-2, 1:-1])),
            jnp.exp(-CONTRAST * (medium_level + grad[1:-1, 2:, 1:-1])),
            jnp.exp(-CONTRAST * (medium_level + grad[1:-1, 1:-1, :-2])),
            jnp.exp(-CONTRAST * (medium_level + grad[1:-1, 1:-1, 2:])))


def pair_sum(arr, dims):
    for axis_dim in dims:
        shape = arr.shape
        arr = arr.reshape(shape[:axis_dim] + (shape[axis_dim] // 2, 2) + shape[axis_dim + 1:]).sum(axis_dim + 1)
    return arr


def restrict_cells(arr):
    return pair_sum(arr, (0, 1, 2))


def coarsen_face_weights(faces):
    result = []
    for axis_dim in range(3):
        others = tuple(d for d in range(3) if d != axis_dim)
        for start in range(2):
            arr = faces[2 * axis_dim + start]
            picked = lax.slice_in_dim(arr, start, arr.shape[axis_dim], 2, axis_dim)
            result.append(pair_sum(picked, others))
    return tuple(result)


def prolong(arr):
    return jnp.repeat(jnp.repeat(jnp.repeat(arr, 2, 0), 2, 1), 2, 2)


def diagonal(cells, faces):
    total = cells
    for face in faces:
        total = total + face
    return total


def apply_operator(field, padded, diag, faces):
    return diag * field - (faces[0] * padded[:-2, 1:-1, 1:-1] + faces[1] * padded[2:, 1:-1, 1:-1]
                           + faces[2] * padded[1:-1, :-2, 1:-1] + faces[3] * padded[1:-1, 2:, 1:-1]
                           + faces[4] * padded[1:-1, 1:-1, :-2] + faces[5] * padded[1:-1, 1:-1, 2:])


def chebyshev(operate, inverse, rhs, field, steps):
    sigma = THETA / DELTA
    if field is None:
        resid = rhs
        field = jnp.zeros_like(rhs)
    else:
        resid = rhs - operate(field)
    update = inverse * resid / THETA
    field = field + update
    rho = 1.0 / sigma
    for step in range(steps - 1):
        resid = rhs - operate(field)
        rho_new = 1.0 / (2.0 * sigma - rho)
        update = rho_new * rho * update + (2.0 * rho_new / DELTA) * inverse * resid
        field = field + update
        rho = rho_new
    return field


def level_operator(diag, faces):
    def operate(field):
        return apply_operator(field, jnp.pad(field, 1), diag, faces)
    return operate


def reference(image, labels):
    grad = soft_gradient(jnp.pad(image, 2))
    faces = face_weights(grad)
    cells = SCREENING + SEED_WEIGHT * (labels != 2).astype(jnp.float32)
    rhs = SEED_WEIGHT * (labels == 1).astype(jnp.float32)
    diag = diagonal(cells, faces)
    fine_op = level_operator(diag, faces)
    field = chebyshev(fine_op, 1.0 / diag, rhs, None, SMOOTH_STEPS)
    resid_mid = restrict_cells(rhs - fine_op(field))
    cells_mid = restrict_cells(cells)
    faces_mid = coarsen_face_weights(faces)
    diag_mid = diagonal(cells_mid, faces_mid)
    mid_op = level_operator(diag_mid, faces_mid)
    corr_mid = chebyshev(mid_op, 1.0 / diag_mid, resid_mid, None, SMOOTH_STEPS)
    resid_low = restrict_cells(resid_mid - mid_op(corr_mid))
    cells_low = restrict_cells(cells_mid)
    faces_low = coarsen_face_weights(faces_mid)
    diag_low = diagonal(cells_low, faces_low)
    corr_low = chebyshev(level_operator(diag_low, faces_low), 1.0 / diag_low, resid_low, None, COARSE_STEPS)
    corr_mid = chebyshev(mid_op, 1.0 / diag_mid, resid_mid, corr_mid + prolong(corr_low), SMOOTH_STEPS)
    return chebyshev(fine_op, 1.0 / diag, rhs, field + prolong(corr_mid), SMOOTH_STEPS)
```

```python
import jax
import jax.numpy as jnp
from jax import lax
from jax.experimental import pallas as pl
from jax.experimental.pallas import tpu as pltpu
from jax.sharding import PartitionSpec as P

SMOOTH_STEPS = 3
COARSE_STEPS = 6
HEAT_CONSTANT = 0.25
SCREENING = 0.002
SEED_WEIGHT = 1.0
THETA = 1.1
DELTA = 0.9

MESH = pl.DeviceIdType.MESH
F32 = jnp.float32
SIZES = {"gx": 4, "gy": 4, "gz": 8}

X0, Y0 = 32, 96
X1, Y1 = 24, 64
X2, Y2 = 24, 48

PLANAR = [(dx, dy) for dx in (1, -1, 0) for dy in (1, -1, 0) if (dx, dy) != (0, 0)]
COLUMN = [(dx, dy) for dx in (1, -1, 2, 0) for dy in (1, -1, 0) if (dx, dy) != (0, 0)]


def factors(steps):
    sigma = THETA / DELTA
    rho = 1.0 / sigma
    out = []
    for _ in range(steps - 1):
        rho_new = 1.0 / (2.0 * sigma - rho)
        out.append((rho_new * rho, 2.0 * rho_new / DELTA))
        rho = rho_new
    return out


def peer(dx, dy, dz):
    shift = {"gx": dx, "gy": dy, "gz": dz}
    return {a: lax.rem(lax.axis_index(a) + shift[a] + n, n) for a, n in SIZES.items()}


def dot(a, b):
    return jnp.dot(a, b, precision=lax.Precision.HIGHEST, preferred_element_type=F32)


def kernel(
    image, labels, out,
    E, L, R, H, UA, UB, DU, C, Q, DH, M,
    zs0, zr0, tmp, bufs, wyb, c1, wx1, wy1, wz1, D1,
    L1, zs1, zr1, A1, I1, C1, ea1, eb1, d1,
    L2, zs2, zr2, A2, I2, C2, ea2, eb2, d2, D2, pro,
    s_e, r_e, s_l, r_l, s_z0, r_z0, s_b0, r_b0,
    s_a1, r_a1, s_b1, r_b1, s_a2, r_a2, s_b2, r_b2,
):
    gx, gy, gz = (lax.axis_index(a) for a in ("gx", "gy", "gz"))
    barrier = pltpu.get_barrier_semaphore()
    partners = [(dx, dy, 0) for dx, dy in COLUMN] + [(0, 0, 1), (0, 0, -1)]
    for p in partners:
        pl.semaphore_signal(barrier, inc=1, device_id=peer(*p), device_id_type=MESH)

    def lanes(rows):
        return lax.broadcasted_iota(jnp.int32, (rows, 128), 1)

    def rows_of(rows):
        return lax.broadcasted_iota(jnp.int32, (rows, 128), 0)

    def send(src, dst, ssem, rsem, to):
        copy = pltpu.make_async_remote_copy(
            src_ref=src, dst_ref=dst, send_sem=ssem, recv_sem=rsem, device_id=to, device_id_type=MESH
        )
        copy.start()
        return copy

    started = []

    def loop(lo, hi, body):
        def step(i, carry):
            body(i)
            return carry
        lax.fori_loop(lo, hi, step, 0)

    def own(x):
        E[0, 8 + x, 16:80] = jnp.exp(image[x] * (1.0 / HEAT_CONSTANT))
        L[0, 8 + x, 16:80] = labels[x].astype(F32)
    loop(0, 16, own)
    pl.semaphore_wait(barrier, len(partners))

    def x_range(dx, start, count, width):
        if dx == 0:
            return pl.ds(start, count), pl.ds(start, count)
        if dx == 1:
            return pl.ds(start + count - width, width), pl.ds(start - width, width)
        return pl.ds(start, width), pl.ds(start + count, width)

    def y_range(dy, start, count):
        if dy == 0:
            return pl.ds(start, count), pl.ds(start, count)
        if dy == 1:
            return pl.ds(start + count - 8, 8), pl.ds(start - 8, 8)
        return pl.ds(start, 8), pl.ds(start + count, 8)

    first = []
    for i, (dx, dy) in enumerate(PLANAR):
        ys, yd = y_range(dy, 16, 64)
        xs, xd = x_range(dx, 8, 16, 7)
        first.append(send(E.at[0, xs, ys], E.at[0, xd, yd], s_e.at[i], r_e.at[i], peer(dx, dy, 0)))
        xs, xd = x_range(dx, 8, 16, 5)
        first.append(send(L.at[0, xs, ys], L.at[0, xd, yd], s_l.at[i], r_l.at[i], peer(dx, dy, 0)))

    group64 = lanes(64) // 8

    def pack(p, carry):
        result = []
        for k, ref in enumerate((E, L)):
            v = ref[0, 8 + p, 16:80]
            low = pltpu.roll(v, lax.rem(8 * p, 128), 1)
            high = pltpu.roll(v, lax.rem(8 * p + 8, 128), 1)
            result.append(jnp.where(group64 == p, low, carry[2 * k]))
            result.append(jnp.where(group64 == p, high, carry[2 * k + 1]))
        return tuple(result)

    zero64 = jnp.zeros((64, 128), F32)
    packed = lax.fori_loop(0, 16, pack, (zero64,) * 4)
    for k in range(2):
        zs0[1, k] = packed[2 * k]
        zs0[0, k] = packed[2 * k + 1]
    za = [
        send(zs0.at[s], zr0.at[1, s, :, pl.ds(8, 64)], s_z0.at[s], r_z0.at[s], peer(0, 0, 1 if s == 0 else -1))
        for s in range(2)
    ]

    for ref in (ea1, eb1, d1):
        def clear(x, ref=ref):
            ref[x] = jnp.zeros((Y1, 128), F32)
        loop(0, X1, clear)
    for ref in (ea2, eb2, d2):
        def clear(x, ref=ref):
            ref[x] = jnp.zeros((Y2, 128), F32)
        loop(0, X2, clear)

    def guard1(a):
        for x in (0, X1 - 1):
            L1[a, x] = jnp.zeros((Y1, 128), F32)

        def edge(x):
            L1[a, x, 0:8] = jnp.zeros((8, 128), F32)
            L1[a, x, 56:64] = jnp.zeros((8, 128), F32)
        loop(1, X1 - 1, edge)
    loop(0, 5, guard1)

    def guard2(a):
        for x in (0, 1, 2, 3, 20, 21, 22, 23):
            L2[a, x] = jnp.zeros((Y2, 128), F32)

        def edge(x):
            L2[a, x, 0:8] = jnp.zeros((8, 128), F32)
            L2[a, x, 40:48] = jnp.zeros((8, 128), F32)
        loop(4, 20, edge)
    loop(0, 5, guard2)

    lane80, row80 = lanes(80), rows_of(80)
    y_in = ((gy * 64 + row80 - 8) >= 0) & ((gy * 64 + row80 - 8) < 256)
    M[0] = jnp.where(y_in, 1.0, 0.0)
    z_in = ((lane80 < 8) & (gz < 7)) | ((lane80 >= 120) & (gz > 0))
    M[1] = jnp.where(y_in & z_in, 1.0, 0.0)

    for copy in za:
        copy.wait_recv()
    zb = []
    for i, (dx, dy) in enumerate(PLANAR):
        ys, yd = y_range(dy, 8, 64)
        zb.append(send(zr0.at[1, :, :, ys], zr0.at[1 - dx, :, :, yd], s_b0.at[i], r_b0.at[i], peer(dx, dy, 0)))
    started += za + zb
    for copy in first:
        copy.wait_recv()
        copy.wait_send()
    for copy in zb:
        copy.wait_recv()

    def x_in(x):
        return ((gx * 16 + x - 8) >= 0) & ((gx * 16 + x - 8) < 64)

    CH = 40
    lane = lanes(CH)
    at0, at127 = lane == 0, lane == 127

    def z_pair(t0, t1):
        r0, r1 = pltpu.roll(t0, 1, 1), pltpu.roll(t1, 1, 1)
        q0, q1 = pltpu.roll(t0, 127, 1), pltpu.roll(t1, 127, 1)
        return (
            jnp.where(at0, r1, r0) + jnp.where(at127, q1, q0),
            jnp.where(at0, r0, r1) + jnp.where(at127, q0, q1),
        )

    def around(ref, x, lo):
        t = [ref[k, x, lo : lo + CH] for k in range(2)]
        z = z_pair(*t)
        total = []
        for k in range(2):
            total.append(
                (ref[k, x - 1, lo : lo + CH] + ref[k, x + 1, lo : lo + CH])
                + (ref[k, x, lo - 1 : lo + CH - 1] + ref[k, x, lo + 1 : lo + CH + 1])
                + z[k]
            )
        return t, total

    def spread(x):
        p, n = lax.rem(x + 8, 16), (x + 8) // 16
        inside = x_in(x)
        for lo in (8, 8 + CH):
            r = pl.ds(lo - 8, CH)
            for k, ref in enumerate((E, L)):
                up = pltpu.roll(zr0[n, 1, k, r], lax.rem(256 - 8 * p, 128), 1)
                down = pltpu.roll(zr0[n, 0, k, r], lax.rem(248 - 8 * p, 128), 1)
                both = jnp.where(lane < 8, up, down)
                if k == 1:
                    ref[1, x, lo : lo + CH] = both
                    continue
                for t, v in ((0, ref[0, x, lo : lo + CH]), (1, both)):
                    m = jnp.where(inside, M[t, r], 0.0) > 0.5
                    v = jnp.where(m, v, 1.0)
                    E[t, x, lo : lo + CH] = v
                    R[t, x, lo : lo + CH] = 1.0 / v
    loop(1, 31, spread)

    def heights(x):
        for lo in (8, 8 + CH):
            e, es = around(E, x, lo)
            c, cs = around(R, x, lo)
            for k in range(2):
                t = (e[k] + es[k]) * (c[k] + cs[k])
                H[k, x, lo : lo + CH] = lax.rsqrt(lax.rsqrt(lax.rsqrt(t)))
    loop(2, 30, heights)

    def cells_of(v):
        return SCREENING + SEED_WEIGHT * jnp.where(v != 2.0, 1.0, 0.0)

    def row_pairs(slot, v):
        n = v.shape[0]
        tmp[slot, 0:n] = v
        return tmp[slot, pl.ds(0, n // 2, stride=2)] + tmp[slot, pl.ds(1, n // 2, stride=2)]

    lane64 = lanes(64)

    def coarse(i):
        x = 8 + 2 * i
        bufs[0, i] = row_pairs(0, cells_of(L[0, x, 16:80]) + cells_of(L[0, x + 1, 16:80]))
        wyb[i] = (
            H[0, x, pl.ds(16, 40, stride=2)] * H[0, x, pl.ds(15, 40, stride=2)]
            + H[0, x + 1, pl.ds(16, 40, stride=2)] * H[0, x + 1, pl.ds(15, 40, stride=2)]
        )
        total = None
        for k in range(2):
            h0, h1 = H[0, x + k, 16:80], H[1, x + k, 16:80]
            r0, r1 = pltpu.roll(h0, 1, 1), pltpu.roll(h1, 1, 1)
            v = h0 * jnp.where(lane64 == 0, r1, r0)
            beyond = pltpu.roll(h1, 1, 1) * pltpu.roll(h0, 2, 1)
            v = jnp.where(lane64 == 1, beyond, v)
            total = v if total is None else total + v
        bufs[1, i] = row_pairs(1, total)
    loop(0, 8, coarse)

    def coarse_x(i):
        x = 8 + 2 * i
        wx1[i] = row_pairs(2, H[0, x, 16:80] * H[0, x - 1, 16:80])
    loop(0, 9, coarse_x)

    wr, wc = rows_of(128), lanes(128)
    restrict = jnp.where(wc == 32 + wr // 2, 1.0, 0.0)
    even = jnp.where((wc == 32 + wr // 2) & (lax.rem(wr, 2) == 0), 1.0, 0.0)
    last = jnp.where((wr == 1) & (wc == 96), 1.0, 0.0)
    c1[...] = dot(bufs[0].reshape(256, 128), restrict).reshape(8, 32, 128)
    wx1[...] = dot(wx1[...].reshape(288, 128), restrict).reshape(9, 32, 128)
    wy1[:, 0:40] = dot(wyb[...].reshape(320, 128), restrict).reshape(8, 40, 128)
    wz1[...] = dot(bufs[1].reshape(256, 128), even + last).reshape(8, 32, 128)

    lane32 = lanes(32)
    own1 = (lane32 >= 32) & (lane32 < 96)

    def level1(i):
        wz = wz1[i]
        d = (
            c1[i] + (wx1[i] + wx1[i + 1]) + (wy1[i, 0:32] + wy1[i, 1:33])
            + (wz + pltpu.roll(wz, 127, 1))
        )
        D1[i] = jnp.where(own1, d, 0.0)
        L1[0, 8 + i, 16:48] = jnp.where(own1, 1.0 / jnp.where(own1, d, 1.0), 0.0)
        L1[1, 8 + i, 16:48] = wx1[i]
        L1[2, 8 + i, 16:48] = wy1[i, 0:32]
        L1[3, 8 + i, 16:48] = wz
    loop(0, 8, level1)

    lane16 = lanes(16)
    own2 = (lane16 >= 48) & (lane16 < 80)
    c2 = [row_pairs(0, c1[2 * i] + c1[2 * i + 1]) for i in range(4)]
    z2 = [row_pairs(1, wz1[2 * i] + wz1[2 * i + 1]) for i in range(4)]
    x2 = [row_pairs(2, wx1[2 * i]) for i in range(5)]
    y2 = [
        wy1[2 * i, pl.ds(0, 24, stride=2)] + wy1[2 * i + 1, pl.ds(0, 24, stride=2)] for i in range(4)
    ]
    c2 = dot(jnp.concatenate(c2, 0), restrict)
    x2 = dot(jnp.concatenate(x2, 0), restrict)
    y2 = dot(jnp.concatenate(y2, 0), restrict)
    z2 = dot(jnp.concatenate(z2, 0), even)
    for i in range(4):
        for k in range(3):
            tmp[k, 0:24] = y2[24 * i : 24 * i + 24]
        wz = z2[16 * i : 16 * i + 16]
        d = (
            c2[16 * i : 16 * i + 16]
            + (x2[16 * i : 16 * i + 16] + x2[16 * i + 16 : 16 * i + 32])
            + (tmp[0, 0:16] + tmp[0, 1:17]) + (wz + pltpu.roll(wz, 127, 1))
        )
        D2[i] = jnp.where(own2, d, 0.0)
        at = 4 + 4 * gx + i
        L2[0, at, 16:32] = jnp.where(own2, 1.0 / jnp.where(own2, d, 1.0), 0.0)
        L2[1, at, 16:32] = x2[16 * i : 16 * i + 16]
        L2[2, at, 16:32] = tmp[0, 0:16]
        L2[3, at, 16:32] = wz

    group32, group16 = lane32 // 8, lane16 // 8

    def pack_z(ref, a, base, planes, rows, lo, hi, group, dst):
        acc = jnp.zeros((rows, 128), F32)
        for p in range(planes):
            v = ref[a, base + p, 16 : 16 + rows]
            acc = jnp.where(group == p, pltpu.roll(v, (8 * p - lo) % 128, 1), acc)
            acc = jnp.where(group == 8 + p, pltpu.roll(v, (64 + 8 * p - hi) % 128, 1), acc)
        dst[a] = acc

    def unpack_z(ref, a, base, planes, rows, lo, hi, ln, src):
        below, above = src[0, a], src[1, a]
        for p in range(planes):
            v = ref[a, base + p, 16 : 16 + rows]
            v = jnp.where((ln >= lo - 8) & (ln < lo), pltpu.roll(below, (lo - 8 - 64 - 8 * p) % 128, 1), v)
            v = jnp.where((ln >= hi + 8) & (ln < hi + 16), pltpu.roll(above, (hi + 8 - 8 * p) % 128, 1), v)
            ref[a, base + p, 16 : 16 + rows] = v

    def pack1(a):
        pack_z(L1, a, 8, 8, 32, 32, 88, group32, zs1)

    def unpack1(a):
        unpack_z(L1, a, 8, 8, 32, 32, 88, lane32, zr1)

    def pack2(a):
        pack_z(L2, a, 4 + 4 * gx, 4, 16, 48, 72, group16, zs2)

    def unpack2(a):
        unpack_z(L2, a, 4 + 4 * gx, 4, 16, 48, 72, lane16, zr2)

    def send_z(zs, zr, which, n, ssem, rsem, slot):
        return [
            send(zs.at[pl.ds(which, n)], zr.at[s, pl.ds(which, n)], ssem.at[slot, s], rsem.at[slot, s],
                 peer(0, 0, 1 if s == 0 else -1))
            for s in range(2)
        ]

    def send_1(which, n, slot):
        copies = []
        for i, (dx, dy) in enumerate(PLANAR):
            ys, yd = y_range(dy, 16, 32)
            xs, xd = x_range(dx, 8, 8, 7)
            copies.append(send(L1.at[pl.ds(which, n), xs, ys], L1.at[pl.ds(which, n), xd, yd],
                               s_b1.at[slot, i], r_b1.at[slot, i], peer(dx, dy, 0)))
        return copies

    def send_2(which, n, slot):
        copies = []
        planes = pl.ds(4 + 4 * gx, 4)
        for i, (dx, dy) in enumerate(COLUMN):
            ys, yd = y_range(dy, 16, 16)
            copies.append(send(L2.at[pl.ds(which, n), planes, ys], L2.at[pl.ds(which, n), planes, yd],
                               s_b2.at[slot, i], r_b2.at[slot, i], peer(dx, dy, 0)))
        return copies

    loop(0, 4, pack1)
    a1 = send_z(zs1, zr1, 0, 4, s_a1, r_a1, 0)
    loop(0, 4, pack2)
    a2 = send_z(zs2, zr2, 0, 4, s_a2, r_a2, 0)

    def diagonal(x):
        inside = x_in(x)
        for lo in (8, 8 + CH):
            h, hs = around(H, x, lo)
            r = pl.ds(lo - 8, CH)
            for k in range(2):
                m = jnp.where(inside, M[k, r], 0.0)
                lab = L[k, x, lo : lo + CH]
                d = cells_of(lab) + h[k] * hs[k]
                hi = m * h[k] / d
                c = jnp.where(lab == 1.0, SEED_WEIGHT * hi, 0.0)
                C[k, x, lo : lo + CH] = c
                Q[k, x, lo : lo + CH] = hi * h[k]
                u = c * (1.0 / THETA)
                UA[k, x, lo : lo + CH] = u
                DU[k, x, lo : lo + CH] = u
                if k == 0:
                    DH[x, lo - 8 : lo - 8 + CH] = d / h[k]
    loop(3, 29, diagonal)

    for copy in a1 + a2:
        copy.wait_recv()
    loop(0, 4, unpack1)
    b1 = send_1(0, 4, 0)
    loop(0, 4, unpack2)
    b2 = send_2(0, 4, 0)
    started += a1 + a2 + b1 + b2

    def smooth(src, dst, lo_x, hi_x, alpha, beta, keep=True):
        def body(x):
            for lo in (8, 8 + CH):
                u, us = around(src, x, lo)
                for k in range(2):
                    s = slice(lo, lo + CH)
                    g = beta * (C[k, x, s] - u[k] + Q[k, x, s] * us[k])
                    d = g if alpha is None else alpha * DU[k, x, s] + g
                    if keep:
                        DU[k, x, s] = d
                    dst[k, x, s] = u[k] + d
        loop(lo_x, hi_x, body)

    fine = factors(SMOOTH_STEPS)
    smooth(UA, UB, 4, 28, *fine[0])
    smooth(UB, UA, 5, 27, *fine[1], keep=False)

    def own_sum(ref, x):
        t0, t1 = ref[0, x, 16:80], ref[1, x, 16:80]
        low = jnp.where(lane64 == 0, pltpu.roll(t1, 1, 1), pltpu.roll(t0, 1, 1))
        high = jnp.where(lane64 == 127, pltpu.roll(t1, 127, 1), pltpu.roll(t0, 127, 1))
        return t0, (
            (ref[0, x - 1, 16:80] + ref[0, x + 1, 16:80])
            + (ref[0, x, 15:79] + ref[0, x, 17:81]) + (low + high)
        )

    def residual(i):
        total = None
        for k in range(2):
            x = 8 + 2 * i + k
            u, us = own_sum(UA, x)
            r = DH[x, 8:72] * (C[0, x, 16:80] - u + Q[0, x, 16:80] * us)
            total = r if total is None else total + r
        bufs[0, i] = row_pairs(0, total)
    loop(0, 8, residual)
    L1[4, 8:16, 16:48] = dot(bufs[0].reshape(256, 128), restrict).reshape(8, 32, 128)
    pack1(4)
    a1 = send_z(zs1, zr1, 4, 1, s_a1, r_a1, 1)

    def prepare(ref, inv, a, x_lo, x_hi, rows, inside):
        def body(x):
            i = jnp.where(inside(x), ref[0, x, 8 : 8 + rows], 0.0)
            inv[x, 8 : 8 + rows] = i
            a[0, x] = i * ref[1, x, 8 : 8 + rows]
            a[1, x] = i * ref[1, x + 1, 8 : 8 + rows]
            a[2, x] = i * ref[2, x, 8 : 8 + rows]
            a[3, x] = i * ref[2, x, 9 : 9 + rows]
            a[4, x] = i * ref[3, x, 8 : 8 + rows]
            a[5, x] = i * pltpu.roll(ref[3, x, 8 : 8 + rows], 127, 1)
        loop(x_lo, x_hi, body)

    def apply(c, a, e, x, rows):
        v = e[x, 8 : 8 + rows]
        return v, (
            (c[x] - v)
            + (a[0, x] * e[x - 1, 8 : 8 + rows] + a[1, x] * e[x + 1, 8 : 8 + rows])
            + (a[2, x] * e[x, 7 : 7 + rows] + a[3, x] * e[x, 9 : 9 + rows])
            + (a[4, x] * pltpu.roll(v, 1, 1) + a[5, x] * pltpu.roll(v, 127, 1))
        )

    def begin(c, e, d, x_lo, x_hi, rows):
        def body(x):
            u = c[x] * (1.0 / THETA)
            e[x, 8 : 8 + rows] = u
            d[x, 0:rows] = u
        loop(x_lo, x_hi, body)

    def relax(c, a, e, new, d, x_lo, x_hi, rows, alpha, beta):
        def body(x):
            v, g = apply(c, a, e, x, rows)
            step = beta * g if alpha is None else alpha * d[x, 0:rows] + beta * g
            d[x, 0:rows] = step
            new[x, 8 : 8 + rows] = v + step
        loop(x_lo, x_hi, body)

    lane48, row48 = lanes(48), rows_of(48)
    yz1 = (
        (gy * 32 + row48 - 8 >= 0) & (gy * 32 + row48 - 8 < 128)
        & (gz * 64 + lane48 - 32 >= 0) & (gz * 64 + lane48 - 32 < 512)
    )

    def inside1(x):
        ok = ((gx * 8 + x - 8) >= 0) & ((gx * 8 + x - 8) < 32)
        return jnp.where(ok, jnp.where(yz1, 1.0, 0.0), 0.0) > 0.5

    row32 = rows_of(32)
    yz2 = (
        (gy * 16 + row32 - 8 >= 0) & (gy * 16 + row32 - 8 < 64)
        & (gz * 32 + lane32 - 48 >= 0) & (gz * 32 + lane32 - 48 < 256)
    )

    for copy in a1:
        copy.wait_recv()
    unpack1(4)
    r1 = send_1(4, 1, 1)
    started += a1 + r1
    for copy in b1:
        copy.wait_recv()
    prepare(L1, I1, A1, 1, X1 - 1, 48, inside1)
    for copy in r1:
        copy.wait_recv()

    def scale1(x):
        C1[x] = I1[x, 8:56] * L1[4, x, 8:56]
    loop(1, X1 - 1, scale1)
    begin(C1, ea1, d1, 1, X1 - 1, 48)
    relax(C1, A1, ea1, eb1, d1, 2, X1 - 2, 48, *fine[0])
    relax(C1, A1, eb1, ea1, d1, 3, X1 - 3, 48, *fine[1])

    def residual1(i):
        total = None
        for k in range(2):
            x = 8 + 2 * i + k
            _, g = apply(C1, A1, ea1, x, 48)
            r = D1[2 * i + k] * g[8:40]
            total = r if total is None else total + r
        bufs[1, i, 0:16] = row_pairs(1, total)
    loop(0, 4, residual1)
    r2 = dot(jnp.concatenate([bufs[1, i, 0:16] for i in range(4)], 0), restrict)
    for i in range(4):
        L2[4, 4 + 4 * gx + i, 16:32] = r2[16 * i : 16 * i + 16]
    pack2(4)
    a2 = send_z(zs2, zr2, 4, 1, s_a2, r_a2, 1)
    for copy in b2:
        copy.wait_recv()
    prepare(L2, I2, A2, 4, 20, 32, lambda x: yz2)
    for copy in a2:
        copy.wait_recv()
    unpack2(4)
    r2 = send_2(4, 1, 1)
    started += a2 + r2
    for copy in r2:
        copy.wait_recv()

    def scale2(x):
        C2[x] = I2[x, 8:40] * L2[4, x, 8:40]
    loop(4, 20, scale2)
    begin(C2, ea2, d2, 4, 20, 32)
    pair = (ea2, eb2)
    for n, f in enumerate(factors(COARSE_STEPS)):
        relax(C2, A2, pair[n % 2], pair[1 - n % 2], d2, 4, 20, 32, *f)
    e2 = pair[(COARSE_STEPS - 1) % 2]

    widen = jnp.where(wr == 32 + wc // 2, 1.0, 0.0)

    def up1(i):
        v = dot(e2[4 * gx + i, 8:40], widen)
        pro[0, pl.ds(0, 32, stride=2)] = v
        pro[0, pl.ds(1, 32, stride=2)] = v
        for k in range(2):
            ea1[2 * i + k, 8:56] = ea1[2 * i + k, 8:56] + pro[0, 8:56]
    loop(1, 11, up1)
    relax(C1, A1, ea1, eb1, d1, 3, X1 - 3, 48, None, 1.0 / THETA)
    relax(C1, A1, eb1, ea1, d1, 4, X1 - 4, 48, *fine[0])
    relax(C1, A1, ea1, eb1, d1, 5, X1 - 5, 48, *fine[1])

    beyond = jnp.where(
        ((wc < 8) & (wr == 96 + wc // 2)) | ((wc >= 120) & (wr == 28 + (wc - 120) // 2)), 1.0, 0.0
    )

    def up0(i):
        e = eb1[4 + i, 8:56]
        for k, w in enumerate((widen, beyond)):
            v = dot(e, w)
            pro[k, pl.ds(0, 48, stride=2)] = v
            pro[k, pl.ds(1, 48, stride=2)] = v
        for n in range(2):
            for k in range(2):
                x = 2 * i + n
                UA[k, x, 8:88] = UA[k, x, 8:88] + H[k, x, 8:88] * pro[k, 8:88]
    loop(2, 14, up0)
    smooth(UA, UB, 6, 26, None, 1.0 / THETA)
    smooth(UB, UA, 7, 25, *fine[0])

    def finish(x):
        u, us = own_sum(UA, 8 + x)
        alpha, beta = fine[1]
        d = alpha * DU[0, 8 + x, 16:80] + beta * (C[0, 8 + x, 16:80] - u + Q[0, 8 + x, 16:80] * us)
        out[x] = (u + d) / H[0, 8 + x, 16:80]
    loop(0, 16, finish)

    for copy in started:
        copy.wait_send()


def shards(image, labels):
    def level0():
        return pltpu.VMEM((2, X0, Y0, 128), F32)

    def vmem(*shape):
        return pltpu.VMEM(shape, F32)

    def sems(*shape):
        return pltpu.SemaphoreType.DMA(shape)

    scratch = [level0() for _ in range(9)] + [
        vmem(X0, 80, 128), vmem(2, 80, 128),
        vmem(2, 2, 64, 128), vmem(3, 2, 2, 80, 128), vmem(3, 64, 128), vmem(2, 8, 32, 128), vmem(8, 40, 128),
        vmem(8, 32, 128), vmem(9, 32, 128), vmem(8, 48, 128), vmem(8, 32, 128), vmem(8, 32, 128),
        vmem(5, X1, Y1, 128), vmem(5, 32, 128), vmem(2, 5, 32, 128), vmem(6, X1, 48, 128),
        vmem(X1, Y1, 128), vmem(X1, 48, 128), vmem(X1, Y1, 128), vmem(X1, Y1, 128), vmem(X1, Y1, 128),
        vmem(5, X2, Y2, 128), vmem(5, 16, 128), vmem(2, 5, 16, 128), vmem(6, X2, 32, 128),
        vmem(X2, Y2, 128), vmem(X2, 32, 128), vmem(X2, Y2, 128), vmem(X2, Y2, 128), vmem(X2, Y2, 128),
        vmem(4, 16, 128), vmem(2, 96, 128),
        sems(8), sems(8), sems(8), sems(8), sems(2), sems(2), sems(8), sems(8),
        sems(2, 2), sems(2, 2), sems(2, 8), sems(2, 8), sems(2, 2), sems(2, 2), sems(2, 11), sems(2, 11),
    ]
    return pl.pallas_call(
        kernel,
        out_shape=jax.ShapeDtypeStruct(image.shape, F32),
        in_specs=[pl.BlockSpec(memory_space=pltpu.VMEM)] * 2,
        out_specs=pl.BlockSpec(memory_space=pltpu.VMEM),
        scratch_shapes=scratch,
        compiler_params=pltpu.CompilerParams(
            collective_id=0, has_side_effects=True, vmem_limit_bytes=56 * 1024 * 1024
        ),
    )(image, labels)


def solution(mesh):
    placed = (P("gx", "gy", "gz"), P("gx", "gy", "gz"))
    return jax.shard_map(
        shards, mesh=mesh, in_specs=placed, out_specs=P("gx", "gy", "gz"), check_vma=False
    )
```

```python
import jax
import jax.numpy as jnp
from jax import lax
from jax.experimental import pallas as pl
from jax.experimental.pallas import tpu as pltpu
from jax.sharding import PartitionSpec as P

SMOOTH_STEPS = 3
COARSE_STEPS = 6
HEAT_CONSTANT = 0.25
SCREENING = 0.002
SEED_WEIGHT = 1.0
THETA = 1.1
DELTA = 0.9

MESH = pl.DeviceIdType.MESH
F32 = jnp.float32
SIZES = {"gx": 4, "gy": 4, "gz": 8}

X0, Y0 = 32, 96
X1, Y1 = 24, 64
X2, Y2 = 24, 48

PLANAR = [(dx, dy) for dx in (1, -1, 0) for dy in (1, -1, 0) if (dx, dy) != (0, 0)]
COLUMN = [(dx, dy) for dx in (1, -1, 2, 0) for dy in (1, -1, 0) if (dx, dy) != (0, 0)]


def factors(steps):
    sigma = THETA / DELTA
    rho = 1.0 / sigma
    out = []
    for _ in range(steps - 1):
        rho_new = 1.0 / (2.0 * sigma - rho)
        out.append((rho_new * rho, 2.0 * rho_new / DELTA))
        rho = rho_new
    return out


def peer(dx, dy, dz):
    shift = {"gx": dx, "gy": dy, "gz": dz}
    return {a: lax.rem(lax.axis_index(a) + shift[a] + n, n) for a, n in SIZES.items()}


def dot(a, b):
    return jnp.dot(a, b, precision=lax.Precision.HIGHEST, preferred_element_type=F32)


def kernel(
    image, labels, out,
    E, L, EM, R, H, UA, UB, DU, C, Q, DH, M,
    zs0, zr0, tmp, bufs, wyb, c1, wx1, wy1, wz1, D1,
    L1, LP, zs1, zr1, zc1, A1, I1, C1, ea1, eb1, d1,
    L2, LQ, zs2, zr2, zc2, A2, I2, C2, ea2, eb2, d2, D2, pro,
    s_e, r_e, s_l, r_l, s_z0, r_z0, s_b0, r_b0,
    s_a1, r_a1, s_b1, r_b1, s_c1, r_c1, s_a2, r_a2, s_b2, r_b2, s_c2, r_c2,
):
    gx, gy, gz = (lax.axis_index(a) for a in ("gx", "gy", "gz"))
    barrier = pltpu.get_barrier_semaphore()
    partners = [(dx, dy, 0) for dx, dy in COLUMN] + [(0, 0, 1), (0, 0, -1)]
    for p in partners:
        pl.semaphore_signal(barrier, inc=1, device_id=peer(*p), device_id_type=MESH)

    def lanes(rows):
        return lax.broadcasted_iota(jnp.int32, (rows, 128), 1)

    def rows_of(rows):
        return lax.broadcasted_iota(jnp.int32, (rows, 128), 0)

    def send(src, dst, ssem, rsem, to):
        copy = pltpu.make_async_remote_copy(
            src_ref=src, dst_ref=dst, send_sem=ssem, recv_sem=rsem, device_id=to, device_id_type=MESH
        )
        copy.start()
        return copy

    started = []

    def loop(lo, hi, body):
        def step(i, carry):
            body(i)
            return carry
        lax.fori_loop(lo, hi, step, 0)

    def grouped(lo, hi, n, work):
        def step(i, carry):
            stores = []
            for j in range(n):
                stores += work(lo + n * i + j)
            for ref, index, value in stores:
                ref[index] = value
            return carry
        lax.fori_loop(0, (hi - lo) // n, step, 0)
        for j in range(lo + (hi - lo) // n * n, hi):
            for ref, index, value in work(j):
                ref[index] = value

    def own(x):
        E[8 + x, 16:80] = jnp.exp(image[x] * (1.0 / HEAT_CONSTANT))
        L[8 + x, 16:80] = labels[x].astype(F32)
    loop(0, 16, own)
    pl.semaphore_wait(barrier, len(partners))

    def x_range(dx, start, count, width):
        if dx == 0:
            return pl.ds(start, count), pl.ds(start, count)
        if dx == 1:
            return pl.ds(start + count - width, width), pl.ds(start - width, width)
        return pl.ds(start, width), pl.ds(start + count, width)

    def y_range(dy, start, count):
        if dy == 0:
            return pl.ds(start, count), pl.ds(start, count)
        if dy == 1:
            return pl.ds(start + count - 8, 8), pl.ds(start - 8, 8)
        return pl.ds(start, 8), pl.ds(start + count, 8)

    def send_own(ref, width, ssem, rsem):
        copies = []
        for i, (dx, dy) in enumerate(PLANAR):
            ys, yd = y_range(dy, 16, 64)
            xs, xd = x_range(dx, 8, 16, width)
            copies.append(send(ref.at[xs, ys], ref.at[xd, yd], ssem.at[i], rsem.at[i], peer(dx, dy, 0)))
        return copies

    own_e = send_own(E, 7, s_e, r_e)

    group64 = lanes(64) // 8

    def pack(p, carry):
        result = []
        for k, ref in enumerate((E, L)):
            v = ref[8 + p, 16:80]
            low = pltpu.roll(v, lax.rem(8 * p, 128), 1)
            high = pltpu.roll(v, lax.rem(8 * p + 8, 128), 1)
            result.append(jnp.where(group64 == p, low, carry[2 * k]))
            result.append(jnp.where(group64 == p, high, carry[2 * k + 1]))
        return tuple(result)

    zero64 = jnp.zeros((64, 128), F32)
    packed = lax.fori_loop(0, 16, pack, (zero64,) * 4)
    for k in range(2):
        zs0[k, 1] = packed[2 * k]
        zs0[k, 0] = packed[2 * k + 1]
    za = [
        [
            send(zs0.at[k, s], zr0.at[k, 1, s, pl.ds(8, 64)], s_z0.at[k, s], r_z0.at[k, s],
                 peer(0, 0, 1 if s == 0 else -1))
            for s in range(2)
        ]
        for k in range(2)
    ]

    def forward(k):
        for copy in za[k]:
            copy.wait_recv()
        copies = []
        for i, (dx, dy) in enumerate(PLANAR):
            ys, yd = y_range(dy, 8, 64)
            copies.append(send(zr0.at[k, 1, :, ys], zr0.at[k, 1 - dx, :, yd],
                               s_b0.at[k, i], r_b0.at[k, i], peer(dx, dy, 0)))
        return copies

    for ref in (ea1, eb1, d1):
        def clear(x, ref=ref):
            ref[x] = jnp.zeros((Y1, 128), F32)
        loop(0, X1, clear)
    for ref in (ea2, eb2, d2):
        def clear(x, ref=ref):
            ref[x] = jnp.zeros((Y2, 128), F32)
        loop(0, X2, clear)

    def guard1(a):
        for x in (0, X1 - 1):
            L1[a, x] = jnp.zeros((Y1, 128), F32)

        def edge(x):
            L1[a, x, 0:8] = jnp.zeros((8, 128), F32)
            L1[a, x, 56:64] = jnp.zeros((8, 128), F32)
        loop(1, X1 - 1, edge)
    loop(0, 5, guard1)

    def guard2(a):
        for x in (0, 1, 2, 3, 20, 21, 22, 23):
            L2[a, x] = jnp.zeros((Y2, 128), F32)

        def edge(x):
            L2[a, x, 0:8] = jnp.zeros((8, 128), F32)
            L2[a, x, 40:48] = jnp.zeros((8, 128), F32)
        loop(4, 20, edge)
    loop(0, 5, guard2)

    lane80, row80 = lanes(80), rows_of(80)
    y_in = ((gy * 64 + row80 - 8) >= 0) & ((gy * 64 + row80 - 8) < 256)
    M[0] = jnp.where(y_in, 1.0, 0.0)
    z_in = ((lane80 < 8) & (gz < 7)) | ((lane80 >= 120) & (gz > 0))
    M[1] = jnp.where(y_in & z_in, 1.0, 0.0)

    zb_e = forward(0)
    own_l = send_own(L, 5, s_l, r_l)
    zb_l = forward(1)
    started += za[0] + za[1] + own_e + own_l + zb_e + zb_l
    for i, (dx, dy) in enumerate(PLANAR):
        if dx == 0:
            own_e[i].wait_recv()
            zb_e[i].wait_recv()

    def x_in(x):
        return ((gx * 16 + x - 8) >= 0) & ((gx * 16 + x - 8) < 64)

    CH = 40
    lane = lanes(CH)
    at0, at127 = lane == 0, lane == 127

    def z_pair(t0, t1):
        r0, r1 = pltpu.roll(t0, 1, 1), pltpu.roll(t1, 1, 1)
        q0, q1 = pltpu.roll(t0, 127, 1), pltpu.roll(t1, 127, 1)
        return (
            jnp.where(at0, r1, r0) + jnp.where(at127, q1, q0),
            jnp.where(at0, r0, r1) + jnp.where(at127, q0, q1),
        )

    def around(ref, x, lo):
        t = [ref[k, x, lo : lo + CH] for k in range(2)]
        z = z_pair(*t)
        total = []
        for k in range(2):
            total.append(
                (ref[k, x - 1, lo : lo + CH] + ref[k, x + 1, lo : lo + CH])
                + (ref[k, x, lo - 1 : lo + CH - 1] + ref[k, x, lo + 1 : lo + CH + 1])
                + z[k]
            )
        return t, total

    def ends(k, x, r):
        p, n = lax.rem(x + 8, 16), (x + 8) // 16
        up = pltpu.roll(zr0[k, n, 1, r], lax.rem(256 - 8 * p, 128), 1)
        down = pltpu.roll(zr0[k, n, 0, r], lax.rem(248 - 8 * p, 128), 1)
        return jnp.where(lane < 8, up, down)

    def spread(x):
        inside = x_in(x)
        for lo in (8, 8 + CH):
            r = pl.ds(lo - 8, CH)
            for t, v in ((0, E[x, lo : lo + CH]), (1, ends(0, x, r))):
                m = jnp.where(inside, M[t, r], 0.0) > 0.5
                v = jnp.where(m, v, 1.0)
                EM[t, x, lo : lo + CH] = v
                R[t, x, lo : lo + CH] = 1.0 / v
    loop(8, 24, spread)

    def heights(x):
        for lo in (8, 8 + CH):
            e, es = around(EM, x, lo)
            c, cs = around(R, x, lo)
            for k in range(2):
                t = (e[k] + es[k]) * (c[k] + cs[k])
                H[k, x, lo : lo + CH] = lax.rsqrt(lax.rsqrt(lax.rsqrt(t)))
    loop(9, 23, heights)
    for i, (dx, dy) in enumerate(PLANAR):
        if dx != 0:
            own_e[i].wait_recv()
            zb_e[i].wait_recv()
    loop(6, 8, spread)
    loop(24, 26, spread)
    loop(7, 9, heights)
    loop(23, 25, heights)

    def cells_of(v):
        return SCREENING + SEED_WEIGHT * jnp.where(v != 2.0, 1.0, 0.0)

    def row_pairs(slot, v):
        n = v.shape[0]
        tmp[slot, 0:n] = v
        return tmp[slot, pl.ds(0, n // 2, stride=2)] + tmp[slot, pl.ds(1, n // 2, stride=2)]

    lane64 = lanes(64)

    def coarse(i):
        x = 8 + 2 * i
        bufs[0, i] = row_pairs(0, cells_of(L[x, 16:80]) + cells_of(L[x + 1, 16:80]))
        wyb[i] = (
            H[0, x, pl.ds(16, 40, stride=2)] * H[0, x, pl.ds(15, 40, stride=2)]
            + H[0, x + 1, pl.ds(16, 40, stride=2)] * H[0, x + 1, pl.ds(15, 40, stride=2)]
        )
        total = None
        for k in range(2):
            h0, h1 = H[0, x + k, 16:80], H[1, x + k, 16:80]
            r0, r1 = pltpu.roll(h0, 1, 1), pltpu.roll(h1, 1, 1)
            v = h0 * jnp.where(lane64 == 0, r1, r0)
            beyond = pltpu.roll(h1, 1, 1) * pltpu.roll(h0, 2, 1)
            v = jnp.where(lane64 == 1, beyond, v)
            total = v if total is None else total + v
        bufs[1, i] = row_pairs(1, total)
    loop(0, 8, coarse)

    def coarse_x(i):
        x = 8 + 2 * i
        wx1[i] = row_pairs(2, H[0, x, 16:80] * H[0, x - 1, 16:80])
    loop(0, 9, coarse_x)

    wr, wc = rows_of(128), lanes(128)
    restrict = jnp.where(wc == 32 + wr // 2, 1.0, 0.0)
    even = jnp.where((wc == 32 + wr // 2) & (lax.rem(wr, 2) == 0), 1.0, 0.0)
    last = jnp.where((wr == 1) & (wc == 96), 1.0, 0.0)
    c1[...] = dot(bufs[0].reshape(256, 128), restrict).reshape(8, 32, 128)
    wx1[...] = dot(wx1[...].reshape(288, 128), restrict).reshape(9, 32, 128)
    wy1[:, 0:40] = dot(wyb[...].reshape(320, 128), restrict).reshape(8, 40, 128)
    wz1[...] = dot(bufs[1].reshape(256, 128), even + last).reshape(8, 32, 128)

    lane32 = lanes(32)
    own1 = (lane32 >= 32) & (lane32 < 96)

    def level1(i):
        wz = wz1[i]
        d = (
            c1[i] + (wx1[i] + wx1[i + 1]) + (wy1[i, 0:32] + wy1[i, 1:33])
            + (wz + pltpu.roll(wz, 127, 1))
        )
        D1[i] = jnp.where(own1, d, 0.0)
        four = (jnp.where(own1, 1.0 / jnp.where(own1, d, 1.0), 0.0), wx1[i], wy1[i, 0:32], wz)
        for a in range(4):
            L1[a, 8 + i, 16:48] = four[a]
        for a in range(2):
            LP[a, 8 + i, 16:48] = jnp.where(
                lane32 < 64, pltpu.roll(four[2 * a], 96, 1), pltpu.roll(four[2 * a + 1], 32, 1)
            )
    loop(0, 8, level1)

    def send_1(src, which, width, ssem, rsem):
        copies = []
        for i, (dx, dy) in enumerate(PLANAR):
            ys, yd = y_range(dy, 16, 32)
            xs, xd = x_range(dx, 8, 8, 7)
            copies.append(send(src.at[pl.ds(which, width), xs, ys], src.at[pl.ds(which, width), xd, yd],
                               ssem.at[i], rsem.at[i], peer(dx, dy, 0)))
        return copies

    b1 = send_1(LP, 0, 2, s_b1.at[0], r_b1.at[0])

    lane16 = lanes(16)
    own2 = (lane16 >= 48) & (lane16 < 80)
    c2 = [row_pairs(0, c1[2 * i] + c1[2 * i + 1]) for i in range(4)]
    z2 = [row_pairs(1, wz1[2 * i] + wz1[2 * i + 1]) for i in range(4)]
    x2 = [row_pairs(2, wx1[2 * i]) for i in range(5)]
    y2 = [
        wy1[2 * i, pl.ds(0, 24, stride=2)] + wy1[2 * i + 1, pl.ds(0, 24, stride=2)] for i in range(4)
    ]
    c2 = dot(jnp.concatenate(c2, 0), restrict)
    x2 = dot(jnp.concatenate(x2, 0), restrict)
    y2 = dot(jnp.concatenate(y2, 0), restrict)
    z2 = dot(jnp.concatenate(z2, 0), even)
    for i in range(4):
        for k in range(3):
            tmp[k, 0:24] = y2[24 * i : 24 * i + 24]
        wz = z2[16 * i : 16 * i + 16]
        d = (
            c2[16 * i : 16 * i + 16]
            + (x2[16 * i : 16 * i + 16] + x2[16 * i + 16 : 16 * i + 32])
            + (tmp[0, 0:16] + tmp[0, 1:17]) + (wz + pltpu.roll(wz, 127, 1))
        )
        D2[i] = jnp.where(own2, d, 0.0)
        at = 4 + 4 * gx + i
        L2[0, at, 16:32] = jnp.where(own2, 1.0 / jnp.where(own2, d, 1.0), 0.0)
        L2[1, at, 16:32] = x2[16 * i : 16 * i + 16]
        L2[2, at, 16:32] = tmp[0, 0:16]
        L2[3, at, 16:32] = wz

    group32, group16 = lane32 // 8, lane16 // 8

    def pack_z(ref, a, base, planes, rows, lo, hi, group, dst):
        acc = jnp.zeros((rows, 128), F32)
        for p in range(planes):
            v = ref[a, base + p, 16 : 16 + rows]
            acc = jnp.where(group == p, pltpu.roll(v, (8 * p - lo) % 128, 1), acc)
            acc = jnp.where(group == 8 + p, pltpu.roll(v, (64 + 8 * p - hi) % 128, 1), acc)
        dst[a] = acc

    def joined(zr, zc, a, slot, rows, ln):
        zc[a, slot, 8 : 8 + rows] = jnp.where(ln < 64, zr[1, a], zr[0, a])

    def extended(base, ends, p, ln, lo, hi):
        down = pltpu.roll(ends, lax.rem(256 + lo - 8 - 64 - 8 * p, 128), 1)
        up = pltpu.roll(ends, lax.rem(256 + hi + 8 - 8 * p, 128), 1)
        v = jnp.where((ln >= lo) & (ln < hi + 8), base, 0.0)
        v = jnp.where((ln >= lo - 8) & (ln < lo), down, v)
        return jnp.where((ln >= hi + 8) & (ln < hi + 16), up, v)

    def pack1(a):
        pack_z(L1, a, 8, 8, 32, 32, 88, group32, zs1)

    def join1(a):
        joined(zr1, zc1, a, 1, 32, lane32)

    def extended1(a, x, base):
        return extended(base, zc1[a, x // 8], lax.rem(x, 8), lane48, 32, 88)

    def pack2(a):
        pack_z(L2, a, 4 + 4 * gx, 4, 16, 48, 72, group16, zs2)

    def join2(a):
        joined(zr2, zc2, a, gx, 16, lane16)

    def pack_own2(a):
        acc = jnp.zeros((16, 128), F32)
        for p in range(4):
            v = pltpu.roll(L2[a, 4 + 4 * gx + p, 16:32], (32 * p - 48) % 128, 1)
            acc = jnp.where(lane16 // 32 == p, v, acc)
        LQ[a, gx, 8:24] = acc

    def extended2(a, slot, p):
        base = pltpu.roll(LQ[a, slot], (48 - 32 * p) % 128, 1)
        return extended(base, zc2[a, slot], p, lane32, 48, 72)

    def send_z(zs, zr, which, n, ssem, rsem, slot):
        return [
            send(zs.at[pl.ds(which, n)], zr.at[s, pl.ds(which, n)], ssem.at[slot, s], rsem.at[slot, s],
                 peer(0, 0, 1 if s == 0 else -1))
            for s in range(2)
        ]

    def send_c1(which, n, slot):
        copies = []
        for i, (dx, dy) in enumerate(PLANAR):
            ys, yd = y_range(dy, 8, 32)
            copies.append(send(zc1.at[pl.ds(which, n), 1, ys], zc1.at[pl.ds(which, n), 1 - dx, yd],
                               s_c1.at[slot, i], r_c1.at[slot, i], peer(dx, dy, 0)))
        return copies

    def send_2(ref, which, n, ssem, rsem):
        copies = []
        for i, (dx, dy) in enumerate(COLUMN):
            ys, yd = y_range(dy, 8, 16)
            copies.append(send(ref.at[pl.ds(which, n), gx, ys], ref.at[pl.ds(which, n), gx, yd],
                               ssem.at[i], rsem.at[i], peer(dx, dy, 0)))
        return copies

    lane48, row48 = lanes(48), rows_of(48)
    loop(0, 4, pack1)
    a1 = send_z(zs1, zr1, 0, 4, s_a1, r_a1, 0)
    loop(0, 4, pack2)
    a2 = send_z(zs2, zr2, 0, 4, s_a2, r_a2, 0)
    loop(0, 4, pack_own2)
    loop(1, 6, spread)
    loop(26, 31, spread)
    loop(2, 7, heights)
    loop(25, 30, heights)
    for copy in a1:
        copy.wait_recv()
    loop(0, 4, join1)
    c1s = send_c1(0, 4, 0)

    def diagonal(x):
        inside = x_in(x)
        for lo in (8, 8 + CH):
            h, hs = around(H, x, lo)
            r = pl.ds(lo - 8, CH)
            for k in range(2):
                m = jnp.where(inside, M[k, r], 0.0)
                lab = L[x, lo : lo + CH] if k == 0 else ends(1, x, r)
                d = cells_of(lab) + h[k] * hs[k]
                hi = m * h[k] / d
                c = jnp.where(lab == 1.0, SEED_WEIGHT * hi, 0.0)
                C[k, x, lo : lo + CH] = c
                Q[k, x, lo : lo + CH] = hi * h[k]
                u = c * (1.0 / THETA)
                UA[k, x, lo : lo + CH] = u
                DU[k, x, lo : lo + CH] = u
                if k == 0:
                    DH[x, lo - 8 : lo - 8 + CH] = d / h[k]
    for copy in own_l + zb_l:
        copy.wait_recv()
    loop(3, 29, diagonal)
    started += a1 + a2 + b1 + c1s

    def smooth(src, dst, lo_x, hi_x, alpha, beta, keep=True):
        def body(x):
            for lo in (8, 8 + CH):
                u, us = around(src, x, lo)
                for k in range(2):
                    s = slice(lo, lo + CH)
                    g = beta * (C[k, x, s] - u[k] + Q[k, x, s] * us[k])
                    d = g if alpha is None else alpha * DU[k, x, s] + g
                    if keep:
                        DU[k, x, s] = d
                    dst[k, x, s] = u[k] + d
        loop(lo_x, hi_x, body)

    fine = factors(SMOOTH_STEPS)
    smooth(UA, UB, 4, 28, *fine[0])
    smooth(UB, UA, 5, 27, *fine[1], keep=False)

    def own_sum(ref, x):
        t0, t1 = ref[0, x, 16:80], ref[1, x, 16:80]
        low = jnp.where(lane64 == 0, pltpu.roll(t1, 1, 1), pltpu.roll(t0, 1, 1))
        high = jnp.where(lane64 == 127, pltpu.roll(t1, 127, 1), pltpu.roll(t0, 127, 1))
        return t0, (
            (ref[0, x - 1, 16:80] + ref[0, x + 1, 16:80])
            + (ref[0, x, 15:79] + ref[0, x, 17:81]) + (low + high)
        )

    def residual(i):
        total = None
        for k in range(2):
            x = 8 + 2 * i + k
            u, us = own_sum(UA, x)
            r = DH[x, 8:72] * (C[0, x, 16:80] - u + Q[0, x, 16:80] * us)
            total = r if total is None else total + r
        bufs[0, i] = row_pairs(0, total)
    loop(0, 8, residual)
    L1[4, 8:16, 16:48] = dot(bufs[0].reshape(256, 128), restrict).reshape(8, 32, 128)
    pack1(4)
    a1 = send_z(zs1, zr1, 4, 1, s_a1, r_a1, 1)
    r1 = send_1(L1, 4, 1, s_b1.at[1], r_b1.at[1])

    def prepare(ref, inv, a, x_lo, x_hi, rows, inside):
        def body(x):
            i = jnp.where(inside(x), ref[0, x, 8 : 8 + rows], 0.0)
            inv[x, 8 : 8 + rows] = i
            a[0, x] = i * ref[1, x, 8 : 8 + rows]
            a[1, x] = i * ref[1, x + 1, 8 : 8 + rows]
            a[2, x] = i * ref[2, x, 8 : 8 + rows]
            a[3, x] = i * ref[2, x, 9 : 9 + rows]
            a[4, x] = i * ref[3, x, 8 : 8 + rows]
            a[5, x] = i * pltpu.roll(ref[3, x, 8 : 8 + rows], 127, 1)
        loop(x_lo, x_hi, body)

    def apply(c, a, e, x, rows):
        v = e[x, 8 : 8 + rows]
        return v, (
            (c[x] - v)
            + (a[0, x] * e[x - 1, 8 : 8 + rows] + a[1, x] * e[x + 1, 8 : 8 + rows])
            + (a[2, x] * e[x, 7 : 7 + rows] + a[3, x] * e[x, 9 : 9 + rows])
            + (a[4, x] * pltpu.roll(v, 1, 1) + a[5, x] * pltpu.roll(v, 127, 1))
        )

    def begin(c, e, d, x_lo, x_hi, rows):
        def body(x):
            u = c[x] * (1.0 / THETA)
            e[x, 8 : 8 + rows] = u
            d[x, 0:rows] = u
        loop(x_lo, x_hi, body)

    def relax(c, a, e, new, d, x_lo, x_hi, rows, alpha, beta):
        def body(x):
            v, g = apply(c, a, e, x, rows)
            step = beta * g if alpha is None else alpha * d[x, 0:rows] + beta * g
            return [
                (d, (x, slice(0, rows)), step),
                (new, (x, slice(8, 8 + rows)), v + step),
            ]
        grouped(x_lo, x_hi, 4 if rows == 32 else 2, body)

    yz1 = (
        (gy * 32 + row48 - 8 >= 0) & (gy * 32 + row48 - 8 < 128)
        & (gz * 64 + lane48 - 32 >= 0) & (gz * 64 + lane48 - 32 < 512)
    )

    def inside1(x):
        ok = ((gx * 8 + x - 8) >= 0) & ((gx * 8 + x - 8) < 32)
        return jnp.where(ok, jnp.where(yz1, 1.0, 0.0), 0.0) > 0.5

    row32 = rows_of(32)
    yz2 = (
        (gy * 16 + row32 - 8 >= 0) & (gy * 16 + row32 - 8 < 64)
        & (gz * 32 + lane32 - 48 >= 0) & (gz * 32 + lane32 - 48 < 256)
    )

    def assemble1(x):
        for a in range(4):
            base = pltpu.roll(LP[a // 2, x, 8:56], 32 if a % 2 == 0 else 96, 1)
            L1[a, x, 8:56] = extended1(a, x, base)
    for copy in a1:
        copy.wait_recv()
    join1(4)
    c1r = send_c1(4, 1, 1)
    for copy in a2:
        copy.wait_recv()
    loop(0, 4, join2)
    b2 = send_2(LQ, 0, 4, s_b2.at[0], r_b2.at[0])
    c2 = send_2(zc2, 0, 4, s_c2.at[0], r_c2.at[0])
    started += a1 + r1 + c1r + b2 + c2
    for copy in b1 + c1s:
        copy.wait_recv()
    loop(1, X1 - 1, assemble1)
    prepare(L1, I1, A1, 1, X1 - 1, 48, inside1)
    for copy in r1 + c1r:
        copy.wait_recv()

    def scale1(x):
        C1[x] = I1[x, 8:56] * extended1(4, x, L1[4, x, 8:56])
    loop(1, X1 - 1, scale1)
    begin(C1, ea1, d1, 1, X1 - 1, 48)
    relax(C1, A1, ea1, eb1, d1, 2, X1 - 2, 48, *fine[0])
    relax(C1, A1, eb1, ea1, d1, 3, X1 - 3, 48, *fine[1])

    def residual1(i):
        total = None
        for k in range(2):
            x = 8 + 2 * i + k
            _, g = apply(C1, A1, ea1, x, 48)
            r = D1[2 * i + k] * g[8:40]
            total = r if total is None else total + r
        bufs[1, i, 0:16] = row_pairs(1, total)
    loop(0, 4, residual1)
    r2 = dot(jnp.concatenate([bufs[1, i, 0:16] for i in range(4)], 0), restrict)
    for i in range(4):
        L2[4, 4 + 4 * gx + i, 16:32] = r2[16 * i : 16 * i + 16]
    pack2(4)
    a2 = send_z(zs2, zr2, 4, 1, s_a2, r_a2, 1)
    pack_own2(4)
    r2 = send_2(LQ, 4, 1, s_b2.at[1], r_b2.at[1])
    for copy in b2 + c2:
        copy.wait_recv()

    def assemble2(slot):
        for a in range(4):
            for p in range(4):
                L2[a, 4 + 4 * slot + p, 8:40] = extended2(a, slot, p)
    for copy in a2:
        copy.wait_recv()
    join2(4)
    c2r = send_2(zc2, 4, 1, s_c2.at[1], r_c2.at[1])
    loop(0, 4, assemble2)
    prepare(L2, I2, A2, 4, 20, 32, lambda x: yz2)
    started += a2 + r2 + c2r
    for copy in r2 + c2r:
        copy.wait_recv()

    def scale2(slot):
        for p in range(4):
            x = 4 + 4 * slot + p
            C2[x] = I2[x, 8:40] * extended2(4, slot, p)
    loop(0, 4, scale2)
    begin(C2, ea2, d2, 4, 20, 32)
    pair = (ea2, eb2)
    for n, f in enumerate(factors(COARSE_STEPS)):
        relax(C2, A2, pair[n % 2], pair[1 - n % 2], d2, 4, 20, 32, *f)
    e2 = pair[(COARSE_STEPS - 1) % 2]

    widen = jnp.where(wr == 32 + wc // 2, 1.0, 0.0)

    def up1(i):
        v = dot(e2[4 * gx + i, 8:40], widen)
        pro[0, pl.ds(0, 32, stride=2)] = v
        pro[0, pl.ds(1, 32, stride=2)] = v
        for k in range(2):
            ea1[2 * i + k, 8:56] = ea1[2 * i + k, 8:56] + pro[0, 8:56]
    loop(1, 11, up1)
    relax(C1, A1, ea1, eb1, d1, 3, X1 - 3, 48, None, 1.0 / THETA)
    relax(C1, A1, eb1, ea1, d1, 4, X1 - 4, 48, *fine[0])
    relax(C1, A1, ea1, eb1, d1, 5, X1 - 5, 48, *fine[1])

    beyond = jnp.where(
        ((wc < 8) & (wr == 96 + wc // 2)) | ((wc >= 120) & (wr == 28 + (wc - 120) // 2)), 1.0, 0.0
    )

    def up0(i):
        e = eb1[4 + i, 8:56]
        for k, w in enumerate((widen, beyond)):
            v = dot(e, w)
            pro[k, pl.ds(0, 48, stride=2)] = v
            pro[k, pl.ds(1, 48, stride=2)] = v
        for n in range(2):
            for k in range(2):
                x = 2 * i + n
                UA[k, x, 8:88] = UA[k, x, 8:88] + H[k, x, 8:88] * pro[k, 8:88]
    loop(2, 14, up0)
    smooth(UA, UB, 6, 26, None, 1.0 / THETA)
    smooth(UB, UA, 7, 25, *fine[0])

    def finish(x):
        u, us = own_sum(UA, 8 + x)
        alpha, beta = fine[1]
        d = alpha * DU[0, 8 + x, 16:80] + beta * (C[0, 8 + x, 16:80] - u + Q[0, 8 + x, 16:80] * us)
        out[x] = (u + d) / H[0, 8 + x, 16:80]
    loop(0, 16, finish)

    for copy in started:
        copy.wait_send()


def shards(image, labels):
    def level0():
        return pltpu.VMEM((2, X0, Y0, 128), F32)

    def vmem(*shape):
        return pltpu.VMEM(shape, F32)

    def sems(*shape):
        return pltpu.SemaphoreType.DMA(shape)

    scratch = [vmem(X0, Y0, 128), vmem(X0, Y0, 128)] + [level0() for _ in range(8)] + [
        vmem(X0, 80, 128), vmem(2, 80, 128),
        vmem(2, 2, 64, 128), vmem(2, 3, 2, 80, 128), vmem(3, 64, 128), vmem(2, 8, 32, 128), vmem(8, 40, 128),
        vmem(8, 32, 128), vmem(9, 32, 128), vmem(8, 48, 128), vmem(8, 32, 128), vmem(8, 32, 128),
        vmem(5, X1, Y1, 128), vmem(2, X1, Y1, 128), vmem(5, 32, 128), vmem(2, 5, 32, 128), vmem(5, 3, 48, 128), vmem(6, X1, 48, 128),
        vmem(X1, Y1, 128), vmem(X1, 48, 128), vmem(X1, Y1, 128), vmem(X1, Y1, 128), vmem(X1, Y1, 128),
        vmem(5, X2, Y2, 128), vmem(5, 4, 32, 128), vmem(5, 16, 128), vmem(2, 5, 16, 128), vmem(5, 4, 32, 128), vmem(6, X2, 32, 128),
        vmem(X2, Y2, 128), vmem(X2, 32, 128), vmem(X2, Y2, 128), vmem(X2, Y2, 128), vmem(X2, Y2, 128),
        vmem(4, 16, 128), vmem(2, 96, 128),
        sems(8), sems(8), sems(8), sems(8), sems(2, 2), sems(2, 2), sems(2, 8), sems(2, 8),
        sems(2, 2), sems(2, 2), sems(2, 8), sems(2, 8), sems(2, 8), sems(2, 8),
        sems(2, 2), sems(2, 2), sems(2, 11), sems(2, 11), sems(2, 11), sems(2, 11),
    ]
    return pl.pallas_call(
        kernel,
        out_shape=jax.ShapeDtypeStruct(image.shape, F32),
        in_specs=[pl.BlockSpec(memory_space=pltpu.VMEM)] * 2,
        out_specs=pl.BlockSpec(memory_space=pltpu.VMEM),
        scratch_shapes=scratch,
        compiler_params=pltpu.CompilerParams(
            collective_id=0, has_side_effects=True, vmem_limit_bytes=56 * 1024 * 1024
        ),
    )(image, labels)


def solution(mesh):
    placed = (P("gx", "gy", "gz"), P("gx", "gy", "gz"))
    return jax.shard_map(
        shards, mesh=mesh, in_specs=placed, out_specs=P("gx", "gy", "gz"), check_vma=False
    )
```

```python
import jax
import jax.numpy as jnp
from jax import lax
from jax.experimental import pallas as pl
from jax.experimental.pallas import tpu as pltpu
from jax.sharding import PartitionSpec as P

SMOOTH_STEPS = 3
COARSE_STEPS = 6
HEAT_CONSTANT = 0.25
SCREENING = 0.002
SEED_WEIGHT = 1.0
THETA = 1.1
DELTA = 0.9

MESH = pl.DeviceIdType.MESH
F32 = jnp.float32
SIZES = {"gx": 4, "gy": 4, "gz": 8}

X0, Y0 = 32, 96
X1, Y1 = 24, 64
X2, Y2 = 24, 48

PLANAR = [(dx, dy) for dx in (1, -1, 0) for dy in (1, -1, 0) if (dx, dy) != (0, 0)]
COLUMN = [(dx, dy) for dx in (1, -1, 2, 0) for dy in (1, -1, 0) if (dx, dy) != (0, 0)]


def factors(steps):
    sigma = THETA / DELTA
    rho = 1.0 / sigma
    out = []
    for _ in range(steps - 1):
        rho_new = 1.0 / (2.0 * sigma - rho)
        out.append((rho_new * rho, 2.0 * rho_new / DELTA))
        rho = rho_new
    return out


def peer(dx, dy, dz):
    shift = {"gx": dx, "gy": dy, "gz": dz}
    return {a: lax.rem(lax.axis_index(a) + shift[a] + n, n) for a, n in SIZES.items()}


def dot(a, b):
    return jnp.dot(a, b, precision=lax.Precision.HIGHEST, preferred_element_type=F32)


def kernel(
    image_hbm, labels_hbm, out_hbm,
    image, labels, out,
    E, L, EM, R, H, UA, UB, DU, C, Q, DH, M,
    zs0, zr0, tmp, bufs, wyb, c1, wx1, wy1, wz1, D1,
    L1, LP, zs1, zr1, zc1, A1, I1, C1, ea1, eb1, d1,
    L2, LQ, zs2, zr2, zc2, A2, I2, C2, ea2, eb2, d2, D2, pro, PR,
    s_e, r_e, s_l, r_l, s_z0, r_z0, s_b0, r_b0,
    s_a1, r_a1, s_b1, r_b1, s_c1, r_c1, s_a2, r_a2, s_b2, r_b2, s_c2, r_c2,
    s_in, s_out,
):
    gx, gy, gz = (lax.axis_index(a) for a in ("gx", "gy", "gz"))
    barrier = pltpu.get_barrier_semaphore()
    partners = [(dx, dy, 0) for dx, dy in COLUMN] + [(0, 0, 1), (0, 0, -1)]
    for p in partners:
        pl.semaphore_signal(barrier, inc=1, device_id=peer(*p), device_id_type=MESH)

    loads = [
        pltpu.make_async_copy(image_hbm, image, s_in.at[0]),
        pltpu.make_async_copy(labels_hbm, labels, s_in.at[1]),
    ]
    for copy in loads:
        copy.start()

    def lanes(rows):
        return lax.broadcasted_iota(jnp.int32, (rows, 128), 1)

    def rows_of(rows):
        return lax.broadcasted_iota(jnp.int32, (rows, 128), 0)

    def send(src, dst, ssem, rsem, to):
        copy = pltpu.make_async_remote_copy(
            src_ref=src, dst_ref=dst, send_sem=ssem, recv_sem=rsem, device_id=to, device_id_type=MESH
        )
        copy.start()
        return copy

    started = []

    def loop(lo, hi, body):
        def step(i, carry):
            body(i)
            return carry
        lax.fori_loop(lo, hi, step, 0)

    loads[0].wait()

    def own(x):
        E[8 + x, 16:80] = jnp.exp(image[x] * (1.0 / HEAT_CONSTANT))
    loop(0, 16, own)
    pl.semaphore_wait(barrier, len(partners))

    def x_range(dx, start, count, width):
        if dx == 0:
            return pl.ds(start, count), pl.ds(start, count)
        if dx == 1:
            return pl.ds(start + count - width, width), pl.ds(start - width, width)
        return pl.ds(start, width), pl.ds(start + count, width)

    def y_range(dy, start, count):
        if dy == 0:
            return pl.ds(start, count), pl.ds(start, count)
        if dy == 1:
            return pl.ds(start + count - 8, 8), pl.ds(start - 8, 8)
        return pl.ds(start, 8), pl.ds(start + count, 8)

    def send_own(ref, width, ssem, rsem):
        copies = []
        for i, (dx, dy) in enumerate(PLANAR):
            ys, yd = y_range(dy, 16, 64)
            xs, xd = x_range(dx, 8, 16, width)
            copies.append(send(ref.at[xs, ys], ref.at[xd, yd], ssem.at[i], rsem.at[i], peer(dx, dy, 0)))
        return copies

    own_e = send_own(E, 7, s_e, r_e)
    loads[1].wait()

    def own_labels(x):
        L[8 + x, 16:80] = labels[x].astype(F32)
    loop(0, 16, own_labels)

    group64 = lanes(64) // 8

    def pack(p, carry):
        result = []
        for k, ref in enumerate((E, L)):
            v = ref[8 + p, 16:80]
            low = pltpu.roll(v, lax.rem(8 * p, 128), 1)
            high = pltpu.roll(v, lax.rem(8 * p + 8, 128), 1)
            result.append(jnp.where(group64 == p, low, carry[2 * k]))
            result.append(jnp.where(group64 == p, high, carry[2 * k + 1]))
        return tuple(result)

    zero64 = jnp.zeros((64, 128), F32)
    packed = lax.fori_loop(0, 16, pack, (zero64,) * 4)
    for k in range(2):
        zs0[k, 1] = packed[2 * k]
        zs0[k, 0] = packed[2 * k + 1]
    za = [
        [
            send(zs0.at[k, s], zr0.at[k, 1, s, pl.ds(8, 64)], s_z0.at[k, s], r_z0.at[k, s],
                 peer(0, 0, 1 if s == 0 else -1))
            for s in range(2)
        ]
        for k in range(2)
    ]

    def forward(k):
        for copy in za[k]:
            copy.wait_recv()
        copies = []
        for i, (dx, dy) in enumerate(PLANAR):
            ys, yd = y_range(dy, 8, 64)
            copies.append(send(zr0.at[k, 1, :, ys], zr0.at[k, 1 - dx, :, yd],
                               s_b0.at[k, i], r_b0.at[k, i], peer(dx, dy, 0)))
        return copies

    for ref in (ea1, eb1, d1):
        def clear(x, ref=ref):
            ref[x] = jnp.zeros((Y1, 128), F32)
        loop(0, X1, clear)
    for ref in (ea2, eb2, d2):
        def clear(x, ref=ref):
            ref[x] = jnp.zeros((Y2, 128), F32)
        loop(0, X2, clear)

    def guard1(a):
        for x in (0, X1 - 1):
            L1[a, x] = jnp.zeros((Y1, 128), F32)

        def edge(x):
            L1[a, x, 0:8] = jnp.zeros((8, 128), F32)
            L1[a, x, 56:64] = jnp.zeros((8, 128), F32)
        loop(1, X1 - 1, edge)
    loop(0, 5, guard1)

    def guard2(a):
        for x in (0, 1, 2, 3, 20, 21, 22, 23):
            L2[a, x] = jnp.zeros((Y2, 128), F32)

        def edge(x):
            L2[a, x, 0:8] = jnp.zeros((8, 128), F32)
            L2[a, x, 40:48] = jnp.zeros((8, 128), F32)
        loop(4, 20, edge)
    loop(0, 5, guard2)

    lane80, row80 = lanes(80), rows_of(80)
    y_in = ((gy * 64 + row80 - 8) >= 0) & ((gy * 64 + row80 - 8) < 256)
    M[0] = jnp.where(y_in, 1.0, 0.0)
    z_in = ((lane80 < 8) & (gz < 7)) | ((lane80 >= 120) & (gz > 0))
    M[1] = jnp.where(y_in & z_in, 1.0, 0.0)

    zb_e = forward(0)
    own_l = send_own(L, 5, s_l, r_l)
    zb_l = forward(1)
    started += za[0] + za[1] + own_e + own_l + zb_e + zb_l
    for i, (dx, dy) in enumerate(PLANAR):
        if dx == 0:
            own_e[i].wait_recv()
            zb_e[i].wait_recv()

    def x_in(x):
        return ((gx * 16 + x - 8) >= 0) & ((gx * 16 + x - 8) < 64)

    CH, GROUP, CHC = 16, 4, 16

    def sweep(lo_x, hi_x, work, n=GROUP):
        def step(x, n):
            for lo in range(8, 88, CH):
                stores = []
                for j in range(n):
                    stores += work(x + j, lo)
                for ref, index, value in stores:
                    ref[index] = value

        def body(i, carry):
            step(lo_x + n * i, n)
            return carry
        lax.fori_loop(0, (hi_x - lo_x) // n, body, 0)
        if (hi_x - lo_x) % n:
            step(hi_x - (hi_x - lo_x) % n, (hi_x - lo_x) % n)

    lane = lanes(CH)
    at0, at127 = lane == 0, lane == 127

    def z_pair(t0, t1):
        r0, r1 = pltpu.roll(t0, 1, 1), pltpu.roll(t1, 1, 1)
        q0, q1 = pltpu.roll(t0, 127, 1), pltpu.roll(t1, 127, 1)
        return (
            jnp.where(at0, r1, r0) + jnp.where(at127, q1, q0),
            jnp.where(at0, r0, r1) + jnp.where(at127, q0, q1),
        )

    def around(ref, x, lo):
        t = [ref[k, x, lo : lo + CH] for k in range(2)]
        z = z_pair(*t)
        total = []
        for k in range(2):
            total.append(
                (ref[k, x - 1, lo : lo + CH] + ref[k, x + 1, lo : lo + CH])
                + (ref[k, x, lo - 1 : lo + CH - 1] + ref[k, x, lo + 1 : lo + CH + 1])
                + z[k]
            )
        return t, total

    def ends(k, x, r):
        p, n = lax.rem(x + 8, 16), (x + 8) // 16
        up = pltpu.roll(zr0[k, n, 1, r], lax.rem(256 - 8 * p, 128), 1)
        down = pltpu.roll(zr0[k, n, 0, r], lax.rem(248 - 8 * p, 128), 1)
        return jnp.where(lane < 8, up, down)

    def spread(x, lo):
        inside = x_in(x)
        r = pl.ds(lo - 8, CH)
        s = slice(lo, lo + CH)
        stores = []
        for t, v in ((0, E[x, s]), (1, ends(0, x, r))):
            m = jnp.where(inside, M[t, r], 0.0) > 0.5
            v = jnp.where(m, v, 1.0)
            stores += [(EM, (t, x, s), v), (R, (t, x, s), 1.0 / v)]
        return stores

    sweep(8, 24, spread)

    def heights(x, lo):
        e, es = around(EM, x, lo)
        c, cs = around(R, x, lo)
        stores = []
        for k in range(2):
            t = (e[k] + es[k]) * (c[k] + cs[k])
            stores.append((H, (k, x, slice(lo, lo + CH)), lax.rsqrt(lax.rsqrt(lax.rsqrt(t)))))
        return stores

    sweep(9, 23, heights)
    for i, (dx, dy) in enumerate(PLANAR):
        if dx != 0:
            own_e[i].wait_recv()
            zb_e[i].wait_recv()
    sweep(6, 8, spread)
    sweep(24, 26, spread)
    sweep(7, 9, heights)
    sweep(23, 25, heights)

    def cells_of(v):
        return SCREENING + SEED_WEIGHT * jnp.where(v != 2.0, 1.0, 0.0)

    def row_pairs(slot, v):
        n = v.shape[0]
        tmp[slot, 0:n] = v
        return tmp[slot, pl.ds(0, n // 2, stride=2)] + tmp[slot, pl.ds(1, n // 2, stride=2)]

    lane64 = lanes(64)

    def coarse(i):
        x = 8 + 2 * i
        bufs[0, i] = row_pairs(0, cells_of(L[x, 16:80]) + cells_of(L[x + 1, 16:80]))
        wyb[i] = (
            H[0, x, pl.ds(16, 40, stride=2)] * H[0, x, pl.ds(15, 40, stride=2)]
            + H[0, x + 1, pl.ds(16, 40, stride=2)] * H[0, x + 1, pl.ds(15, 40, stride=2)]
        )
        total = None
        for k in range(2):
            h0, h1 = H[0, x + k, 16:80], H[1, x + k, 16:80]
            r0, r1 = pltpu.roll(h0, 1, 1), pltpu.roll(h1, 1, 1)
            v = h0 * jnp.where(lane64 == 0, r1, r0)
            beyond = pltpu.roll(h1, 1, 1) * pltpu.roll(h0, 2, 1)
            v = jnp.where(lane64 == 1, beyond, v)
            total = v if total is None else total + v
        bufs[1, i] = row_pairs(1, total)
    loop(0, 8, coarse)

    def coarse_x(i):
        x = 8 + 2 * i
        wx1[i] = row_pairs(2, H[0, x, 16:80] * H[0, x - 1, 16:80])
    loop(0, 9, coarse_x)

    wr, wc = rows_of(128), lanes(128)
    restrict = jnp.where(wc == 32 + wr // 2, 1.0, 0.0)
    even = jnp.where((wc == 32 + wr // 2) & (lax.rem(wr, 2) == 0), 1.0, 0.0)
    last = jnp.where((wr == 1) & (wc == 96), 1.0, 0.0)
    c1[...] = dot(bufs[0].reshape(256, 128), restrict).reshape(8, 32, 128)
    wx1[...] = dot(wx1[...].reshape(288, 128), restrict).reshape(9, 32, 128)
    wy1[:, 0:40] = dot(wyb[...].reshape(320, 128), restrict).reshape(8, 40, 128)
    wz1[...] = dot(bufs[1].reshape(256, 128), even + last).reshape(8, 32, 128)

    lane32 = lanes(32)
    own1 = (lane32 >= 32) & (lane32 < 96)

    def level1(i):
        wz = wz1[i]
        d = (
            c1[i] + (wx1[i] + wx1[i + 1]) + (wy1[i, 0:32] + wy1[i, 1:33])
            + (wz + pltpu.roll(wz, 127, 1))
        )
        D1[i] = jnp.where(own1, d, 0.0)
        four = (jnp.where(own1, 1.0 / jnp.where(own1, d, 1.0), 0.0), wx1[i], wy1[i, 0:32], wz)
        for a in range(4):
            L1[a, 8 + i, 16:48] = four[a]
        for a in range(2):
            LP[a, 8 + i, 16:48] = jnp.where(
                lane32 < 64, pltpu.roll(four[2 * a], 96, 1), pltpu.roll(four[2 * a + 1], 32, 1)
            )
    loop(0, 8, level1)

    def send_1(src, which, width, ssem, rsem):
        copies = []
        for i, (dx, dy) in enumerate(PLANAR):
            ys, yd = y_range(dy, 16, 32)
            xs, xd = x_range(dx, 8, 8, 7)
            copies.append(send(src.at[pl.ds(which, width), xs, ys], src.at[pl.ds(which, width), xd, yd],
                               ssem.at[i], rsem.at[i], peer(dx, dy, 0)))
        return copies

    b1 = send_1(LP, 0, 2, s_b1.at[0], r_b1.at[0])

    lane16 = lanes(16)
    own2 = (lane16 >= 48) & (lane16 < 80)
    c2 = [row_pairs(0, c1[2 * i] + c1[2 * i + 1]) for i in range(4)]
    z2 = [row_pairs(1, wz1[2 * i] + wz1[2 * i + 1]) for i in range(4)]
    x2 = [row_pairs(2, wx1[2 * i]) for i in range(5)]
    y2 = [
        wy1[2 * i, pl.ds(0, 24, stride=2)] + wy1[2 * i + 1, pl.ds(0, 24, stride=2)] for i in range(4)
    ]
    c2 = dot(jnp.concatenate(c2, 0), restrict)
    x2 = dot(jnp.concatenate(x2, 0), restrict)
    y2 = dot(jnp.concatenate(y2, 0), restrict)
    z2 = dot(jnp.concatenate(z2, 0), even)
    for i in range(4):
        for k in range(3):
            tmp[k, 0:24] = y2[24 * i : 24 * i + 24]
        wz = z2[16 * i : 16 * i + 16]
        d = (
            c2[16 * i : 16 * i + 16]
            + (x2[16 * i : 16 * i + 16] + x2[16 * i + 16 : 16 * i + 32])
            + (tmp[0, 0:16] + tmp[0, 1:17]) + (wz + pltpu.roll(wz, 127, 1))
        )
        D2[i] = jnp.where(own2, d, 0.0)
        at = 4 + 4 * gx + i
        L2[0, at, 16:32] = jnp.where(own2, 1.0 / jnp.where(own2, d, 1.0), 0.0)
        L2[1, at, 16:32] = x2[16 * i : 16 * i + 16]
        L2[2, at, 16:32] = tmp[0, 0:16]
        L2[3, at, 16:32] = wz

    group32, group16 = lane32 // 8, lane16 // 8

    def pack_z(ref, a, base, planes, rows, lo, hi, group, dst):
        acc = jnp.zeros((rows, 128), F32)
        for p in range(planes):
            v = ref[a, base + p, 16 : 16 + rows]
            acc = jnp.where(group == p, pltpu.roll(v, (8 * p - lo) % 128, 1), acc)
            acc = jnp.where(group == 8 + p, pltpu.roll(v, (64 + 8 * p - hi) % 128, 1), acc)
        dst[a] = acc

    def joined(zr, zc, a, slot, rows, ln):
        zc[a, slot, 8 : 8 + rows] = jnp.where(ln < 64, zr[1, a], zr[0, a])

    def extended(base, ends, p, ln, lo, hi):
        down = pltpu.roll(ends, lax.rem(256 + lo - 8 - 64 - 8 * p, 128), 1)
        up = pltpu.roll(ends, lax.rem(256 + hi + 8 - 8 * p, 128), 1)
        v = jnp.where((ln >= lo) & (ln < hi + 8), base, 0.0)
        v = jnp.where((ln >= lo - 8) & (ln < lo), down, v)
        return jnp.where((ln >= hi + 8) & (ln < hi + 16), up, v)

    def pack1(a):
        pack_z(L1, a, 8, 8, 32, 32, 88, group32, zs1)

    def join1(a):
        joined(zr1, zc1, a, 1, 32, lane32)

    def extended1(a, x, base):
        return extended(base, zc1[a, x // 8], lax.rem(x, 8), lane48, 32, 88)

    def pack2(a):
        pack_z(L2, a, 4 + 4 * gx, 4, 16, 48, 72, group16, zs2)

    def join2(a):
        joined(zr2, zc2, a, gx, 16, lane16)

    def pack_own2(a):
        acc = jnp.zeros((16, 128), F32)
        for p in range(4):
            v = pltpu.roll(L2[a, 4 + 4 * gx + p, 16:32], (32 * p - 48) % 128, 1)
            acc = jnp.where(lane16 // 32 == p, v, acc)
        LQ[a, gx, 8:24] = acc

    def extended2(a, slot, p):
        base = pltpu.roll(LQ[a, slot], (48 - 32 * p) % 128, 1)
        return extended(base, zc2[a, slot], p, lane32, 48, 72)

    def send_z(zs, zr, which, n, ssem, rsem, slot):
        return [
            send(zs.at[pl.ds(which, n)], zr.at[s, pl.ds(which, n)], ssem.at[slot, s], rsem.at[slot, s],
                 peer(0, 0, 1 if s == 0 else -1))
            for s in range(2)
        ]

    def send_c1(which, n, slot):
        copies = []
        for i, (dx, dy) in enumerate(PLANAR):
            ys, yd = y_range(dy, 8, 32)
            copies.append(send(zc1.at[pl.ds(which, n), 1, ys], zc1.at[pl.ds(which, n), 1 - dx, yd],
                               s_c1.at[slot, i], r_c1.at[slot, i], peer(dx, dy, 0)))
        return copies

    def send_2(ref, which, n, ssem, rsem):
        copies = []
        for i, (dx, dy) in enumerate(COLUMN):
            ys, yd = y_range(dy, 8, 16)
            copies.append(send(ref.at[pl.ds(which, n), gx, ys], ref.at[pl.ds(which, n), gx, yd],
                               ssem.at[i], rsem.at[i], peer(dx, dy, 0)))
        return copies

    lane48, row48 = lanes(48), rows_of(48)
    loop(0, 4, pack1)
    a1 = send_z(zs1, zr1, 0, 4, s_a1, r_a1, 0)
    loop(0, 4, pack2)
    a2 = send_z(zs2, zr2, 0, 4, s_a2, r_a2, 0)
    loop(0, 4, pack_own2)
    sweep(1, 6, spread)
    sweep(26, 31, spread)
    sweep(2, 7, heights)
    sweep(25, 30, heights)
    for copy in a1:
        copy.wait_recv()
    loop(0, 4, join1)
    c1s = send_c1(0, 4, 0)

    def diagonal(x, lo):
        inside = x_in(x)
        h, hs = around(H, x, lo)
        r = pl.ds(lo - 8, CH)
        s = slice(lo, lo + CH)
        stores = []
        for k in range(2):
            m = jnp.where(inside, M[k, r], 0.0)
            lab = L[x, s] if k == 0 else ends(1, x, r)
            d = cells_of(lab) + h[k] * hs[k]
            hi = m * h[k] / d
            c = jnp.where(lab == 1.0, SEED_WEIGHT * hi, 0.0)
            u = c * (1.0 / THETA)
            stores += [
                (C, (k, x, s), c), (Q, (k, x, s), hi * h[k]), (UA, (k, x, s), u), (DU, (k, x, s), u)
            ]
            if k == 0:
                stores.append((DH, (x, r), d / h[k]))
        return stores

    for copy in own_l + zb_l:
        copy.wait_recv()
    sweep(3, 29, diagonal)
    started += a1 + a2 + b1 + c1s

    def smooth(src, dst, lo_x, hi_x, alpha, beta, keep=True):
        def work(x, lo):
            u, us = around(src, x, lo)
            s = slice(lo, lo + CH)
            stores = []
            for k in range(2):
                g = beta * (C[k, x, s] - u[k] + Q[k, x, s] * us[k])
                d = g if alpha is None else alpha * DU[k, x, s] + g
                if keep:
                    stores.append((DU, (k, x, s), d))
                stores.append((dst, (k, x, s), u[k] + d))
            return stores
        sweep(lo_x, hi_x, work)

    fine = factors(SMOOTH_STEPS)
    smooth(UA, UB, 4, 28, *fine[0])
    smooth(UB, UA, 5, 27, *fine[1], keep=False)

    lane_ch = lanes(CH)

    def own_sum(ref, x, lo):
        t0, t1 = ref[0, x, lo : lo + CH], ref[1, x, lo : lo + CH]
        low = jnp.where(lane_ch == 0, pltpu.roll(t1, 1, 1), pltpu.roll(t0, 1, 1))
        high = jnp.where(lane_ch == 127, pltpu.roll(t1, 127, 1), pltpu.roll(t0, 127, 1))
        return t0, (
            (ref[0, x - 1, lo : lo + CH] + ref[0, x + 1, lo : lo + CH])
            + (ref[0, x, lo - 1 : lo + CH - 1] + ref[0, x, lo + 1 : lo + CH + 1]) + (low + high)
        )

    def residual(i):
        x = 8 + 2 * i
        for lo in range(16, 80, CH):
            total = None
            for k in range(2):
                u, us = own_sum(UA, x + k, lo)
                r = DH[x + k, lo - 8 : lo - 8 + CH] * (
                    C[0, x + k, lo : lo + CH] - u + Q[0, x + k, lo : lo + CH] * us
                )
                total = r if total is None else total + r
            tmp[0, lo - 16 : lo - 16 + CH] = total
        bufs[0, i] = tmp[0, pl.ds(0, 32, stride=2)] + tmp[0, pl.ds(1, 32, stride=2)]
    loop(0, 8, residual)
    L1[4, 8:16, 16:48] = dot(bufs[0].reshape(256, 128), restrict).reshape(8, 32, 128)
    pack1(4)
    a1 = send_z(zs1, zr1, 4, 1, s_a1, r_a1, 1)
    r1 = send_1(L1, 4, 1, s_b1.at[1], r_b1.at[1])

    def prepare(ref, inv, a, x_lo, x_hi, rows, inside):
        def body(x):
            i = jnp.where(inside(x), ref[0, x, 8 : 8 + rows], 0.0)
            inv[x, 8 : 8 + rows] = i
            a[0, x] = i * ref[1, x, 8 : 8 + rows]
            a[1, x] = i * ref[1, x + 1, 8 : 8 + rows]
            a[2, x] = i * ref[2, x, 8 : 8 + rows]
            a[3, x] = i * ref[2, x, 9 : 9 + rows]
            a[4, x] = i * ref[3, x, 8 : 8 + rows]
            a[5, x] = i * pltpu.roll(ref[3, x, 8 : 8 + rows], 127, 1)
        loop(x_lo, x_hi, body)

    def apply(c, a, e, x, lo, n):
        r, s = slice(lo - 8, lo - 8 + n), slice(lo, lo + n)
        v = e[x, s]
        return v, (
            (c[x, r] - v)
            + (a[0, x, r] * e[x - 1, s] + a[1, x, r] * e[x + 1, s])
            + (a[2, x, r] * e[x, lo - 1 : lo - 1 + n] + a[3, x, r] * e[x, lo + 1 : lo + 1 + n])
            + (a[4, x, r] * pltpu.roll(v, 1, 1) + a[5, x, r] * pltpu.roll(v, 127, 1))
        )

    def begin(c, e, d, x_lo, x_hi, rows):
        def body(x):
            u = c[x] * (1.0 / THETA)
            e[x, 8 : 8 + rows] = u
            d[x, 0:rows] = u
        loop(x_lo, x_hi, body)

    def relax(c, a, e, new, d, x_lo, x_hi, rows, alpha, beta):
        n = 2 if rows == 48 else 4

        def step(x, n):
            for lo in range(8, 8 + rows, CHC):
                values = []
                for j in range(n):
                    v, g = apply(c, a, e, x + j, lo, CHC)
                    r = slice(lo - 8, lo - 8 + CHC)
                    move = beta * g if alpha is None else alpha * d[x + j, r] + beta * g
                    values += [(d, (x + j, r), move), (new, (x + j, slice(lo, lo + CHC)), v + move)]
                for ref, index, value in values:
                    ref[index] = value

        def body(i, carry):
            step(x_lo + n * i, n)
            return carry
        lax.fori_loop(0, (x_hi - x_lo) // n, body, 0)
        if (x_hi - x_lo) % n:
            step(x_hi - (x_hi - x_lo) % n, (x_hi - x_lo) % n)

    yz1 = (
        (gy * 32 + row48 - 8 >= 0) & (gy * 32 + row48 - 8 < 128)
        & (gz * 64 + lane48 - 32 >= 0) & (gz * 64 + lane48 - 32 < 512)
    )

    def inside1(x):
        ok = ((gx * 8 + x - 8) >= 0) & ((gx * 8 + x - 8) < 32)
        return jnp.where(ok, jnp.where(yz1, 1.0, 0.0), 0.0) > 0.5

    row32 = rows_of(32)
    yz2 = (
        (gy * 16 + row32 - 8 >= 0) & (gy * 16 + row32 - 8 < 64)
        & (gz * 32 + lane32 - 48 >= 0) & (gz * 32 + lane32 - 48 < 256)
    )

    def assemble1(x):
        for a in range(4):
            base = pltpu.roll(LP[a // 2, x, 8:56], 32 if a % 2 == 0 else 96, 1)
            L1[a, x, 8:56] = extended1(a, x, base)
    for copy in a1:
        copy.wait_recv()
    join1(4)
    c1r = send_c1(4, 1, 1)
    for copy in a2:
        copy.wait_recv()
    loop(0, 4, join2)
    b2 = send_2(LQ, 0, 4, s_b2.at[0], r_b2.at[0])
    c2 = send_2(zc2, 0, 4, s_c2.at[0], r_c2.at[0])
    started += a1 + r1 + c1r + b2 + c2
    for copy in b1 + c1s:
        copy.wait_recv()
    loop(1, X1 - 1, assemble1)
    prepare(L1, I1, A1, 1, X1 - 1, 48, inside1)
    for copy in r1 + c1r:
        copy.wait_recv()

    def scale1(x):
        C1[x] = I1[x, 8:56] * extended1(4, x, L1[4, x, 8:56])
    loop(1, X1 - 1, scale1)
    begin(C1, ea1, d1, 1, X1 - 1, 48)
    relax(C1, A1, ea1, eb1, d1, 2, X1 - 2, 48, *fine[0])
    relax(C1, A1, eb1, ea1, d1, 3, X1 - 3, 48, *fine[1])

    def residual1(i):
        total = None
        for k in range(2):
            x = 8 + 2 * i + k
            _, g = apply(C1, A1, ea1, x, 16, 32)
            r = D1[2 * i + k] * g
            total = r if total is None else total + r
        bufs[1, i, 0:16] = row_pairs(1, total)
    loop(0, 4, residual1)
    r2 = dot(jnp.concatenate([bufs[1, i, 0:16] for i in range(4)], 0), restrict)
    for i in range(4):
        L2[4, 4 + 4 * gx + i, 16:32] = r2[16 * i : 16 * i + 16]
    pack2(4)
    a2 = send_z(zs2, zr2, 4, 1, s_a2, r_a2, 1)
    pack_own2(4)
    r2 = send_2(LQ, 4, 1, s_b2.at[1], r_b2.at[1])
    for copy in b2 + c2:
        copy.wait_recv()

    def assemble2(slot):
        for a in range(4):
            for p in range(4):
                L2[a, 4 + 4 * slot + p, 8:40] = extended2(a, slot, p)
    for copy in a2:
        copy.wait_recv()
    join2(4)
    c2r = send_2(zc2, 4, 1, s_c2.at[1], r_c2.at[1])
    loop(0, 4, assemble2)
    prepare(L2, I2, A2, 4, 20, 32, lambda x: yz2)
    started += a2 + r2 + c2r
    for copy in r2 + c2r:
        copy.wait_recv()

    def scale2(slot):
        for p in range(4):
            x = 4 + 4 * slot + p
            C2[x] = I2[x, 8:40] * extended2(4, slot, p)
    loop(0, 4, scale2)
    begin(C2, ea2, d2, 4, 20, 32)
    pair = (ea2, eb2)
    for n, f in enumerate(factors(COARSE_STEPS)):
        relax(C2, A2, pair[n % 2], pair[1 - n % 2], d2, 4, 20, 32, *f)
    e2 = pair[(COARSE_STEPS - 1) % 2]

    widen = jnp.where(wr == 32 + wc // 2, 1.0, 0.0)

    PR[0, 0:10, 0:32] = dot(
        e2[pl.ds(4 * gx + 1, 10), 8:40].reshape(320, 128), widen
    ).reshape(10, 32, 128)

    def up1(i):
        for j in range(2):
            v = PR[0, 2 * i + j, 0:32]
            pro[j, pl.ds(0, 32, stride=2)] = v
            pro[j, pl.ds(1, 32, stride=2)] = v
        values = []
        for j in range(2):
            for k in range(2):
                x = 2 + 4 * i + 2 * j + k
                values.append((x, ea1[x, 8:56] + pro[j, 8:56]))
        for x, value in values:
            ea1[x, 8:56] = value
    loop(0, 5, up1)
    relax(C1, A1, ea1, eb1, d1, 3, X1 - 3, 48, None, 1.0 / THETA)
    relax(C1, A1, eb1, ea1, d1, 4, X1 - 4, 48, *fine[0])
    relax(C1, A1, ea1, eb1, d1, 5, X1 - 5, 48, *fine[1])

    beyond = jnp.where(
        ((wc < 8) & (wr == 96 + wc // 2)) | ((wc >= 120) & (wr == 28 + (wc - 120) // 2)), 1.0, 0.0
    )

    both = jnp.concatenate([widen, beyond], 1)
    wide = dot(eb1[6:18, 8:56].reshape(576, 128), both)
    for k in range(2):
        PR[k] = wide[:, 128 * k : 128 * k + 128].reshape(12, 48, 128)

    def up0(i):
        for j in range(2):
            for k in range(2):
                v = PR[k, 2 * i + j]
                pro[2 * j + k, pl.ds(0, 48, stride=2)] = v
                pro[2 * j + k, pl.ds(1, 48, stride=2)] = v
        for lo in range(8, 88, CH):
            s = slice(lo, lo + CH)
            values = []
            for j in range(2):
                for n in range(2):
                    x = 4 + 4 * i + 2 * j + n
                    for k in range(2):
                        values.append(((k, x, s), UA[k, x, s] + H[k, x, s] * pro[2 * j + k, s]))
            for index, value in values:
                UA[index] = value
    loop(0, 6, up0)
    smooth(UA, UB, 6, 26, None, 1.0 / THETA)
    smooth(UB, UA, 7, 25, *fine[0])

    alpha, beta = fine[1]

    def finish(i):
        for lo in range(16, 80, CH):
            values = []
            for k in range(2):
                x = 8 + 2 * i + k
                s = slice(lo, lo + CH)
                u, us = own_sum(UA, x, lo)
                d = alpha * DU[0, x, s] + beta * (C[0, x, s] - u + Q[0, x, s] * us)
                values.append((u + d) / H[0, x, s])
            for k in range(2):
                out[2 * i + k, lo - 16 : lo - 16 + CH] = values[k]
    stores = []
    for part in range(4):
        loop(2 * part, 2 * part + 2, finish)
        planes = pl.ds(4 * part, 4)
        stores.append(pltpu.make_async_copy(out.at[planes], out_hbm.at[planes], s_out.at[part]))
        stores[-1].start()
    for copy in stores:
        copy.wait()

    for copy in started:
        copy.wait_send()


def shards(image, labels):
    def level0():
        return pltpu.VMEM((2, X0, Y0, 128), F32)

    def vmem(*shape):
        return pltpu.VMEM(shape, F32)

    def sems(*shape):
        return pltpu.SemaphoreType.DMA(shape)

    scratch = [vmem(16, 64, 128), pltpu.VMEM((16, 64, 128), jnp.int32), vmem(16, 64, 128)]
    scratch += [vmem(X0, Y0, 128), vmem(X0, Y0, 128)] + [level0() for _ in range(8)] + [
        vmem(X0, 80, 128), vmem(2, 80, 128),
        vmem(2, 2, 64, 128), vmem(2, 3, 2, 80, 128), vmem(3, 64, 128), vmem(2, 8, 32, 128), vmem(8, 40, 128),
        vmem(8, 32, 128), vmem(9, 32, 128), vmem(8, 48, 128), vmem(8, 32, 128), vmem(8, 32, 128),
        vmem(5, X1, Y1, 128), vmem(2, X1, Y1, 128), vmem(5, 32, 128), vmem(2, 5, 32, 128), vmem(5, 3, 48, 128), vmem(6, X1, 48, 128),
        vmem(X1, Y1, 128), vmem(X1, 48, 128), vmem(X1, Y1, 128), vmem(X1, Y1, 128), vmem(X1, Y1, 128),
        vmem(5, X2, Y2, 128), vmem(5, 4, 32, 128), vmem(5, 16, 128), vmem(2, 5, 16, 128), vmem(5, 4, 32, 128), vmem(6, X2, 32, 128),
        vmem(X2, Y2, 128), vmem(X2, 32, 128), vmem(X2, Y2, 128), vmem(X2, Y2, 128), vmem(X2, Y2, 128),
        vmem(4, 16, 128), vmem(4, 96, 128), vmem(2, 12, 48, 128),
        sems(8), sems(8), sems(8), sems(8), sems(2, 2), sems(2, 2), sems(2, 8), sems(2, 8),
        sems(2, 2), sems(2, 2), sems(2, 8), sems(2, 8), sems(2, 8), sems(2, 8),
        sems(2, 2), sems(2, 2), sems(2, 11), sems(2, 11), sems(2, 11), sems(2, 11),
        sems(2), sems(4),
    ]
    return pl.pallas_call(
        kernel,
        out_shape=jax.ShapeDtypeStruct(image.shape, F32),
        in_specs=[pl.BlockSpec(memory_space=pl.ANY)] * 2,
        out_specs=pl.BlockSpec(memory_space=pl.ANY),
        scratch_shapes=scratch,
        compiler_params=pltpu.CompilerParams(
            collective_id=0, has_side_effects=True, vmem_limit_bytes=56 * 1024 * 1024
        ),
    )(image, labels)


def solution(mesh):
    placed = (P("gx", "gy", "gz"), P("gx", "gy", "gz"))
    return jax.shard_map(
        shards, mesh=mesh, in_specs=placed, out_specs=P("gx", "gy", "gz"), check_vma=False
    )
```

```python
import jax
import jax.numpy as jnp
from jax import lax
from jax.experimental import pallas as pl
from jax.experimental.pallas import tpu as pltpu
from jax.sharding import PartitionSpec as P

SMOOTH_STEPS = 3
COARSE_STEPS = 6
HEAT_CONSTANT = 0.25
SCREENING = 0.002
SEED_WEIGHT = 1.0
THETA = 1.1
DELTA = 0.9

MESH = pl.DeviceIdType.MESH
F32 = jnp.float32
SIZES = {"gx": 4, "gy": 4, "gz": 8}

X0, Y0 = 32, 96
X1, Y1 = 24, 64
X2, Y2 = 24, 48

PLANAR = [(dx, dy) for dx in (1, -1, 0) for dy in (1, -1, 0) if (dx, dy) != (0, 0)]
COLUMN = [(dx, dy) for dx in (1, -1, 2, 0) for dy in (1, -1, 0) if (dx, dy) != (0, 0)]


def factors(steps):
    sigma = THETA / DELTA
    rho = 1.0 / sigma
    out = []
    for _ in range(steps - 1):
        rho_new = 1.0 / (2.0 * sigma - rho)
        out.append((rho_new * rho, 2.0 * rho_new / DELTA))
        rho = rho_new
    return out


def peer(dx, dy, dz):
    shift = {"gx": dx, "gy": dy, "gz": dz}
    return {a: lax.rem(lax.axis_index(a) + shift[a] + n, n) for a, n in SIZES.items()}


def dot(a, b):
    return jnp.dot(a, b, precision=lax.Precision.HIGHEST, preferred_element_type=F32)


def kernel(
    image_hbm, labels_hbm, out_hbm,
    image, labels, out,
    E, L, EM, R, H, UA, UB, DU, C, Q, DH, M,
    zs0, zr0, tmp, bufs, wyb, c1, wx1, wy1, wz1, D1,
    L1, LP, zs1, zr1, zc1, A1, I1, C1, ea1, eb1, d1,
    L2, LQ, zs2, zr2, zc2, A2, I2, C2, ea2, eb2, d2, D2, pro, PR,
    s_e, r_e, s_l, r_l, s_z0, r_z0, s_b0, r_b0,
    s_a1, r_a1, s_b1, r_b1, s_c1, r_c1, s_a2, r_a2, s_b2, r_b2, s_c2, r_c2,
    s_in, s_out, XU, s_u, r_u,
):
    gx, gy, gz = (lax.axis_index(a) for a in ("gx", "gy", "gz"))
    barrier = pltpu.get_barrier_semaphore()
    partners = [(dx, dy, 0) for dx, dy in COLUMN] + [(0, 0, 1), (0, 0, -1)]
    for p in partners:
        pl.semaphore_signal(barrier, inc=1, device_id=peer(*p), device_id_type=MESH)

    loads = [
        pltpu.make_async_copy(image_hbm, image, s_in.at[0]),
        pltpu.make_async_copy(labels_hbm, labels, s_in.at[1]),
    ]
    for copy in loads:
        copy.start()

    def lanes(rows):
        return lax.broadcasted_iota(jnp.int32, (rows, 128), 1)

    def rows_of(rows):
        return lax.broadcasted_iota(jnp.int32, (rows, 128), 0)

    def send(src, dst, ssem, rsem, to):
        copy = pltpu.make_async_remote_copy(
            src_ref=src, dst_ref=dst, send_sem=ssem, recv_sem=rsem, device_id=to, device_id_type=MESH
        )
        copy.start()
        return copy

    started = []

    def loop(lo, hi, body):
        def step(i, carry):
            body(i)
            return carry
        lax.fori_loop(lo, hi, step, 0)

    loads[0].wait()

    def own(x):
        E[8 + x, 16:80] = jnp.exp(image[x] * (1.0 / HEAT_CONSTANT))
    loop(0, 16, own)
    pl.semaphore_wait(barrier, len(partners))

    def x_range(dx, start, count, width):
        if dx == 0:
            return pl.ds(start, count), pl.ds(start, count)
        if dx == 1:
            return pl.ds(start + count - width, width), pl.ds(start - width, width)
        return pl.ds(start, width), pl.ds(start + count, width)

    def y_range(dy, start, count):
        if dy == 0:
            return pl.ds(start, count), pl.ds(start, count)
        if dy == 1:
            return pl.ds(start + count - 8, 8), pl.ds(start - 8, 8)
        return pl.ds(start, 8), pl.ds(start + count, 8)

    def send_own(ref, width, ssem, rsem):
        copies = []
        for i, (dx, dy) in enumerate(PLANAR):
            ys, yd = y_range(dy, 16, 64)
            xs, xd = x_range(dx, 8, 16, width)
            copies.append(send(ref.at[xs, ys], ref.at[xd, yd], ssem.at[i], rsem.at[i], peer(dx, dy, 0)))
        return copies

    own_e = send_own(E, 5, s_e, r_e)
    loads[1].wait()

    def own_labels(x):
        L[8 + x, 16:80] = labels[x].astype(F32)
    loop(0, 16, own_labels)

    group64 = lanes(64) // 8

    def pack(p, carry):
        result = []
        for k, ref in enumerate((E, L)):
            v = ref[8 + p, 16:80]
            low = pltpu.roll(v, lax.rem(8 * p, 128), 1)
            high = pltpu.roll(v, lax.rem(8 * p + 8, 128), 1)
            result.append(jnp.where(group64 == p, low, carry[2 * k]))
            result.append(jnp.where(group64 == p, high, carry[2 * k + 1]))
        return tuple(result)

    zero64 = jnp.zeros((64, 128), F32)
    packed = lax.fori_loop(0, 16, pack, (zero64,) * 4)
    for k in range(2):
        zs0[k, 1] = packed[2 * k]
        zs0[k, 0] = packed[2 * k + 1]
    za = [
        [
            send(zs0.at[k, s], zr0.at[k, 1, s, pl.ds(8, 64)], s_z0.at[k, s], r_z0.at[k, s],
                 peer(0, 0, 1 if s == 0 else -1))
            for s in range(2)
        ]
        for k in range(2)
    ]

    def forward(k):
        for copy in za[k]:
            copy.wait_recv()
        copies = []
        for i, (dx, dy) in enumerate(PLANAR):
            ys, yd = y_range(dy, 8, 64)
            copies.append(send(zr0.at[k, 1, :, ys], zr0.at[k, 1 - dx, :, yd],
                               s_b0.at[k, i], r_b0.at[k, i], peer(dx, dy, 0)))
        return copies

    for ref in (ea1, eb1, d1):
        def clear(x, ref=ref):
            ref[x] = jnp.zeros((Y1, 128), F32)
        loop(0, X1, clear)
    for ref in (ea2, eb2, d2):
        def clear(x, ref=ref):
            ref[x] = jnp.zeros((Y2, 128), F32)
        loop(0, X2, clear)

    def guard1(a):
        for x in (0, X1 - 1):
            L1[a, x] = jnp.zeros((Y1, 128), F32)

        def edge(x):
            L1[a, x, 0:8] = jnp.zeros((8, 128), F32)
            L1[a, x, 56:64] = jnp.zeros((8, 128), F32)
        loop(1, X1 - 1, edge)
    loop(0, 5, guard1)

    def guard2(a):
        for x in (0, 1, 2, 3, 20, 21, 22, 23):
            L2[a, x] = jnp.zeros((Y2, 128), F32)

        def edge(x):
            L2[a, x, 0:8] = jnp.zeros((8, 128), F32)
            L2[a, x, 40:48] = jnp.zeros((8, 128), F32)
        loop(4, 20, edge)
    loop(0, 5, guard2)

    lane80, row80 = lanes(80), rows_of(80)
    y_in = ((gy * 64 + row80 - 8) >= 0) & ((gy * 64 + row80 - 8) < 256)
    M[0] = jnp.where(y_in, 1.0, 0.0)
    z_in = ((lane80 < 8) & (gz < 7)) | ((lane80 >= 120) & (gz > 0))
    M[1] = jnp.where(y_in & z_in, 1.0, 0.0)

    zb_e = forward(0)
    own_l = send_own(L, 3, s_l, r_l)
    zb_l = forward(1)
    started += za[0] + za[1] + own_e + own_l + zb_e + zb_l
    for i, (dx, dy) in enumerate(PLANAR):
        if dx == 0:
            own_e[i].wait_recv()
            zb_e[i].wait_recv()

    def x_in(x):
        return ((gx * 16 + x - 8) >= 0) & ((gx * 16 + x - 8) < 64)

    CH, GROUP, CHC = 16, 4, 16

    def sweep(lo_x, hi_x, work, n=GROUP):
        def step(x, n):
            for lo in range(8, 88, CH):
                stores = []
                for j in range(n):
                    stores += work(x + j, lo)
                for ref, index, value in stores:
                    ref[index] = value

        def body(i, carry):
            step(lo_x + n * i, n)
            return carry
        lax.fori_loop(0, (hi_x - lo_x) // n, body, 0)
        if (hi_x - lo_x) % n:
            step(hi_x - (hi_x - lo_x) % n, (hi_x - lo_x) % n)

    lane = lanes(CH)
    at0, at127 = lane == 0, lane == 127

    def z_pair(t0, t1):
        r0, r1 = pltpu.roll(t0, 1, 1), pltpu.roll(t1, 1, 1)
        q0, q1 = pltpu.roll(t0, 127, 1), pltpu.roll(t1, 127, 1)
        return (
            jnp.where(at0, r1, r0) + jnp.where(at127, q1, q0),
            jnp.where(at0, r0, r1) + jnp.where(at127, q0, q1),
        )

    def around(ref, x, lo):
        t = [ref[k, x, lo : lo + CH] for k in range(2)]
        z = z_pair(*t)
        total = []
        for k in range(2):
            total.append(
                (ref[k, x - 1, lo : lo + CH] + ref[k, x + 1, lo : lo + CH])
                + (ref[k, x, lo - 1 : lo + CH - 1] + ref[k, x, lo + 1 : lo + CH + 1])
                + z[k]
            )
        return t, total

    def ends(k, x, r):
        p, n = lax.rem(x + 8, 16), (x + 8) // 16
        up = pltpu.roll(zr0[k, n, 1, r], lax.rem(256 - 8 * p, 128), 1)
        down = pltpu.roll(zr0[k, n, 0, r], lax.rem(248 - 8 * p, 128), 1)
        return jnp.where(lane < 8, up, down)

    def spread(x, lo):
        inside = x_in(x)
        r = pl.ds(lo - 8, CH)
        s = slice(lo, lo + CH)
        stores = []
        for t, v in ((0, E[x, s]), (1, ends(0, x, r))):
            m = jnp.where(inside, M[t, r], 0.0) > 0.5
            v = jnp.where(m, v, 1.0)
            stores += [(EM, (t, x, s), v), (R, (t, x, s), 1.0 / v)]
        return stores

    sweep(8, 24, spread)

    def heights(x, lo):
        e, es = around(EM, x, lo)
        c, cs = around(R, x, lo)
        stores = []
        for k in range(2):
            t = (e[k] + es[k]) * (c[k] + cs[k])
            stores.append((H, (k, x, slice(lo, lo + CH)), lax.rsqrt(lax.rsqrt(lax.rsqrt(t)))))
        return stores

    sweep(9, 23, heights)
    for i, (dx, dy) in enumerate(PLANAR):
        if dx != 0:
            own_e[i].wait_recv()
            zb_e[i].wait_recv()
    sweep(6, 8, spread)
    sweep(24, 26, spread)
    sweep(7, 9, heights)
    sweep(23, 25, heights)

    def cells_of(v):
        return SCREENING + SEED_WEIGHT * jnp.where(v != 2.0, 1.0, 0.0)

    def row_pairs(slot, v):
        n = v.shape[0]
        tmp[slot, 0:n] = v
        return tmp[slot, pl.ds(0, n // 2, stride=2)] + tmp[slot, pl.ds(1, n // 2, stride=2)]

    lane64 = lanes(64)

    def coarse(i):
        x = 8 + 2 * i
        bufs[0, i] = row_pairs(0, cells_of(L[x, 16:80]) + cells_of(L[x + 1, 16:80]))
        wyb[i] = (
            H[0, x, pl.ds(16, 40, stride=2)] * H[0, x, pl.ds(15, 40, stride=2)]
            + H[0, x + 1, pl.ds(16, 40, stride=2)] * H[0, x + 1, pl.ds(15, 40, stride=2)]
        )
        total = None
        for k in range(2):
            h0, h1 = H[0, x + k, 16:80], H[1, x + k, 16:80]
            r0, r1 = pltpu.roll(h0, 1, 1), pltpu.roll(h1, 1, 1)
            v = h0 * jnp.where(lane64 == 0, r1, r0)
            beyond = pltpu.roll(h1, 1, 1) * pltpu.roll(h0, 2, 1)
            v = jnp.where(lane64 == 1, beyond, v)
            total = v if total is None else total + v
        bufs[1, i] = row_pairs(1, total)
    loop(0, 8, coarse)

    def coarse_x(i):
        x = 8 + 2 * i
        wx1[i] = row_pairs(2, H[0, x, 16:80] * H[0, x - 1, 16:80])
    loop(0, 9, coarse_x)

    wr, wc = rows_of(128), lanes(128)
    restrict = jnp.where(wc == 32 + wr // 2, 1.0, 0.0)
    even = jnp.where((wc == 32 + wr // 2) & (lax.rem(wr, 2) == 0), 1.0, 0.0)
    last = jnp.where((wr == 1) & (wc == 96), 1.0, 0.0)
    c1[...] = dot(bufs[0].reshape(256, 128), restrict).reshape(8, 32, 128)
    wx1[...] = dot(wx1[...].reshape(288, 128), restrict).reshape(9, 32, 128)
    wy1[:, 0:40] = dot(wyb[...].reshape(320, 128), restrict).reshape(8, 40, 128)
    wz1[...] = dot(bufs[1].reshape(256, 128), even + last).reshape(8, 32, 128)

    lane32 = lanes(32)
    own1 = (lane32 >= 32) & (lane32 < 96)

    def level1(i):
        wz = wz1[i]
        d = (
            c1[i] + (wx1[i] + wx1[i + 1]) + (wy1[i, 0:32] + wy1[i, 1:33])
            + (wz + pltpu.roll(wz, 127, 1))
        )
        D1[i] = jnp.where(own1, d, 0.0)
        four = (jnp.where(own1, 1.0 / jnp.where(own1, d, 1.0), 0.0), wx1[i], wy1[i, 0:32], wz)
        for a in range(4):
            L1[a, 8 + i, 16:48] = four[a]
        for a in range(2):
            LP[a, 8 + i, 16:48] = jnp.where(
                lane32 < 64, pltpu.roll(four[2 * a], 96, 1), pltpu.roll(four[2 * a + 1], 32, 1)
            )
    loop(0, 8, level1)

    def send_1(src, which, width, ssem, rsem):
        copies = []
        for i, (dx, dy) in enumerate(PLANAR):
            ys, yd = y_range(dy, 16, 32)
            xs, xd = x_range(dx, 8, 8, 7)
            copies.append(send(src.at[pl.ds(which, width), xs, ys], src.at[pl.ds(which, width), xd, yd],
                               ssem.at[i], rsem.at[i], peer(dx, dy, 0)))
        return copies

    b1 = send_1(LP, 0, 2, s_b1.at[0], r_b1.at[0])

    lane16 = lanes(16)
    own2 = (lane16 >= 48) & (lane16 < 80)
    c2 = [row_pairs(0, c1[2 * i] + c1[2 * i + 1]) for i in range(4)]
    z2 = [row_pairs(1, wz1[2 * i] + wz1[2 * i + 1]) for i in range(4)]
    x2 = [row_pairs(2, wx1[2 * i]) for i in range(5)]
    y2 = [
        wy1[2 * i, pl.ds(0, 24, stride=2)] + wy1[2 * i + 1, pl.ds(0, 24, stride=2)] for i in range(4)
    ]
    c2 = dot(jnp.concatenate(c2, 0), restrict)
    x2 = dot(jnp.concatenate(x2, 0), restrict)
    y2 = dot(jnp.concatenate(y2, 0), restrict)
    z2 = dot(jnp.concatenate(z2, 0), even)
    for i in range(4):
        for k in range(3):
            tmp[k, 0:24] = y2[24 * i : 24 * i + 24]
        wz = z2[16 * i : 16 * i + 16]
        d = (
            c2[16 * i : 16 * i + 16]
            + (x2[16 * i : 16 * i + 16] + x2[16 * i + 16 : 16 * i + 32])
            + (tmp[0, 0:16] + tmp[0, 1:17]) + (wz + pltpu.roll(wz, 127, 1))
        )
        D2[i] = jnp.where(own2, d, 0.0)
        at = 4 + 4 * gx + i
        L2[0, at, 16:32] = jnp.where(own2, 1.0 / jnp.where(own2, d, 1.0), 0.0)
        L2[1, at, 16:32] = x2[16 * i : 16 * i + 16]
        L2[2, at, 16:32] = tmp[0, 0:16]
        L2[3, at, 16:32] = wz

    group32, group16 = lane32 // 8, lane16 // 8

    def pack_z(ref, a, base, planes, rows, lo, hi, group, dst):
        acc = jnp.zeros((rows, 128), F32)
        for p in range(planes):
            v = ref[a, base + p, 16 : 16 + rows]
            acc = jnp.where(group == p, pltpu.roll(v, (8 * p - lo) % 128, 1), acc)
            acc = jnp.where(group == 8 + p, pltpu.roll(v, (64 + 8 * p - hi) % 128, 1), acc)
        dst[a] = acc

    def joined(zr, zc, a, slot, rows, ln):
        zc[a, slot, 8 : 8 + rows] = jnp.where(ln < 64, zr[1, a], zr[0, a])

    def extended(base, ends, p, ln, lo, hi):
        down = pltpu.roll(ends, lax.rem(256 + lo - 8 - 64 - 8 * p, 128), 1)
        up = pltpu.roll(ends, lax.rem(256 + hi + 8 - 8 * p, 128), 1)
        v = jnp.where((ln >= lo) & (ln < hi + 8), base, 0.0)
        v = jnp.where((ln >= lo - 8) & (ln < lo), down, v)
        return jnp.where((ln >= hi + 8) & (ln < hi + 16), up, v)

    def pack1(a):
        pack_z(L1, a, 8, 8, 32, 32, 88, group32, zs1)

    def join1(a):
        joined(zr1, zc1, a, 1, 32, lane32)

    def extended1(a, x, base):
        return extended(base, zc1[a, x // 8], lax.rem(x, 8), lane48, 32, 88)

    def pack2(a):
        pack_z(L2, a, 4 + 4 * gx, 4, 16, 48, 72, group16, zs2)

    def join2(a):
        joined(zr2, zc2, a, gx, 16, lane16)

    def pack_own2(a):
        acc = jnp.zeros((16, 128), F32)
        for p in range(4):
            v = pltpu.roll(L2[a, 4 + 4 * gx + p, 16:32], (32 * p - 48) % 128, 1)
            acc = jnp.where(lane16 // 32 == p, v, acc)
        LQ[a, gx, 8:24] = acc

    def extended2(a, slot, p):
        base = pltpu.roll(LQ[a, slot], (48 - 32 * p) % 128, 1)
        return extended(base, zc2[a, slot], p, lane32, 48, 72)

    def send_z(zs, zr, which, n, ssem, rsem, slot):
        return [
            send(zs.at[pl.ds(which, n)], zr.at[s, pl.ds(which, n)], ssem.at[slot, s], rsem.at[slot, s],
                 peer(0, 0, 1 if s == 0 else -1))
            for s in range(2)
        ]

    def send_c1(which, n, slot):
        copies = []
        for i, (dx, dy) in enumerate(PLANAR):
            ys, yd = y_range(dy, 8, 32)
            copies.append(send(zc1.at[pl.ds(which, n), 1, ys], zc1.at[pl.ds(which, n), 1 - dx, yd],
                               s_c1.at[slot, i], r_c1.at[slot, i], peer(dx, dy, 0)))
        return copies

    def send_2(ref, which, n, ssem, rsem):
        copies = []
        for i, (dx, dy) in enumerate(COLUMN):
            ys, yd = y_range(dy, 8, 16)
            copies.append(send(ref.at[pl.ds(which, n), gx, ys], ref.at[pl.ds(which, n), gx, yd],
                               ssem.at[i], rsem.at[i], peer(dx, dy, 0)))
        return copies

    lane48, row48 = lanes(48), rows_of(48)
    loop(0, 4, pack1)
    a1 = send_z(zs1, zr1, 0, 4, s_a1, r_a1, 0)
    loop(0, 4, pack2)
    a2 = send_z(zs2, zr2, 0, 4, s_a2, r_a2, 0)
    loop(0, 4, pack_own2)
    sweep(3, 6, spread)
    sweep(26, 29, spread)
    sweep(4, 7, heights)
    sweep(25, 28, heights)
    for copy in a1:
        copy.wait_recv()
    loop(0, 4, join1)
    c1s = send_c1(0, 4, 0)

    def diagonal(x, lo):
        inside = x_in(x)
        h, hs = around(H, x, lo)
        r = pl.ds(lo - 8, CH)
        s = slice(lo, lo + CH)
        stores = []
        for k in range(2):
            m = jnp.where(inside, M[k, r], 0.0)
            lab = L[x, s] if k == 0 else ends(1, x, r)
            d = cells_of(lab) + h[k] * hs[k]
            hi = m * h[k] / d
            c = jnp.where(lab == 1.0, SEED_WEIGHT * hi, 0.0)
            u = c * (1.0 / THETA)
            stores += [
                (C, (k, x, s), c), (Q, (k, x, s), hi * h[k]), (UA, (k, x, s), u), (DU, (k, x, s), u)
            ]
            if k == 0:
                stores.append((DH, (x, r), d / h[k]))
        return stores

    for copy in own_l + zb_l:
        copy.wait_recv()
    sweep(5, 27, diagonal)
    started += a1 + a2 + b1 + c1s

    def smooth(src, dst, lo_x, hi_x, alpha, beta, keep=True):
        def work(x, lo):
            u, us = around(src, x, lo)
            s = slice(lo, lo + CH)
            stores = []
            for k in range(2):
                g = beta * (C[k, x, s] - u[k] + Q[k, x, s] * us[k])
                d = g if alpha is None else alpha * DU[k, x, s] + g
                if keep:
                    stores.append((DU, (k, x, s), d))
                stores.append((dst, (k, x, s), u[k] + d))
            return stores
        sweep(lo_x, hi_x, work)

    fine = factors(SMOOTH_STEPS)
    smooth(UA, UB, 6, 26, *fine[0])
    smooth(UB, UA, 7, 25, *fine[1], keep=False)

    lane_ch = lanes(CH)

    def own_sum(ref, x, lo):
        t0, t1 = ref[0, x, lo : lo + CH], ref[1, x, lo : lo + CH]
        low = jnp.where(lane_ch == 0, pltpu.roll(t1, 1, 1), pltpu.roll(t0, 1, 1))
        high = jnp.where(lane_ch == 127, pltpu.roll(t1, 127, 1), pltpu.roll(t0, 127, 1))
        return t0, (
            (ref[0, x - 1, lo : lo + CH] + ref[0, x + 1, lo : lo + CH])
            + (ref[0, x, lo - 1 : lo + CH - 1] + ref[0, x, lo + 1 : lo + CH + 1]) + (low + high)
        )

    def residual(i):
        x = 8 + 2 * i
        for lo in range(16, 80, CH):
            total = None
            for k in range(2):
                u, us = own_sum(UA, x + k, lo)
                r = DH[x + k, lo - 8 : lo - 8 + CH] * (
                    C[0, x + k, lo : lo + CH] - u + Q[0, x + k, lo : lo + CH] * us
                )
                total = r if total is None else total + r
            tmp[0, lo - 16 : lo - 16 + CH] = total
        bufs[0, i] = tmp[0, pl.ds(0, 32, stride=2)] + tmp[0, pl.ds(1, 32, stride=2)]
    loop(0, 8, residual)
    L1[4, 8:16, 16:48] = dot(bufs[0].reshape(256, 128), restrict).reshape(8, 32, 128)
    pack1(4)
    a1 = send_z(zs1, zr1, 4, 1, s_a1, r_a1, 1)
    r1 = send_1(L1, 4, 1, s_b1.at[1], r_b1.at[1])

    def prepare(ref, inv, a, x_lo, x_hi, rows, inside):
        def body(x):
            i = jnp.where(inside(x), ref[0, x, 8 : 8 + rows], 0.0)
            inv[x, 8 : 8 + rows] = i
            a[0, x] = i * ref[1, x, 8 : 8 + rows]
            a[1, x] = i * ref[1, x + 1, 8 : 8 + rows]
            a[2, x] = i * ref[2, x, 8 : 8 + rows]
            a[3, x] = i * ref[2, x, 9 : 9 + rows]
            a[4, x] = i * ref[3, x, 8 : 8 + rows]
            a[5, x] = i * pltpu.roll(ref[3, x, 8 : 8 + rows], 127, 1)
        loop(x_lo, x_hi, body)

    def apply(c, a, e, x, lo, n):
        r, s = slice(lo - 8, lo - 8 + n), slice(lo, lo + n)
        v = e[x, s]
        return v, (
            (c[x, r] - v)
            + (a[0, x, r] * e[x - 1, s] + a[1, x, r] * e[x + 1, s])
            + (a[2, x, r] * e[x, lo - 1 : lo - 1 + n] + a[3, x, r] * e[x, lo + 1 : lo + 1 + n])
            + (a[4, x, r] * pltpu.roll(v, 1, 1) + a[5, x, r] * pltpu.roll(v, 127, 1))
        )

    def begin(c, e, d, x_lo, x_hi, rows):
        def body(x):
            u = c[x] * (1.0 / THETA)
            e[x, 8 : 8 + rows] = u
            d[x, 0:rows] = u
        loop(x_lo, x_hi, body)

    def relax(c, a, e, new, d, x_lo, x_hi, rows, alpha, beta):
        n = 2 if rows == 48 else 4

        def step(x, n):
            for lo in range(8, 8 + rows, CHC):
                values = []
                for j in range(n):
                    v, g = apply(c, a, e, x + j, lo, CHC)
                    r = slice(lo - 8, lo - 8 + CHC)
                    move = beta * g if alpha is None else alpha * d[x + j, r] + beta * g
                    values += [(d, (x + j, r), move), (new, (x + j, slice(lo, lo + CHC)), v + move)]
                for ref, index, value in values:
                    ref[index] = value

        def body(i, carry):
            step(x_lo + n * i, n)
            return carry
        lax.fori_loop(0, (x_hi - x_lo) // n, body, 0)
        if (x_hi - x_lo) % n:
            step(x_hi - (x_hi - x_lo) % n, (x_hi - x_lo) % n)

    yz1 = (
        (gy * 32 + row48 - 8 >= 0) & (gy * 32 + row48 - 8 < 128)
        & (gz * 64 + lane48 - 32 >= 0) & (gz * 64 + lane48 - 32 < 512)
    )

    def inside1(x):
        ok = ((gx * 8 + x - 8) >= 0) & ((gx * 8 + x - 8) < 32)
        return jnp.where(ok, jnp.where(yz1, 1.0, 0.0), 0.0) > 0.5

    row32 = rows_of(32)
    yz2 = (
        (gy * 16 + row32 - 8 >= 0) & (gy * 16 + row32 - 8 < 64)
        & (gz * 32 + lane32 - 48 >= 0) & (gz * 32 + lane32 - 48 < 256)
    )

    def assemble1(x):
        for a in range(4):
            base = pltpu.roll(LP[a // 2, x, 8:56], 32 if a % 2 == 0 else 96, 1)
            L1[a, x, 8:56] = extended1(a, x, base)
    for copy in b1 + c1s:
        copy.wait_recv()
    loop(1, X1 - 1, assemble1)
    for copy in a1:
        copy.wait_recv()
    join1(4)
    c1r = send_c1(4, 1, 1)
    for copy in a2:
        copy.wait_recv()
    loop(0, 4, join2)
    b2 = send_2(LQ, 0, 4, s_b2.at[0], r_b2.at[0])
    c2 = send_2(zc2, 0, 4, s_c2.at[0], r_c2.at[0])
    fu = [
        send(UA.at[:, pl.ds(21, 3), pl.ds(8, 80)], XU.at[0], s_u.at[0], r_u.at[0], peer(1, 0, 0)),
        send(UA.at[:, pl.ds(8, 3), pl.ds(8, 80)], XU.at[1], s_u.at[1], r_u.at[1], peer(-1, 0, 0)),
    ]
    started += a1 + r1 + c1r + b2 + c2
    prepare(L1, I1, A1, 1, X1 - 1, 48, inside1)
    for copy in r1 + c1r:
        copy.wait_recv()

    def scale1(x):
        C1[x] = I1[x, 8:56] * extended1(4, x, L1[4, x, 8:56])
    loop(1, X1 - 1, scale1)
    begin(C1, ea1, d1, 1, X1 - 1, 48)
    relax(C1, A1, ea1, eb1, d1, 2, X1 - 2, 48, *fine[0])
    relax(C1, A1, eb1, ea1, d1, 3, X1 - 3, 48, *fine[1])

    def residual1(i):
        total = None
        for k in range(2):
            x = 8 + 2 * i + k
            _, g = apply(C1, A1, ea1, x, 16, 32)
            r = D1[2 * i + k] * g
            total = r if total is None else total + r
        bufs[1, i, 0:16] = row_pairs(1, total)
    loop(0, 4, residual1)
    r2 = dot(jnp.concatenate([bufs[1, i, 0:16] for i in range(4)], 0), restrict)
    for i in range(4):
        L2[4, 4 + 4 * gx + i, 16:32] = r2[16 * i : 16 * i + 16]
    pack2(4)
    a2 = send_z(zs2, zr2, 4, 1, s_a2, r_a2, 1)
    pack_own2(4)
    r2 = send_2(LQ, 4, 1, s_b2.at[1], r_b2.at[1])
    for copy in b2 + c2:
        copy.wait_recv()

    def assemble2(slot):
        for a in range(4):
            for p in range(4):
                L2[a, 4 + 4 * slot + p, 8:40] = extended2(a, slot, p)
    loop(0, 4, assemble2)
    for copy in a2:
        copy.wait_recv()
    join2(4)
    c2r = send_2(zc2, 4, 1, s_c2.at[1], r_c2.at[1])
    prepare(L2, I2, A2, 4, 20, 32, lambda x: yz2)
    started += a2 + r2 + c2r
    for copy in r2 + c2r:
        copy.wait_recv()

    def scale2(slot):
        for p in range(4):
            x = 4 + 4 * slot + p
            C2[x] = I2[x, 8:40] * extended2(4, slot, p)
    loop(0, 4, scale2)
    begin(C2, ea2, d2, 4, 20, 32)
    pair = (ea2, eb2)
    for n, f in enumerate(factors(COARSE_STEPS)):
        relax(C2, A2, pair[n % 2], pair[1 - n % 2], d2, 4, 20, 32, *f)
    e2 = pair[(COARSE_STEPS - 1) % 2]

    widen = jnp.where(wr == 32 + wc // 2, 1.0, 0.0)

    PR[0, 0:10, 0:32] = dot(
        e2[pl.ds(4 * gx + 1, 10), 8:40].reshape(320, 128), widen
    ).reshape(10, 32, 128)

    def up1(i):
        for j in range(2):
            v = PR[0, 2 * i + j, 0:32]
            pro[j, pl.ds(0, 32, stride=2)] = v
            pro[j, pl.ds(1, 32, stride=2)] = v
        values = []
        for j in range(2):
            for k in range(2):
                x = 2 + 4 * i + 2 * j + k
                values.append((x, ea1[x, 8:56] + pro[j, 8:56]))
        for x, value in values:
            ea1[x, 8:56] = value
    loop(0, 5, up1)
    relax(C1, A1, ea1, eb1, d1, 3, X1 - 3, 48, None, 1.0 / THETA)
    relax(C1, A1, eb1, ea1, d1, 4, X1 - 4, 48, *fine[0])
    relax(C1, A1, ea1, eb1, d1, 5, X1 - 5, 48, *fine[1])

    beyond = jnp.where(
        ((wc < 8) & (wr == 96 + wc // 2)) | ((wc >= 120) & (wr == 28 + (wc - 120) // 2)), 1.0, 0.0
    )

    for copy in fu:
        copy.wait_recv()
        copy.wait_send()

    def beside(i):
        for side, x in ((0, 5 + i), (1, 24 + i)):
            scale = jnp.where(x_in(x), 1.0, 0.0)
            for k in range(2):
                UA[k, x, 8:88] = XU[side, k, i] * scale
    loop(0, 3, beside)

    both = jnp.concatenate([widen, beyond], 1)
    wide = dot(eb1[6:18, 8:56].reshape(576, 128), both)
    for k in range(2):
        PR[k] = wide[:, 128 * k : 128 * k + 128].reshape(12, 48, 128)

    def up0(i):
        for j in range(2):
            for k in range(2):
                v = PR[k, 2 * i + j]
                pro[2 * j + k, pl.ds(0, 48, stride=2)] = v
                pro[2 * j + k, pl.ds(1, 48, stride=2)] = v
        for lo in range(8, 88, CH):
            s = slice(lo, lo + CH)
            values = []
            for j in range(2):
                for n in range(2):
                    x = 4 + 4 * i + 2 * j + n
                    for k in range(2):
                        values.append(((k, x, s), UA[k, x, s] + H[k, x, s] * pro[2 * j + k, s]))
            for index, value in values:
                UA[index] = value
    loop(0, 6, up0)
    smooth(UA, UB, 6, 26, None, 1.0 / THETA)
    smooth(UB, UA, 7, 25, *fine[0])

    alpha, beta = fine[1]

    def finish(i):
        for lo in range(16, 80, CH):
            values = []
            for k in range(2):
                x = 8 + 2 * i + k
                s = slice(lo, lo + CH)
                u, us = own_sum(UA, x, lo)
                d = alpha * DU[0, x, s] + beta * (C[0, x, s] - u + Q[0, x, s] * us)
                values.append((u + d) / H[0, x, s])
            for k in range(2):
                out[2 * i + k, lo - 16 : lo - 16 + CH] = values[k]
    stores = []
    for part in range(4):
        loop(2 * part, 2 * part + 2, finish)
        planes = pl.ds(4 * part, 4)
        stores.append(pltpu.make_async_copy(out.at[planes], out_hbm.at[planes], s_out.at[part]))
        stores[-1].start()
    for copy in stores:
        copy.wait()

    for copy in started:
        copy.wait_send()


def shards(image, labels):
    def level0():
        return pltpu.VMEM((2, X0, Y0, 128), F32)

    def vmem(*shape):
        return pltpu.VMEM(shape, F32)

    def sems(*shape):
        return pltpu.SemaphoreType.DMA(shape)

    scratch = [vmem(16, 64, 128), pltpu.VMEM((16, 64, 128), jnp.int32), vmem(16, 64, 128)]
    scratch += [vmem(X0, Y0, 128), vmem(X0, Y0, 128)] + [level0() for _ in range(8)] + [
        vmem(X0, 80, 128), vmem(2, 80, 128),
        vmem(2, 2, 64, 128), vmem(2, 3, 2, 80, 128), vmem(3, 64, 128), vmem(2, 8, 32, 128), vmem(8, 40, 128),
        vmem(8, 32, 128), vmem(9, 32, 128), vmem(8, 48, 128), vmem(8, 32, 128), vmem(8, 32, 128),
        vmem(5, X1, Y1, 128), vmem(2, X1, Y1, 128), vmem(5, 32, 128), vmem(2, 5, 32, 128), vmem(5, 3, 48, 128), vmem(6, X1, 48, 128),
        vmem(X1, Y1, 128), vmem(X1, 48, 128), vmem(X1, Y1, 128), vmem(X1, Y1, 128), vmem(X1, Y1, 128),
        vmem(5, X2, Y2, 128), vmem(5, 4, 32, 128), vmem(5, 16, 128), vmem(2, 5, 16, 128), vmem(5, 4, 32, 128), vmem(6, X2, 32, 128),
        vmem(X2, Y2, 128), vmem(X2, 32, 128), vmem(X2, Y2, 128), vmem(X2, Y2, 128), vmem(X2, Y2, 128),
        vmem(4, 16, 128), vmem(4, 96, 128), vmem(2, 12, 48, 128),
        sems(8), sems(8), sems(8), sems(8), sems(2, 2), sems(2, 2), sems(2, 8), sems(2, 8),
        sems(2, 2), sems(2, 2), sems(2, 8), sems(2, 8), sems(2, 8), sems(2, 8),
        sems(2, 2), sems(2, 2), sems(2, 11), sems(2, 11), sems(2, 11), sems(2, 11),
        sems(2), sems(4), vmem(2, 2, 3, 80, 128), sems(2), sems(2),
    ]
    return pl.pallas_call(
        kernel,
        out_shape=jax.ShapeDtypeStruct(image.shape, F32),
        in_specs=[pl.BlockSpec(memory_space=pl.ANY)] * 2,
        out_specs=pl.BlockSpec(memory_space=pl.ANY),
        scratch_shapes=scratch,
        compiler_params=pltpu.CompilerParams(
            collective_id=0, has_side_effects=True, vmem_limit_bytes=56 * 1024 * 1024
        ),
    )(image, labels)


def solution(mesh):
    placed = (P("gx", "gy", "gz"), P("gx", "gy", "gz"))
    return jax.shard_map(
        shards, mesh=mesh, in_specs=placed, out_specs=P("gx", "gy", "gz"), check_vma=False
    )
```

```python
import jax
import jax.numpy as jnp
from jax import lax
from jax.experimental import pallas as pl
from jax.experimental.pallas import tpu as pltpu
from jax.sharding import PartitionSpec as P

SMOOTH_STEPS = 3
COARSE_STEPS = 6
HEAT_CONSTANT = 0.25
SCREENING = 0.002
SEED_WEIGHT = 1.0
THETA = 1.1
DELTA = 0.9

MESH = pl.DeviceIdType.MESH
F32 = jnp.float32
SIZES = {"gx": 4, "gy": 4, "gz": 8}

X0, Y0 = 32, 96
X1, Y1 = 24, 64
X2, Y2 = 24, 48

PLANAR = [(dx, dy) for dx in (1, -1, 0) for dy in (1, -1, 0) if (dx, dy) != (0, 0)]
COLUMN = [(dx, dy) for dx in (1, -1, 2, 0) for dy in (1, -1, 0) if (dx, dy) != (0, 0)]


def factors(steps):
    sigma = THETA / DELTA
    rho = 1.0 / sigma
    out = []
    for _ in range(steps - 1):
        rho_new = 1.0 / (2.0 * sigma - rho)
        out.append((rho_new * rho, 2.0 * rho_new / DELTA))
        rho = rho_new
    return out


def peer(dx, dy, dz):
    shift = {"gx": dx, "gy": dy, "gz": dz}
    return {a: lax.rem(lax.axis_index(a) + shift[a] + n, n) for a, n in SIZES.items()}


def dot(a, b):
    return jnp.dot(a, b, precision=lax.Precision.HIGHEST, preferred_element_type=F32)


def kernel(
    image_hbm, labels_hbm, out_hbm,
    image, labels, out,
    E, L, EM, R, H, UA, UB, DU, C, Q, DH, M,
    zs0, zr0, tmp, bufs, wyb, c1, wx1, wy1, wz1, D1,
    L1, LP, zs1, zr1, zc1, A1, I1, C1, ea1, eb1, d1,
    L2, LQ, zs2, zr2, zc2, A2, I2, C2, ea2, eb2, d2, D2, pro, PR,
    s_e, r_e, s_l, r_l, s_z0, r_z0, s_b0, r_b0,
    s_a1, r_a1, s_b1, r_b1, s_c1, r_c1, s_a2, r_a2, s_b2, r_b2, s_c2, r_c2,
    s_in, s_out, XU, s_u, r_u,
):
    gx, gy, gz = (lax.axis_index(a) for a in ("gx", "gy", "gz"))
    barrier = pltpu.get_barrier_semaphore()
    partners = [(dx, dy, 0) for dx, dy in COLUMN] + [(0, 0, 1), (0, 0, -1)]
    for p in partners:
        pl.semaphore_signal(barrier, inc=1, device_id=peer(*p), device_id_type=MESH)

    loads = [
        pltpu.make_async_copy(image_hbm, image, s_in.at[0]),
        pltpu.make_async_copy(labels_hbm, labels, s_in.at[1]),
    ]
    for copy in loads:
        copy.start()

    def lanes(rows):
        return lax.broadcasted_iota(jnp.int32, (rows, 128), 1)

    def rows_of(rows):
        return lax.broadcasted_iota(jnp.int32, (rows, 128), 0)

    def send(src, dst, ssem, rsem, to):
        copy = pltpu.make_async_remote_copy(
            src_ref=src, dst_ref=dst, send_sem=ssem, recv_sem=rsem, device_id=to, device_id_type=MESH
        )
        copy.start()
        return copy

    started = []

    def loop(lo, hi, body, unroll=1):
        def step(i, carry):
            body(i)
            return carry
        lax.fori_loop(lo, hi, step, 0, unroll=unroll)

    loads[0].wait()

    def own(x):
        E[8 + x, 16:80] = jnp.exp(image[x] * (1.0 / HEAT_CONSTANT))
    loop(0, 16, own)
    pl.semaphore_wait(barrier, len(partners))

    def x_range(dx, start, count, width):
        if dx == 0:
            return pl.ds(start, count), pl.ds(start, count)
        if dx == 1:
            return pl.ds(start + count - width, width), pl.ds(start - width, width)
        return pl.ds(start, width), pl.ds(start + count, width)

    def y_range(dy, start, count):
        if dy == 0:
            return pl.ds(start, count), pl.ds(start, count)
        if dy == 1:
            return pl.ds(start + count - 8, 8), pl.ds(start - 8, 8)
        return pl.ds(start, 8), pl.ds(start + count, 8)

    def send_own(ref, width, ssem, rsem):
        copies = []
        for i, (dx, dy) in enumerate(PLANAR):
            ys, yd = y_range(dy, 16, 64)
            xs, xd = x_range(dx, 8, 16, width)
            copies.append(send(ref.at[xs, ys], ref.at[xd, yd], ssem.at[i], rsem.at[i], peer(dx, dy, 0)))
        return copies

    own_e = send_own(E, 5, s_e, r_e)
    loads[1].wait()

    def own_labels(x):
        L[8 + x, 16:80] = labels[x].astype(F32)
    loop(0, 16, own_labels)

    group64 = lanes(64) // 8

    def pack(p, carry):
        result = []
        for k, ref in enumerate((E, L)):
            v = ref[8 + p, 16:80]
            low = pltpu.roll(v, lax.rem(8 * p, 128), 1)
            high = pltpu.roll(v, lax.rem(8 * p + 8, 128), 1)
            result.append(jnp.where(group64 == p, low, carry[2 * k]))
            result.append(jnp.where(group64 == p, high, carry[2 * k + 1]))
        return tuple(result)

    zero64 = jnp.zeros((64, 128), F32)
    packed = lax.fori_loop(0, 16, pack, (zero64,) * 4)
    for k in range(2):
        zs0[k, 1] = packed[2 * k]
        zs0[k, 0] = packed[2 * k + 1]
    za = [
        [
            send(zs0.at[k, s], zr0.at[k, 1, s, pl.ds(8, 64)], s_z0.at[k, s], r_z0.at[k, s],
                 peer(0, 0, 1 if s == 0 else -1))
            for s in range(2)
        ]
        for k in range(2)
    ]

    def forward(k):
        for copy in za[k]:
            copy.wait_recv()
        copies = []
        for i, (dx, dy) in enumerate(PLANAR):
            ys, yd = y_range(dy, 8, 64)
            copies.append(send(zr0.at[k, 1, :, ys], zr0.at[k, 1 - dx, :, yd],
                               s_b0.at[k, i], r_b0.at[k, i], peer(dx, dy, 0)))
        return copies

    for ref in (ea1, eb1, d1):
        def clear(x, ref=ref):
            ref[x] = jnp.zeros((Y1, 128), F32)
        loop(0, X1, clear)
    for ref in (ea2, eb2, d2):
        def clear(x, ref=ref):
            ref[x] = jnp.zeros((Y2, 128), F32)
        loop(0, X2, clear)

    def guard1(a):
        for x in (0, X1 - 1):
            L1[a, x] = jnp.zeros((Y1, 128), F32)

        def edge(x):
            L1[a, x, 0:8] = jnp.zeros((8, 128), F32)
            L1[a, x, 56:64] = jnp.zeros((8, 128), F32)
        loop(1, X1 - 1, edge)
    loop(0, 5, guard1)

    def guard2(a):
        for x in (0, 1, 2, 3, 20, 21, 22, 23):
            L2[a, x] = jnp.zeros((Y2, 128), F32)

        def edge(x):
            L2[a, x, 0:8] = jnp.zeros((8, 128), F32)
            L2[a, x, 40:48] = jnp.zeros((8, 128), F32)
        loop(4, 20, edge)
    loop(0, 5, guard2)

    lane80, row80 = lanes(80), rows_of(80)
    y_in = ((gy * 64 + row80 - 8) >= 0) & ((gy * 64 + row80 - 8) < 256)
    M[0] = jnp.where(y_in, 1.0, 0.0)
    z_in = ((lane80 < 8) & (gz < 7)) | ((lane80 >= 120) & (gz > 0))
    M[1] = jnp.where(y_in & z_in, 1.0, 0.0)

    zb_e = forward(0)
    own_l = send_own(L, 3, s_l, r_l)
    zb_l = forward(1)
    started += za[0] + za[1] + own_e + own_l + zb_e + zb_l
    for i, (dx, dy) in enumerate(PLANAR):
        if dx == 0:
            own_e[i].wait_recv()
            zb_e[i].wait_recv()

    def x_in(x):
        return ((gx * 16 + x - 8) >= 0) & ((gx * 16 + x - 8) < 64)

    CH, GROUP, CHC = 16, 4, 16

    def sweep(lo_x, hi_x, work, n=GROUP):
        def step(x, n):
            for lo in range(8, 88, CH):
                stores = []
                for j in range(n):
                    stores += work(x + j, lo)
                for ref, index, value in stores:
                    ref[index] = value

        def body(i, carry):
            step(lo_x + n * i, n)
            return carry
        lax.fori_loop(0, (hi_x - lo_x) // n, body, 0)
        if (hi_x - lo_x) % n:
            step(hi_x - (hi_x - lo_x) % n, (hi_x - lo_x) % n)

    lane = lanes(CH)
    at0, at127 = lane == 0, lane == 127

    def z_pair(t0, t1):
        r0, r1 = pltpu.roll(t0, 1, 1), pltpu.roll(t1, 1, 1)
        q0, q1 = pltpu.roll(t0, 127, 1), pltpu.roll(t1, 127, 1)
        return (
            jnp.where(at0, r1, r0) + jnp.where(at127, q1, q0),
            jnp.where(at0, r0, r1) + jnp.where(at127, q0, q1),
        )

    def around(ref, x, lo):
        t = [ref[k, x, lo : lo + CH] for k in range(2)]
        z = z_pair(*t)
        total = []
        for k in range(2):
            total.append(
                (ref[k, x - 1, lo : lo + CH] + ref[k, x + 1, lo : lo + CH])
                + (ref[k, x, lo - 1 : lo + CH - 1] + ref[k, x, lo + 1 : lo + CH + 1])
                + z[k]
            )
        return t, total

    def ends(k, x, r):
        p, n = lax.rem(x + 8, 16), (x + 8) // 16
        up = pltpu.roll(zr0[k, n, 1, r], lax.rem(256 - 8 * p, 128), 1)
        down = pltpu.roll(zr0[k, n, 0, r], lax.rem(248 - 8 * p, 128), 1)
        return jnp.where(lane < 8, up, down)

    def spread(x, lo):
        inside = x_in(x)
        r = pl.ds(lo - 8, CH)
        s = slice(lo, lo + CH)
        stores = []
        for t, v in ((0, E[x, s]), (1, ends(0, x, r))):
            m = jnp.where(inside, M[t, r], 0.0) > 0.5
            v = jnp.where(m, v, 1.0)
            stores += [(EM, (t, x, s), v), (R, (t, x, s), 1.0 / v)]
        return stores

    sweep(8, 24, spread)

    def heights(x, lo):
        e, es = around(EM, x, lo)
        c, cs = around(R, x, lo)
        stores = []
        for k in range(2):
            t = (e[k] + es[k]) * (c[k] + cs[k])
            stores.append((H, (k, x, slice(lo, lo + CH)), lax.rsqrt(lax.rsqrt(lax.rsqrt(t)))))
        return stores

    sweep(9, 23, heights)
    for i, (dx, dy) in enumerate(PLANAR):
        if dx != 0:
            own_e[i].wait_recv()
            zb_e[i].wait_recv()
    sweep(6, 8, spread)
    sweep(24, 26, spread)
    sweep(7, 9, heights)
    sweep(23, 25, heights)

    def cells_of(v):
        return SCREENING + SEED_WEIGHT * jnp.where(v != 2.0, 1.0, 0.0)

    def row_pairs(slot, v):
        n = v.shape[0]
        tmp[slot, 0:n] = v
        return tmp[slot, pl.ds(0, n // 2, stride=2)] + tmp[slot, pl.ds(1, n // 2, stride=2)]

    lane64 = lanes(64)

    def coarse(i):
        x = 8 + 2 * i
        bufs[0, i] = row_pairs(0, cells_of(L[x, 16:80]) + cells_of(L[x + 1, 16:80]))
        wyb[i] = (
            H[0, x, pl.ds(16, 40, stride=2)] * H[0, x, pl.ds(15, 40, stride=2)]
            + H[0, x + 1, pl.ds(16, 40, stride=2)] * H[0, x + 1, pl.ds(15, 40, stride=2)]
        )
        total = None
        for k in range(2):
            h0, h1 = H[0, x + k, 16:80], H[1, x + k, 16:80]
            r0, r1 = pltpu.roll(h0, 1, 1), pltpu.roll(h1, 1, 1)
            v = h0 * jnp.where(lane64 == 0, r1, r0)
            beyond = pltpu.roll(h1, 1, 1) * pltpu.roll(h0, 2, 1)
            v = jnp.where(lane64 == 1, beyond, v)
            total = v if total is None else total + v
        bufs[1, i] = row_pairs(1, total)
    loop(0, 8, coarse, 2)

    def coarse_x(i):
        x = 8 + 2 * i
        wx1[i] = row_pairs(2, H[0, x, 16:80] * H[0, x - 1, 16:80])
    loop(0, 9, coarse_x, 3)

    wr, wc = rows_of(128), lanes(128)
    restrict = jnp.where(wc == 32 + wr // 2, 1.0, 0.0)
    even = jnp.where((wc == 32 + wr // 2) & (lax.rem(wr, 2) == 0), 1.0, 0.0)
    last = jnp.where((wr == 1) & (wc == 96), 1.0, 0.0)
    c1[...] = dot(bufs[0].reshape(256, 128), restrict).reshape(8, 32, 128)
    wx1[...] = dot(wx1[...].reshape(288, 128), restrict).reshape(9, 32, 128)
    wy1[:, 0:40] = dot(wyb[...].reshape(320, 128), restrict).reshape(8, 40, 128)
    wz1[...] = dot(bufs[1].reshape(256, 128), even + last).reshape(8, 32, 128)

    lane32 = lanes(32)
    own1 = (lane32 >= 32) & (lane32 < 96)

    def level1(i):
        wz = wz1[i]
        d = (
            c1[i] + (wx1[i] + wx1[i + 1]) + (wy1[i, 0:32] + wy1[i, 1:33])
            + (wz + pltpu.roll(wz, 127, 1))
        )
        D1[i] = jnp.where(own1, d, 0.0)
        four = (jnp.where(own1, 1.0 / jnp.where(own1, d, 1.0), 0.0), wx1[i], wy1[i, 0:32], wz)
        for a in range(4):
            L1[a, 8 + i, 16:48] = four[a]
        for a in range(2):
            LP[a, 8 + i, 16:48] = jnp.where(
                lane32 < 64, pltpu.roll(four[2 * a], 96, 1), pltpu.roll(four[2 * a + 1], 32, 1)
            )
    loop(0, 8, level1)

    def send_1(src, which, width, ssem, rsem):
        copies = []
        for i, (dx, dy) in enumerate(PLANAR):
            ys, yd = y_range(dy, 16, 32)
            xs, xd = x_range(dx, 8, 8, 7)
            copies.append(send(src.at[pl.ds(which, width), xs, ys], src.at[pl.ds(which, width), xd, yd],
                               ssem.at[i], rsem.at[i], peer(dx, dy, 0)))
        return copies

    b1 = send_1(LP, 0, 2, s_b1.at[0], r_b1.at[0])

    lane16 = lanes(16)
    own2 = (lane16 >= 48) & (lane16 < 80)
    c2 = [row_pairs(0, c1[2 * i] + c1[2 * i + 1]) for i in range(4)]
    z2 = [row_pairs(1, wz1[2 * i] + wz1[2 * i + 1]) for i in range(4)]
    x2 = [row_pairs(2, wx1[2 * i]) for i in range(5)]
    y2 = [
        wy1[2 * i, pl.ds(0, 24, stride=2)] + wy1[2 * i + 1, pl.ds(0, 24, stride=2)] for i in range(4)
    ]
    c2 = dot(jnp.concatenate(c2, 0), restrict)
    x2 = dot(jnp.concatenate(x2, 0), restrict)
    y2 = dot(jnp.concatenate(y2, 0), restrict)
    z2 = dot(jnp.concatenate(z2, 0), even)
    for i in range(4):
        for k in range(3):
            tmp[k, 0:24] = y2[24 * i : 24 * i + 24]
        wz = z2[16 * i : 16 * i + 16]
        d = (
            c2[16 * i : 16 * i + 16]
            + (x2[16 * i : 16 * i + 16] + x2[16 * i + 16 : 16 * i + 32])
            + (tmp[0, 0:16] + tmp[0, 1:17]) + (wz + pltpu.roll(wz, 127, 1))
        )
        D2[i] = jnp.where(own2, d, 0.0)
        at = 4 + 4 * gx + i
        L2[0, at, 16:32] = jnp.where(own2, 1.0 / jnp.where(own2, d, 1.0), 0.0)
        L2[1, at, 16:32] = x2[16 * i : 16 * i + 16]
        L2[2, at, 16:32] = tmp[0, 0:16]
        L2[3, at, 16:32] = wz

    group32, group16 = lane32 // 8, lane16 // 8

    def pack_z(ref, a, base, planes, rows, lo, hi, group, dst):
        acc = jnp.zeros((rows, 128), F32)
        for p in range(planes):
            v = ref[a, base + p, 16 : 16 + rows]
            acc = jnp.where(group == p, pltpu.roll(v, (8 * p - lo) % 128, 1), acc)
            acc = jnp.where(group == 8 + p, pltpu.roll(v, (64 + 8 * p - hi) % 128, 1), acc)
        dst[a] = acc

    def joined(zr, zc, a, slot, rows, ln):
        zc[a, slot, 8 : 8 + rows] = jnp.where(ln < 64, zr[1, a], zr[0, a])

    def extended(base, ends, p, ln, lo, hi):
        down = pltpu.roll(ends, lax.rem(256 + lo - 8 - 64 - 8 * p, 128), 1)
        up = pltpu.roll(ends, lax.rem(256 + hi + 8 - 8 * p, 128), 1)
        v = jnp.where((ln >= lo) & (ln < hi + 8), base, 0.0)
        v = jnp.where((ln >= lo - 8) & (ln < lo), down, v)
        return jnp.where((ln >= hi + 8) & (ln < hi + 16), up, v)

    def pack1(a):
        pack_z(L1, a, 8, 8, 32, 32, 88, group32, zs1)

    def join1(a):
        joined(zr1, zc1, a, 1, 32, lane32)

    def extended1(a, x, base):
        return extended(base, zc1[a, x // 8], lax.rem(x, 8), lane48, 32, 88)

    def pack2(a):
        pack_z(L2, a, 4 + 4 * gx, 4, 16, 48, 72, group16, zs2)

    def join2(a):
        joined(zr2, zc2, a, gx, 16, lane16)

    def pack_own2(a):
        acc = jnp.zeros((16, 128), F32)
        for p in range(4):
            v = pltpu.roll(L2[a, 4 + 4 * gx + p, 16:32], (32 * p - 48) % 128, 1)
            acc = jnp.where(lane16 // 32 == p, v, acc)
        LQ[a, gx, 8:24] = acc

    def extended2(a, slot, p):
        base = pltpu.roll(LQ[a, slot], (48 - 32 * p) % 128, 1)
        return extended(base, zc2[a, slot], p, lane32, 48, 72)

    def send_z(zs, zr, which, n, ssem, rsem, slot):
        return [
            send(zs.at[pl.ds(which, n)], zr.at[s, pl.ds(which, n)], ssem.at[slot, s], rsem.at[slot, s],
                 peer(0, 0, 1 if s == 0 else -1))
            for s in range(2)
        ]

    def send_c1(which, n, slot):
        copies = []
        for i, (dx, dy) in enumerate(PLANAR):
            ys, yd = y_range(dy, 8, 32)
            copies.append(send(zc1.at[pl.ds(which, n), 1, ys], zc1.at[pl.ds(which, n), 1 - dx, yd],
                               s_c1.at[slot, i], r_c1.at[slot, i], peer(dx, dy, 0)))
        return copies

    def send_2(ref, which, n, ssem, rsem):
        copies = []
        for i, (dx, dy) in enumerate(COLUMN):
            ys, yd = y_range(dy, 8, 16)
            copies.append(send(ref.at[pl.ds(which, n), gx, ys], ref.at[pl.ds(which, n), gx, yd],
                               ssem.at[i], rsem.at[i], peer(dx, dy, 0)))
        return copies

    lane48, row48 = lanes(48), rows_of(48)
    loop(0, 4, pack1, 2)
    a1 = send_z(zs1, zr1, 0, 4, s_a1, r_a1, 0)
    loop(0, 4, pack2)
    a2 = send_z(zs2, zr2, 0, 4, s_a2, r_a2, 0)
    loop(0, 4, pack_own2)
    sweep(3, 6, spread)
    sweep(26, 29, spread)
    sweep(4, 7, heights)
    sweep(25, 28, heights)
    for copy in a1:
        copy.wait_recv()
    loop(0, 4, join1)
    c1s = send_c1(0, 4, 0)

    def diagonal(x, lo):
        inside = x_in(x)
        h, hs = around(H, x, lo)
        r = pl.ds(lo - 8, CH)
        s = slice(lo, lo + CH)
        stores = []
        for k in range(2):
            m = jnp.where(inside, M[k, r], 0.0)
            lab = L[x, s] if k == 0 else ends(1, x, r)
            d = cells_of(lab) + h[k] * hs[k]
            hi = m * h[k] / d
            c = jnp.where(lab == 1.0, SEED_WEIGHT * hi, 0.0)
            u = c * (1.0 / THETA)
            stores += [
                (C, (k, x, s), c), (Q, (k, x, s), hi * h[k]), (UA, (k, x, s), u), (DU, (k, x, s), u)
            ]
            if k == 0:
                stores.append((DH, (x, r), d / h[k]))
        return stores

    for copy in own_l + zb_l:
        copy.wait_recv()
    sweep(5, 27, diagonal)
    started += a1 + a2 + b1 + c1s

    def smooth(src, dst, lo_x, hi_x, alpha, beta, keep=True):
        def work(x, lo):
            u, us = around(src, x, lo)
            s = slice(lo, lo + CH)
            stores = []
            for k in range(2):
                g = beta * (C[k, x, s] - u[k] + Q[k, x, s] * us[k])
                d = g if alpha is None else alpha * DU[k, x, s] + g
                if keep:
                    stores.append((DU, (k, x, s), d))
                stores.append((dst, (k, x, s), u[k] + d))
            return stores
        sweep(lo_x, hi_x, work)

    fine = factors(SMOOTH_STEPS)
    smooth(UA, UB, 6, 26, *fine[0])
    smooth(UB, UA, 7, 25, *fine[1], keep=False)

    lane_ch = lanes(CH)

    def own_sum(ref, x, lo):
        t0, t1 = ref[0, x, lo : lo + CH], ref[1, x, lo : lo + CH]
        low = jnp.where(lane_ch == 0, pltpu.roll(t1, 1, 1), pltpu.roll(t0, 1, 1))
        high = jnp.where(lane_ch == 127, pltpu.roll(t1, 127, 1), pltpu.roll(t0, 127, 1))
        return t0, (
            (ref[0, x - 1, lo : lo + CH] + ref[0, x + 1, lo : lo + CH])
            + (ref[0, x, lo - 1 : lo + CH - 1] + ref[0, x, lo + 1 : lo + CH + 1]) + (low + high)
        )

    def residual(i):
        x = 8 + 2 * i
        for lo in range(16, 80, CH):
            total = None
            for k in range(2):
                u, us = own_sum(UA, x + k, lo)
                r = DH[x + k, lo - 8 : lo - 8 + CH] * (
                    C[0, x + k, lo : lo + CH] - u + Q[0, x + k, lo : lo + CH] * us
                )
                total = r if total is None else total + r
            tmp[0, lo - 16 : lo - 16 + CH] = total
        bufs[0, i] = tmp[0, pl.ds(0, 32, stride=2)] + tmp[0, pl.ds(1, 32, stride=2)]
    loop(0, 8, residual, 2)
    L1[4, 8:16, 16:48] = dot(bufs[0].reshape(256, 128), restrict).reshape(8, 32, 128)
    pack1(4)
    a1 = send_z(zs1, zr1, 4, 1, s_a1, r_a1, 1)
    r1 = send_1(L1, 4, 1, s_b1.at[1], r_b1.at[1])

    def prepare(ref, inv, a, x_lo, x_hi, rows, inside):
        def body(x):
            i = jnp.where(inside(x), ref[0, x, 8 : 8 + rows], 0.0)
            inv[x, 8 : 8 + rows] = i
            a[0, x] = i * ref[1, x, 8 : 8 + rows]
            a[1, x] = i * ref[1, x + 1, 8 : 8 + rows]
            a[2, x] = i * ref[2, x, 8 : 8 + rows]
            a[3, x] = i * ref[2, x, 9 : 9 + rows]
            a[4, x] = i * ref[3, x, 8 : 8 + rows]
            a[5, x] = i * pltpu.roll(ref[3, x, 8 : 8 + rows], 127, 1)
        loop(x_lo, x_hi, body, 2)

    def apply(c, a, e, x, lo, n):
        r, s = slice(lo - 8, lo - 8 + n), slice(lo, lo + n)
        v = e[x, s]
        return v, (
            (c[x, r] - v)
            + (a[0, x, r] * e[x - 1, s] + a[1, x, r] * e[x + 1, s])
            + (a[2, x, r] * e[x, lo - 1 : lo - 1 + n] + a[3, x, r] * e[x, lo + 1 : lo + 1 + n])
            + (a[4, x, r] * pltpu.roll(v, 1, 1) + a[5, x, r] * pltpu.roll(v, 127, 1))
        )

    def begin(c, e, d, x_lo, x_hi, rows):
        def body(x):
            u = c[x] * (1.0 / THETA)
            e[x, 8 : 8 + rows] = u
            d[x, 0:rows] = u
        loop(x_lo, x_hi, body, 2)

    def relax(c, a, e, new, d, x_lo, x_hi, rows, alpha, beta):
        n = 2 if rows == 48 else 4

        def step(x, n):
            for lo in range(8, 8 + rows, CHC):
                values = []
                for j in range(n):
                    v, g = apply(c, a, e, x + j, lo, CHC)
                    r = slice(lo - 8, lo - 8 + CHC)
                    move = beta * g if alpha is None else alpha * d[x + j, r] + beta * g
                    values += [(d, (x + j, r), move), (new, (x + j, slice(lo, lo + CHC)), v + move)]
                for ref, index, value in values:
                    ref[index] = value

        def body(i, carry):
            step(x_lo + n * i, n)
            return carry
        lax.fori_loop(0, (x_hi - x_lo) // n, body, 0)
        if (x_hi - x_lo) % n:
            step(x_hi - (x_hi - x_lo) % n, (x_hi - x_lo) % n)

    yz1 = (
        (gy * 32 + row48 - 8 >= 0) & (gy * 32 + row48 - 8 < 128)
        & (gz * 64 + lane48 - 32 >= 0) & (gz * 64 + lane48 - 32 < 512)
    )

    def inside1(x):
        ok = ((gx * 8 + x - 8) >= 0) & ((gx * 8 + x - 8) < 32)
        return jnp.where(ok, jnp.where(yz1, 1.0, 0.0), 0.0) > 0.5

    row32 = rows_of(32)
    yz2 = (
        (gy * 16 + row32 - 8 >= 0) & (gy * 16 + row32 - 8 < 64)
        & (gz * 32 + lane32 - 48 >= 0) & (gz * 32 + lane32 - 48 < 256)
    )

    def assemble1(x):
        for a in range(4):
            base = pltpu.roll(LP[a // 2, x, 8:56], 32 if a % 2 == 0 else 96, 1)
            L1[a, x, 8:56] = extended1(a, x, base)
    for copy in b1 + c1s:
        copy.wait_recv()
    loop(1, X1 - 1, assemble1, 2)
    for copy in a1:
        copy.wait_recv()
    join1(4)
    c1r = send_c1(4, 1, 1)
    for copy in a2:
        copy.wait_recv()
    loop(0, 4, join2)
    b2 = send_2(LQ, 0, 4, s_b2.at[0], r_b2.at[0])
    c2 = send_2(zc2, 0, 4, s_c2.at[0], r_c2.at[0])
    fu = [
        send(UA.at[:, pl.ds(21, 3), pl.ds(8, 80)], XU.at[0], s_u.at[0], r_u.at[0], peer(1, 0, 0)),
        send(UA.at[:, pl.ds(8, 3), pl.ds(8, 80)], XU.at[1], s_u.at[1], r_u.at[1], peer(-1, 0, 0)),
    ]
    started += a1 + r1 + c1r + b2 + c2
    prepare(L1, I1, A1, 1, X1 - 1, 48, inside1)
    for copy in r1 + c1r:
        copy.wait_recv()

    def scale1(x):
        C1[x] = I1[x, 8:56] * extended1(4, x, L1[4, x, 8:56])
    loop(1, X1 - 1, scale1, 2)
    begin(C1, ea1, d1, 1, X1 - 1, 48)
    relax(C1, A1, ea1, eb1, d1, 2, X1 - 2, 48, *fine[0])
    relax(C1, A1, eb1, ea1, d1, 3, X1 - 3, 48, *fine[1])

    def residual1(i):
        total = None
        for k in range(2):
            x = 8 + 2 * i + k
            _, g = apply(C1, A1, ea1, x, 16, 32)
            r = D1[2 * i + k] * g
            total = r if total is None else total + r
        bufs[1, i, 0:16] = row_pairs(1, total)
    loop(0, 4, residual1)
    r2 = dot(jnp.concatenate([bufs[1, i, 0:16] for i in range(4)], 0), restrict)
    for i in range(4):
        L2[4, 4 + 4 * gx + i, 16:32] = r2[16 * i : 16 * i + 16]
    pack2(4)
    a2 = send_z(zs2, zr2, 4, 1, s_a2, r_a2, 1)
    pack_own2(4)
    r2 = send_2(LQ, 4, 1, s_b2.at[1], r_b2.at[1])
    for copy in b2 + c2:
        copy.wait_recv()

    def assemble2(slot):
        for a in range(4):
            for p in range(4):
                L2[a, 4 + 4 * slot + p, 8:40] = extended2(a, slot, p)
    loop(0, 4, assemble2)
    for copy in a2:
        copy.wait_recv()
    join2(4)
    c2r = send_2(zc2, 4, 1, s_c2.at[1], r_c2.at[1])
    prepare(L2, I2, A2, 4, 20, 32, lambda x: yz2)
    started += a2 + r2 + c2r
    for copy in r2 + c2r:
        copy.wait_recv()

    def scale2(slot):
        for p in range(4):
            x = 4 + 4 * slot + p
            C2[x] = I2[x, 8:40] * extended2(4, slot, p)
    loop(0, 4, scale2)
    begin(C2, ea2, d2, 4, 20, 32)
    pair = (ea2, eb2)
    for n, f in enumerate(factors(COARSE_STEPS)):
        relax(C2, A2, pair[n % 2], pair[1 - n % 2], d2, 4, 20, 32, *f)
    e2 = pair[(COARSE_STEPS - 1) % 2]

    widen = jnp.where(wr == 32 + wc // 2, 1.0, 0.0)

    PR[0, 0:10, 0:32] = dot(
        e2[pl.ds(4 * gx + 1, 10), 8:40].reshape(320, 128), widen
    ).reshape(10, 32, 128)

    def up1(i):
        for j in range(2):
            v = PR[0, 2 * i + j, 0:32]
            pro[j, pl.ds(0, 32, stride=2)] = v
            pro[j, pl.ds(1, 32, stride=2)] = v
        values = []
        for j in range(2):
            for k in range(2):
                x = 2 + 4 * i + 2 * j + k
                values.append((x, ea1[x, 8:56] + pro[j, 8:56]))
        for x, value in values:
            ea1[x, 8:56] = value
    loop(0, 5, up1)
    relax(C1, A1, ea1, eb1, d1, 3, X1 - 3, 48, None, 1.0 / THETA)
    relax(C1, A1, eb1, ea1, d1, 4, X1 - 4, 48, *fine[0])
    relax(C1, A1, ea1, eb1, d1, 5, X1 - 5, 48, *fine[1])

    beyond = jnp.where(
        ((wc < 8) & (wr == 96 + wc // 2)) | ((wc >= 120) & (wr == 28 + (wc - 120) // 2)), 1.0, 0.0
    )

    for copy in fu:
        copy.wait_recv()
        copy.wait_send()

    def beside(i):
        for side, x in ((0, 5 + i), (1, 24 + i)):
            scale = jnp.where(x_in(x), 1.0, 0.0)
            for k in range(2):
                UA[k, x, 8:88] = XU[side, k, i] * scale
    loop(0, 3, beside)

    both = jnp.concatenate([widen, beyond], 1)
    wide = dot(eb1[6:18, 8:56].reshape(576, 128), both)
    for k in range(2):
        PR[k] = wide[:, 128 * k : 128 * k + 128].reshape(12, 48, 128)

    def up0(i):
        for j in range(2):
            for k in range(2):
                v = PR[k, 2 * i + j]
                pro[2 * j + k, pl.ds(0, 48, stride=2)] = v
                pro[2 * j + k, pl.ds(1, 48, stride=2)] = v
        for lo in range(8, 88, CH):
            s = slice(lo, lo + CH)
            values = []
            for j in range(2):
                for n in range(2):
                    x = 4 + 4 * i + 2 * j + n
                    for k in range(2):
                        values.append(((k, x, s), UA[k, x, s] + H[k, x, s] * pro[2 * j + k, s]))
            for index, value in values:
                UA[index] = value
    loop(0, 6, up0)
    smooth(UA, UB, 6, 26, None, 1.0 / THETA)
    smooth(UB, UA, 7, 25, *fine[0])

    alpha, beta = fine[1]

    def finish(i):
        for lo in range(16, 80, CH):
            values = []
            for k in range(2):
                x = 8 + 2 * i + k
                s = slice(lo, lo + CH)
                u, us = own_sum(UA, x, lo)
                d = alpha * DU[0, x, s] + beta * (C[0, x, s] - u + Q[0, x, s] * us)
                values.append((u + d) / H[0, x, s])
            for k in range(2):
                out[2 * i + k, lo - 16 : lo - 16 + CH] = values[k]
    stores = []
    for part in range(4):
        loop(2 * part, 2 * part + 2, finish)
        planes = pl.ds(4 * part, 4)
        stores.append(pltpu.make_async_copy(out.at[planes], out_hbm.at[planes], s_out.at[part]))
        stores[-1].start()
    for copy in stores:
        copy.wait()

    for copy in started:
        copy.wait_send()


def shards(image, labels):
    def level0():
        return pltpu.VMEM((2, X0, Y0, 128), F32)

    def vmem(*shape):
        return pltpu.VMEM(shape, F32)

    def sems(*shape):
        return pltpu.SemaphoreType.DMA(shape)

    scratch = [vmem(16, 64, 128), pltpu.VMEM((16, 64, 128), jnp.int32), vmem(16, 64, 128)]
    scratch += [vmem(X0, Y0, 128), vmem(X0, Y0, 128)] + [level0() for _ in range(8)] + [
        vmem(X0, 80, 128), vmem(2, 80, 128),
        vmem(2, 2, 64, 128), vmem(2, 3, 2, 80, 128), vmem(3, 64, 128), vmem(2, 8, 32, 128), vmem(8, 40, 128),
        vmem(8, 32, 128), vmem(9, 32, 128), vmem(8, 48, 128), vmem(8, 32, 128), vmem(8, 32, 128),
        vmem(5, X1, Y1, 128), vmem(2, X1, Y1, 128), vmem(5, 32, 128), vmem(2, 5, 32, 128), vmem(5, 3, 48, 128), vmem(6, X1, 48, 128),
        vmem(X1, Y1, 128), vmem(X1, 48, 128), vmem(X1, Y1, 128), vmem(X1, Y1, 128), vmem(X1, Y1, 128),
        vmem(5, X2, Y2, 128), vmem(5, 4, 32, 128), vmem(5, 16, 128), vmem(2, 5, 16, 128), vmem(5, 4, 32, 128), vmem(6, X2, 32, 128),
        vmem(X2, Y2, 128), vmem(X2, 32, 128), vmem(X2, Y2, 128), vmem(X2, Y2, 128), vmem(X2, Y2, 128),
        vmem(4, 16, 128), vmem(4, 96, 128), vmem(2, 12, 48, 128),
        sems(8), sems(8), sems(8), sems(8), sems(2, 2), sems(2, 2), sems(2, 8), sems(2, 8),
        sems(2, 2), sems(2, 2), sems(2, 8), sems(2, 8), sems(2, 8), sems(2, 8),
        sems(2, 2), sems(2, 2), sems(2, 11), sems(2, 11), sems(2, 11), sems(2, 11),
        sems(2), sems(4), vmem(2, 2, 3, 80, 128), sems(2), sems(2),
    ]
    return pl.pallas_call(
        kernel,
        out_shape=jax.ShapeDtypeStruct(image.shape, F32),
        in_specs=[pl.BlockSpec(memory_space=pl.ANY)] * 2,
        out_specs=pl.BlockSpec(memory_space=pl.ANY),
        scratch_shapes=scratch,
        compiler_params=pltpu.CompilerParams(
            collective_id=0, has_side_effects=True, vmem_limit_bytes=56 * 1024 * 1024
        ),
    )(image, labels)


def solution(mesh):
    placed = (P("gx", "gy", "gz"), P("gx", "gy", "gz"))
    return jax.shard_map(
        shards, mesh=mesh, in_specs=placed, out_specs=P("gx", "gy", "gz"), check_vma=False
    )
```

```python
import jax
import jax.numpy as jnp
from jax import lax
from jax.experimental import pallas as pl
from jax.experimental.pallas import tpu as pltpu
from jax.sharding import PartitionSpec as P

SMOOTH_STEPS = 3
COARSE_STEPS = 6
HEAT_CONSTANT = 0.25
SCREENING = 0.002
SEED_WEIGHT = 1.0
THETA = 1.1
DELTA = 0.9

MESH = pl.DeviceIdType.MESH
F32 = jnp.float32
SIZES = {"gx": 4, "gy": 4, "gz": 8}

X0, Y0 = 32, 96
X1, Y1 = 24, 64
X2, Y2 = 24, 48

PLANAR = [(dx, dy) for dx in (1, -1, 0) for dy in (1, -1, 0) if (dx, dy) != (0, 0)]
COLUMN = [(dx, dy) for dx in (1, -1, 2, 0) for dy in (1, -1, 0) if (dx, dy) != (0, 0)]


def factors(steps):
    sigma = THETA / DELTA
    rho = 1.0 / sigma
    out = []
    for _ in range(steps - 1):
        rho_new = 1.0 / (2.0 * sigma - rho)
        out.append((rho_new * rho, 2.0 * rho_new / DELTA))
        rho = rho_new
    return out


def peer(dx, dy, dz):
    shift = {"gx": dx, "gy": dy, "gz": dz}
    return {a: lax.rem(lax.axis_index(a) + shift[a] + n, n) for a, n in SIZES.items()}


def dot(a, b):
    return jnp.dot(a, b, precision=lax.Precision.HIGHEST, preferred_element_type=F32)


def kernel(
    image_hbm, labels_hbm, out_hbm,
    image, labels, out,
    E, L, EM, R, H, UA, UB, DU, C, Q, DH, M,
    zs0, zr0, tmp, bufs, wyb, c1, wx1, wy1, wz1, D1,
    L1, LP, zs1, zr1, zc1, A1, I1, C1, ea1, eb1, d1,
    L2, LQ, zs2, zr2, zc2, A2, I2, C2, ea2, eb2, d2, D2, pro, PR,
    s_e, r_e, s_l, r_l, s_z0, r_z0, s_b0, r_b0,
    s_a1, r_a1, s_b1, r_b1, s_c1, r_c1, s_a2, r_a2, s_b2, r_b2, s_c2, r_c2,
    s_in, s_out, XU, s_u, r_u,
):
    gx, gy, gz = (lax.axis_index(a) for a in ("gx", "gy", "gz"))
    barrier = pltpu.get_barrier_semaphore()
    partners = [(dx, dy, 0) for dx, dy in COLUMN] + [(0, 0, 1), (0, 0, -1)]
    for p in partners:
        pl.semaphore_signal(barrier, inc=1, device_id=peer(*p), device_id_type=MESH)

    loads = [
        pltpu.make_async_copy(image_hbm, image, s_in.at[0]),
        pltpu.make_async_copy(labels_hbm, labels, s_in.at[1]),
    ]
    for copy in loads:
        copy.start()

    def lanes(rows):
        return lax.broadcasted_iota(jnp.int32, (rows, 128), 1)

    def rows_of(rows):
        return lax.broadcasted_iota(jnp.int32, (rows, 128), 0)

    def send(src, dst, ssem, rsem, to):
        copy = pltpu.make_async_remote_copy(
            src_ref=src, dst_ref=dst, send_sem=ssem, recv_sem=rsem, device_id=to, device_id_type=MESH
        )
        copy.start()
        return copy

    started = []

    def loop(lo, hi, body, unroll=1):
        def step(i, carry):
            body(i)
            return carry
        lax.fori_loop(lo, hi, step, 0, unroll=unroll)

    loads[0].wait()

    def own(x):
        E[8 + x, 16:80] = jnp.exp(image[x] * (1.0 / HEAT_CONSTANT))
    loop(0, 16, own, 2)
    pl.semaphore_wait(barrier, len(partners))

    def x_range(dx, start, count, width):
        if dx == 0:
            return pl.ds(start, count), pl.ds(start, count)
        if dx == 1:
            return pl.ds(start + count - width, width), pl.ds(start - width, width)
        return pl.ds(start, width), pl.ds(start + count, width)

    def y_range(dy, start, count):
        if dy == 0:
            return pl.ds(start, count), pl.ds(start, count)
        if dy == 1:
            return pl.ds(start + count - 8, 8), pl.ds(start - 8, 8)
        return pl.ds(start, 8), pl.ds(start + count, 8)

    def send_own(ref, width, ssem, rsem):
        copies = []
        for i, (dx, dy) in enumerate(PLANAR):
            ys, yd = y_range(dy, 16, 64)
            xs, xd = x_range(dx, 8, 16, width)
            copies.append(send(ref.at[xs, ys], ref.at[xd, yd], ssem.at[i], rsem.at[i], peer(dx, dy, 0)))
        return copies

    own_e = send_own(E, 5, s_e, r_e)
    loads[1].wait()

    def own_labels(x):
        L[8 + x, 16:80] = labels[x].astype(F32)
    loop(0, 16, own_labels)

    group64 = lanes(64) // 8

    def pack(p, carry):
        result = []
        for k, ref in enumerate((E, L)):
            v = ref[8 + p, 16:80]
            low = pltpu.roll(v, lax.rem(8 * p, 128), 1)
            high = pltpu.roll(v, lax.rem(8 * p + 8, 128), 1)
            result.append(jnp.where(group64 == p, low, carry[2 * k]))
            result.append(jnp.where(group64 == p, high, carry[2 * k + 1]))
        return tuple(result)

    zero64 = jnp.zeros((64, 128), F32)
    packed = lax.fori_loop(0, 16, pack, (zero64,) * 4)
    for k in range(2):
        zs0[k, 1] = packed[2 * k]
        zs0[k, 0] = packed[2 * k + 1]
    za = [
        [
            send(zs0.at[k, s], zr0.at[k, 1, s, pl.ds(8, 64)], s_z0.at[k, s], r_z0.at[k, s],
                 peer(0, 0, 1 if s == 0 else -1))
            for s in range(2)
        ]
        for k in range(2)
    ]

    def forward(k):
        for copy in za[k]:
            copy.wait_recv()
        copies = []
        for i, (dx, dy) in enumerate(PLANAR):
            ys, yd = y_range(dy, 8, 64)
            copies.append(send(zr0.at[k, 1, :, ys], zr0.at[k, 1 - dx, :, yd],
                               s_b0.at[k, i], r_b0.at[k, i], peer(dx, dy, 0)))
        return copies

    for ref in (ea1, eb1, d1):
        def clear(x, ref=ref):
            ref[x] = jnp.zeros((Y1, 128), F32)
        loop(0, X1, clear)
    for ref in (ea2, eb2, d2):
        def clear(x, ref=ref):
            ref[x] = jnp.zeros((Y2, 128), F32)
        loop(0, X2, clear)

    def guard1(a):
        for x in (0, X1 - 1):
            L1[a, x] = jnp.zeros((Y1, 128), F32)

        def edge(x):
            L1[a, x, 0:8] = jnp.zeros((8, 128), F32)
            L1[a, x, 56:64] = jnp.zeros((8, 128), F32)
        loop(1, X1 - 1, edge)
    loop(0, 5, guard1)

    def guard2(a):
        for x in (0, 1, 2, 3, 20, 21, 22, 23):
            L2[a, x] = jnp.zeros((Y2, 128), F32)

        def edge(x):
            L2[a, x, 0:8] = jnp.zeros((8, 128), F32)
            L2[a, x, 40:48] = jnp.zeros((8, 128), F32)
        loop(4, 20, edge)
    loop(0, 5, guard2)

    lane80, row80 = lanes(80), rows_of(80)
    y_in = ((gy * 64 + row80 - 8) >= 0) & ((gy * 64 + row80 - 8) < 256)
    M[0] = jnp.where(y_in, 1.0, 0.0)
    z_in = ((lane80 < 8) & (gz < 7)) | ((lane80 >= 120) & (gz > 0))
    M[1] = jnp.where(y_in & z_in, 1.0, 0.0)

    zb_e = forward(0)
    own_l = send_own(L, 3, s_l, r_l)
    zb_l = forward(1)
    started += za[0] + za[1] + own_e + own_l + zb_e + zb_l
    for i, (dx, dy) in enumerate(PLANAR):
        if dx == 0:
            own_e[i].wait_recv()
            zb_e[i].wait_recv()

    def x_in(x):
        return ((gx * 16 + x - 8) >= 0) & ((gx * 16 + x - 8) < 64)

    CH, GROUP, CHC = 16, 4, 16

    def sweep(lo_x, hi_x, work, n=GROUP):
        def step(x, n):
            for lo in range(8, 88, CH):
                stores = []
                for j in range(n):
                    stores += work(x + j, lo)
                for ref, index, value in stores:
                    ref[index] = value

        def body(i, carry):
            step(lo_x + n * i, n)
            return carry
        lax.fori_loop(0, (hi_x - lo_x) // n, body, 0)
        if (hi_x - lo_x) % n:
            step(hi_x - (hi_x - lo_x) % n, (hi_x - lo_x) % n)

    lane = lanes(CH)
    at0, at127 = lane == 0, lane == 127

    def z_pair(t0, t1):
        r0, r1 = pltpu.roll(t0, 1, 1), pltpu.roll(t1, 1, 1)
        q0, q1 = pltpu.roll(t0, 127, 1), pltpu.roll(t1, 127, 1)
        return (
            jnp.where(at0, r1, r0) + jnp.where(at127, q1, q0),
            jnp.where(at0, r0, r1) + jnp.where(at127, q0, q1),
        )

    def around(ref, x, lo):
        t = [ref[k, x, lo : lo + CH] for k in range(2)]
        z = z_pair(*t)
        total = []
        for k in range(2):
            total.append(
                (ref[k, x - 1, lo : lo + CH] + ref[k, x + 1, lo : lo + CH])
                + (ref[k, x, lo - 1 : lo + CH - 1] + ref[k, x, lo + 1 : lo + CH + 1])
                + z[k]
            )
        return t, total

    def ends(k, x, r):
        p, n = lax.rem(x + 8, 16), (x + 8) // 16
        up = pltpu.roll(zr0[k, n, 1, r], lax.rem(256 - 8 * p, 128), 1)
        down = pltpu.roll(zr0[k, n, 0, r], lax.rem(248 - 8 * p, 128), 1)
        return jnp.where(lane < 8, up, down)

    def spread(x, lo):
        inside = x_in(x)
        r = pl.ds(lo - 8, CH)
        s = slice(lo, lo + CH)
        stores = []
        for t, v in ((0, E[x, s]), (1, ends(0, x, r))):
            m = jnp.where(inside, M[t, r], 0.0) > 0.5
            v = jnp.where(m, v, 1.0)
            stores += [(EM, (t, x, s), v), (R, (t, x, s), 1.0 / v)]
        return stores

    sweep(8, 24, spread)

    def heights(x, lo):
        e, es = around(EM, x, lo)
        c, cs = around(R, x, lo)
        stores = []
        for k in range(2):
            t = (e[k] + es[k]) * (c[k] + cs[k])
            stores.append((H, (k, x, slice(lo, lo + CH)), lax.rsqrt(lax.rsqrt(lax.rsqrt(t)))))
        return stores

    sweep(9, 23, heights)
    for i, (dx, dy) in enumerate(PLANAR):
        if dx != 0:
            own_e[i].wait_recv()
            zb_e[i].wait_recv()
    sweep(6, 8, spread)
    sweep(24, 26, spread)
    sweep(7, 9, heights)
    sweep(23, 25, heights)

    def cells_of(v):
        return SCREENING + SEED_WEIGHT * jnp.where(v != 2.0, 1.0, 0.0)

    def row_pairs(slot, v):
        n = v.shape[0]
        tmp[slot, 0:n] = v
        return tmp[slot, pl.ds(0, n // 2, stride=2)] + tmp[slot, pl.ds(1, n // 2, stride=2)]

    lane64 = lanes(64)

    def coarse(i):
        x = 8 + 2 * i
        bufs[0, i] = row_pairs(0, cells_of(L[x, 16:80]) + cells_of(L[x + 1, 16:80]))
        wyb[i] = (
            H[0, x, pl.ds(16, 40, stride=2)] * H[0, x, pl.ds(15, 40, stride=2)]
            + H[0, x + 1, pl.ds(16, 40, stride=2)] * H[0, x + 1, pl.ds(15, 40, stride=2)]
        )
        total = None
        for k in range(2):
            h0, h1 = H[0, x + k, 16:80], H[1, x + k, 16:80]
            r0, r1 = pltpu.roll(h0, 1, 1), pltpu.roll(h1, 1, 1)
            v = h0 * jnp.where(lane64 == 0, r1, r0)
            beyond = pltpu.roll(h1, 1, 1) * pltpu.roll(h0, 2, 1)
            v = jnp.where(lane64 == 1, beyond, v)
            total = v if total is None else total + v
        bufs[1, i] = row_pairs(1, total)
    loop(0, 8, coarse, 2)

    def coarse_x(i):
        x = 8 + 2 * i
        wx1[i] = row_pairs(2, H[0, x, 16:80] * H[0, x - 1, 16:80])
    loop(0, 9, coarse_x, 3)

    wr, wc = rows_of(128), lanes(128)
    restrict = jnp.where(wc == 32 + wr // 2, 1.0, 0.0)
    even = jnp.where((wc == 32 + wr // 2) & (lax.rem(wr, 2) == 0), 1.0, 0.0)
    last = jnp.where((wr == 1) & (wc == 96), 1.0, 0.0)
    c1[...] = dot(bufs[0].reshape(256, 128), restrict).reshape(8, 32, 128)
    wx1[...] = dot(wx1[...].reshape(288, 128), restrict).reshape(9, 32, 128)
    wy1[:, 0:40] = dot(wyb[...].reshape(320, 128), restrict).reshape(8, 40, 128)
    wz1[...] = dot(bufs[1].reshape(256, 128), even + last).reshape(8, 32, 128)

    lane32 = lanes(32)
    own1 = (lane32 >= 32) & (lane32 < 96)

    def level1(i):
        wz = wz1[i]
        d = (
            c1[i] + (wx1[i] + wx1[i + 1]) + (wy1[i, 0:32] + wy1[i, 1:33])
            + (wz + pltpu.roll(wz, 127, 1))
        )
        D1[i] = jnp.where(own1, d, 0.0)
        four = (jnp.where(own1, 1.0 / jnp.where(own1, d, 1.0), 0.0), wx1[i], wy1[i, 0:32], wz)
        for a in range(4):
            L1[a, 8 + i, 16:48] = four[a]
        for a in range(2):
            LP[a, 8 + i, 16:48] = jnp.where(
                lane32 < 64, pltpu.roll(four[2 * a], 96, 1), pltpu.roll(four[2 * a + 1], 32, 1)
            )
    loop(0, 8, level1, 2)

    def send_1(src, which, width, ssem, rsem):
        copies = []
        for i, (dx, dy) in enumerate(PLANAR):
            ys, yd = y_range(dy, 16, 32)
            xs, xd = x_range(dx, 8, 8, 7)
            copies.append(send(src.at[pl.ds(which, width), xs, ys], src.at[pl.ds(which, width), xd, yd],
                               ssem.at[i], rsem.at[i], peer(dx, dy, 0)))
        return copies

    b1 = send_1(LP, 0, 2, s_b1.at[0], r_b1.at[0])

    lane16 = lanes(16)
    own2 = (lane16 >= 48) & (lane16 < 80)
    c2 = [row_pairs(0, c1[2 * i] + c1[2 * i + 1]) for i in range(4)]
    z2 = [row_pairs(1, wz1[2 * i] + wz1[2 * i + 1]) for i in range(4)]
    x2 = [row_pairs(2, wx1[2 * i]) for i in range(5)]
    y2 = [
        wy1[2 * i, pl.ds(0, 24, stride=2)] + wy1[2 * i + 1, pl.ds(0, 24, stride=2)] for i in range(4)
    ]
    c2 = dot(jnp.concatenate(c2, 0), restrict)
    x2 = dot(jnp.concatenate(x2, 0), restrict)
    y2 = dot(jnp.concatenate(y2, 0), restrict)
    z2 = dot(jnp.concatenate(z2, 0), even)
    for i in range(4):
        for k in range(3):
            tmp[k, 0:24] = y2[24 * i : 24 * i + 24]
        wz = z2[16 * i : 16 * i + 16]
        d = (
            c2[16 * i : 16 * i + 16]
            + (x2[16 * i : 16 * i + 16] + x2[16 * i + 16 : 16 * i + 32])
            + (tmp[0, 0:16] + tmp[0, 1:17]) + (wz + pltpu.roll(wz, 127, 1))
        )
        D2[i] = jnp.where(own2, d, 0.0)
        at = 4 + 4 * gx + i
        L2[0, at, 16:32] = jnp.where(own2, 1.0 / jnp.where(own2, d, 1.0), 0.0)
        L2[1, at, 16:32] = x2[16 * i : 16 * i + 16]
        L2[2, at, 16:32] = tmp[0, 0:16]
        L2[3, at, 16:32] = wz

    group32, group16 = lane32 // 8, lane16 // 8

    def pack_z(ref, a, base, planes, rows, lo, hi, group, dst):
        acc = jnp.zeros((rows, 128), F32)
        for p in range(planes):
            v = ref[a, base + p, 16 : 16 + rows]
            acc = jnp.where(group == p, pltpu.roll(v, (8 * p - lo) % 128, 1), acc)
            acc = jnp.where(group == 8 + p, pltpu.roll(v, (64 + 8 * p - hi) % 128, 1), acc)
        dst[a] = acc

    def joined(zr, zc, a, slot, rows, ln):
        zc[a, slot, 8 : 8 + rows] = jnp.where(ln < 64, zr[1, a], zr[0, a])

    def extended(base, ends, p, ln, lo, hi):
        down = pltpu.roll(ends, lax.rem(256 + lo - 8 - 64 - 8 * p, 128), 1)
        up = pltpu.roll(ends, lax.rem(256 + hi + 8 - 8 * p, 128), 1)
        v = jnp.where((ln >= lo) & (ln < hi + 8), base, 0.0)
        v = jnp.where((ln >= lo - 8) & (ln < lo), down, v)
        return jnp.where((ln >= hi + 8) & (ln < hi + 16), up, v)

    def pack1(a):
        pack_z(L1, a, 8, 8, 32, 32, 88, group32, zs1)

    def join1(a):
        joined(zr1, zc1, a, 1, 32, lane32)

    def extended1(a, x, base):
        return extended(base, zc1[a, x // 8], lax.rem(x, 8), lane48, 32, 88)

    def pack2(a):
        pack_z(L2, a, 4 + 4 * gx, 4, 16, 48, 72, group16, zs2)

    def join2(a):
        joined(zr2, zc2, a, gx, 16, lane16)

    def pack_own2(a):
        acc = jnp.zeros((16, 128), F32)
        for p in range(4):
            v = pltpu.roll(L2[a, 4 + 4 * gx + p, 16:32], (32 * p - 48) % 128, 1)
            acc = jnp.where(lane16 // 32 == p, v, acc)
        LQ[a, gx, 8:24] = acc

    def extended2(a, slot, p):
        base = pltpu.roll(LQ[a, slot], (48 - 32 * p) % 128, 1)
        return extended(base, zc2[a, slot], p, lane32, 48, 72)

    def send_z(zs, zr, which, n, ssem, rsem, slot):
        return [
            send(zs.at[pl.ds(which, n)], zr.at[s, pl.ds(which, n)], ssem.at[slot, s], rsem.at[slot, s],
                 peer(0, 0, 1 if s == 0 else -1))
            for s in range(2)
        ]

    def send_c1(which, n, slot):
        copies = []
        for i, (dx, dy) in enumerate(PLANAR):
            ys, yd = y_range(dy, 8, 32)
            copies.append(send(zc1.at[pl.ds(which, n), 1, ys], zc1.at[pl.ds(which, n), 1 - dx, yd],
                               s_c1.at[slot, i], r_c1.at[slot, i], peer(dx, dy, 0)))
        return copies

    def send_2(ref, which, n, ssem, rsem):
        copies = []
        for i, (dx, dy) in enumerate(COLUMN):
            ys, yd = y_range(dy, 8, 16)
            copies.append(send(ref.at[pl.ds(which, n), gx, ys], ref.at[pl.ds(which, n), gx, yd],
                               ssem.at[i], rsem.at[i], peer(dx, dy, 0)))
        return copies

    lane48, row48 = lanes(48), rows_of(48)
    loop(0, 4, pack1, 2)
    a1 = send_z(zs1, zr1, 0, 4, s_a1, r_a1, 0)
    loop(0, 4, pack2)
    a2 = send_z(zs2, zr2, 0, 4, s_a2, r_a2, 0)
    loop(0, 4, pack_own2)
    sweep(3, 6, spread)
    sweep(26, 29, spread)
    sweep(4, 7, heights)
    sweep(25, 28, heights)
    for copy in a1:
        copy.wait_recv()
    loop(0, 4, join1)
    c1s = send_c1(0, 4, 0)

    def diagonal(x, lo):
        inside = x_in(x)
        h, hs = around(H, x, lo)
        r = pl.ds(lo - 8, CH)
        s = slice(lo, lo + CH)
        stores = []
        for k in range(2):
            m = jnp.where(inside, M[k, r], 0.0)
            lab = L[x, s] if k == 0 else ends(1, x, r)
            d = cells_of(lab) + h[k] * hs[k]
            hi = m * h[k] / d
            c = jnp.where(lab == 1.0, SEED_WEIGHT * hi, 0.0)
            u = c * (1.0 / THETA)
            stores += [
                (C, (k, x, s), c), (Q, (k, x, s), hi * h[k]), (UA, (k, x, s), u), (DU, (k, x, s), u)
            ]
            if k == 0:
                stores.append((DH, (x, r), d / h[k]))
        return stores

    for copy in own_l + zb_l:
        copy.wait_recv()
    sweep(5, 27, diagonal)
    started += a1 + a2 + b1 + c1s

    def smooth(src, dst, lo_x, hi_x, alpha, beta, keep=True):
        def work(x, lo):
            u, us = around(src, x, lo)
            s = slice(lo, lo + CH)
            stores = []
            for k in range(2):
                g = beta * (C[k, x, s] - u[k] + Q[k, x, s] * us[k])
                d = g if alpha is None else alpha * DU[k, x, s] + g
                if keep:
                    stores.append((DU, (k, x, s), d))
                stores.append((dst, (k, x, s), u[k] + d))
            return stores
        sweep(lo_x, hi_x, work)

    fine = factors(SMOOTH_STEPS)
    smooth(UA, UB, 6, 26, *fine[0])
    smooth(UB, UA, 7, 25, *fine[1], keep=False)

    lane_ch = lanes(CH)

    def own_sum(ref, x, lo):
        t0, t1 = ref[0, x, lo : lo + CH], ref[1, x, lo : lo + CH]
        low = jnp.where(lane_ch == 0, pltpu.roll(t1, 1, 1), pltpu.roll(t0, 1, 1))
        high = jnp.where(lane_ch == 127, pltpu.roll(t1, 127, 1), pltpu.roll(t0, 127, 1))
        return t0, (
            (ref[0, x - 1, lo : lo + CH] + ref[0, x + 1, lo : lo + CH])
            + (ref[0, x, lo - 1 : lo + CH - 1] + ref[0, x, lo + 1 : lo + CH + 1]) + (low + high)
        )

    def residual(i):
        x = 8 + 2 * i
        for lo in range(16, 80, CH):
            total = None
            for k in range(2):
                u, us = own_sum(UA, x + k, lo)
                r = DH[x + k, lo - 8 : lo - 8 + CH] * (
                    C[0, x + k, lo : lo + CH] - u + Q[0, x + k, lo : lo + CH] * us
                )
                total = r if total is None else total + r
            tmp[0, lo - 16 : lo - 16 + CH] = total
        bufs[0, i] = tmp[0, pl.ds(0, 32, stride=2)] + tmp[0, pl.ds(1, 32, stride=2)]
    loop(0, 8, residual, 2)
    L1[4, 8:16, 16:48] = dot(bufs[0].reshape(256, 128), restrict).reshape(8, 32, 128)
    pack1(4)
    a1 = send_z(zs1, zr1, 4, 1, s_a1, r_a1, 1)
    r1 = send_1(L1, 4, 1, s_b1.at[1], r_b1.at[1])

    def prepare(ref, inv, a, x_lo, x_hi, rows, inside):
        def body(x):
            i = jnp.where(inside(x), ref[0, x, 8 : 8 + rows], 0.0)
            inv[x, 8 : 8 + rows] = i
            a[0, x] = i * ref[1, x, 8 : 8 + rows]
            a[1, x] = i * ref[1, x + 1, 8 : 8 + rows]
            a[2, x] = i * ref[2, x, 8 : 8 + rows]
            a[3, x] = i * ref[2, x, 9 : 9 + rows]
            a[4, x] = i * ref[3, x, 8 : 8 + rows]
            a[5, x] = i * pltpu.roll(ref[3, x, 8 : 8 + rows], 127, 1)
        loop(x_lo, x_hi, body, 2)

    def apply(c, a, e, x, lo, n):
        r, s = slice(lo - 8, lo - 8 + n), slice(lo, lo + n)
        v = e[x, s]
        return v, (
            (c[x, r] - v)
            + (a[0, x, r] * e[x - 1, s] + a[1, x, r] * e[x + 1, s])
            + (a[2, x, r] * e[x, lo - 1 : lo - 1 + n] + a[3, x, r] * e[x, lo + 1 : lo + 1 + n])
            + (a[4, x, r] * pltpu.roll(v, 1, 1) + a[5, x, r] * pltpu.roll(v, 127, 1))
        )

    def begin(c, e, d, x_lo, x_hi, rows):
        def body(x):
            u = c[x] * (1.0 / THETA)
            e[x, 8 : 8 + rows] = u
            d[x, 0:rows] = u
        loop(x_lo, x_hi, body, 2)

    def relax(c, a, e, new, d, x_lo, x_hi, rows, alpha, beta):
        n = 2 if rows == 48 else 4

        def step(x, n):
            for lo in range(8, 8 + rows, CHC):
                values = []
                for j in range(n):
                    v, g = apply(c, a, e, x + j, lo, CHC)
                    r = slice(lo - 8, lo - 8 + CHC)
                    move = beta * g if alpha is None else alpha * d[x + j, r] + beta * g
                    values += [(d, (x + j, r), move), (new, (x + j, slice(lo, lo + CHC)), v + move)]
                for ref, index, value in values:
                    ref[index] = value

        def body(i, carry):
            step(x_lo + n * i, n)
            return carry
        lax.fori_loop(0, (x_hi - x_lo) // n, body, 0)
        if (x_hi - x_lo) % n:
            step(x_hi - (x_hi - x_lo) % n, (x_hi - x_lo) % n)

    yz1 = (
        (gy * 32 + row48 - 8 >= 0) & (gy * 32 + row48 - 8 < 128)
        & (gz * 64 + lane48 - 32 >= 0) & (gz * 64 + lane48 - 32 < 512)
    )

    def inside1(x):
        ok = ((gx * 8 + x - 8) >= 0) & ((gx * 8 + x - 8) < 32)
        return jnp.where(ok, jnp.where(yz1, 1.0, 0.0), 0.0) > 0.5

    row32 = rows_of(32)
    yz2 = (
        (gy * 16 + row32 - 8 >= 0) & (gy * 16 + row32 - 8 < 64)
        & (gz * 32 + lane32 - 48 >= 0) & (gz * 32 + lane32 - 48 < 256)
    )

    def assemble1(x):
        for a in range(4):
            base = pltpu.roll(LP[a // 2, x, 8:56], 32 if a % 2 == 0 else 96, 1)
            L1[a, x, 8:56] = extended1(a, x, base)
    for copy in b1 + c1s:
        copy.wait_recv()
    loop(1, X1 - 1, assemble1, 2)
    for copy in a1:
        copy.wait_recv()
    join1(4)
    c1r = send_c1(4, 1, 1)
    for copy in a2:
        copy.wait_recv()
    loop(0, 4, join2)
    b2 = send_2(LQ, 0, 4, s_b2.at[0], r_b2.at[0])
    c2 = send_2(zc2, 0, 4, s_c2.at[0], r_c2.at[0])
    fu = [
        send(UA.at[:, pl.ds(21, 3), pl.ds(8, 80)], XU.at[0], s_u.at[0], r_u.at[0], peer(1, 0, 0)),
        send(UA.at[:, pl.ds(8, 3), pl.ds(8, 80)], XU.at[1], s_u.at[1], r_u.at[1], peer(-1, 0, 0)),
    ]
    started += a1 + r1 + c1r + b2 + c2
    prepare(L1, I1, A1, 1, X1 - 1, 48, inside1)
    for copy in r1 + c1r:
        copy.wait_recv()

    def scale1(x):
        C1[x] = I1[x, 8:56] * extended1(4, x, L1[4, x, 8:56])
    loop(1, X1 - 1, scale1, 2)
    begin(C1, ea1, d1, 1, X1 - 1, 48)
    relax(C1, A1, ea1, eb1, d1, 2, X1 - 2, 48, *fine[0])
    relax(C1, A1, eb1, ea1, d1, 3, X1 - 3, 48, *fine[1])

    def residual1(i):
        total = None
        for k in range(2):
            x = 8 + 2 * i + k
            _, g = apply(C1, A1, ea1, x, 16, 32)
            r = D1[2 * i + k] * g
            total = r if total is None else total + r
        bufs[1, i, 0:16] = row_pairs(1, total)
    loop(0, 4, residual1, 2)
    r2 = dot(jnp.concatenate([bufs[1, i, 0:16] for i in range(4)], 0), restrict)
    for i in range(4):
        L2[4, 4 + 4 * gx + i, 16:32] = r2[16 * i : 16 * i + 16]
    pack2(4)
    a2 = send_z(zs2, zr2, 4, 1, s_a2, r_a2, 1)
    pack_own2(4)
    r2 = send_2(LQ, 4, 1, s_b2.at[1], r_b2.at[1])
    for copy in b2 + c2:
        copy.wait_recv()

    def assemble2(slot):
        for a in range(4):
            for p in range(4):
                L2[a, 4 + 4 * slot + p, 8:40] = extended2(a, slot, p)
    loop(0, 4, assemble2, 2)
    for copy in a2:
        copy.wait_recv()
    join2(4)
    c2r = send_2(zc2, 4, 1, s_c2.at[1], r_c2.at[1])
    prepare(L2, I2, A2, 4, 20, 32, lambda x: yz2)
    started += a2 + r2 + c2r
    for copy in r2 + c2r:
        copy.wait_recv()

    def scale2(slot):
        for p in range(4):
            x = 4 + 4 * slot + p
            C2[x] = I2[x, 8:40] * extended2(4, slot, p)
    loop(0, 4, scale2, 2)
    begin(C2, ea2, d2, 4, 20, 32)
    pair = (ea2, eb2)
    for n, f in enumerate(factors(COARSE_STEPS)):
        relax(C2, A2, pair[n % 2], pair[1 - n % 2], d2, 4, 20, 32, *f)
    e2 = pair[(COARSE_STEPS - 1) % 2]

    widen = jnp.where(wr == 32 + wc // 2, 1.0, 0.0)

    PR[0, 0:10, 0:32] = dot(
        e2[pl.ds(4 * gx + 1, 10), 8:40].reshape(320, 128), widen
    ).reshape(10, 32, 128)

    def up1(i):
        for j in range(2):
            v = PR[0, 2 * i + j, 0:32]
            pro[j, pl.ds(0, 32, stride=2)] = v
            pro[j, pl.ds(1, 32, stride=2)] = v
        values = []
        for j in range(2):
            for k in range(2):
                x = 2 + 4 * i + 2 * j + k
                values.append((x, ea1[x, 8:56] + pro[j, 8:56]))
        for x, value in values:
            ea1[x, 8:56] = value
    loop(0, 5, up1)
    relax(C1, A1, ea1, eb1, d1, 3, X1 - 3, 48, None, 1.0 / THETA)
    relax(C1, A1, eb1, ea1, d1, 4, X1 - 4, 48, *fine[0])
    relax(C1, A1, ea1, eb1, d1, 5, X1 - 5, 48, *fine[1])

    beyond = jnp.where(
        ((wc < 8) & (wr == 96 + wc // 2)) | ((wc >= 120) & (wr == 28 + (wc - 120) // 2)), 1.0, 0.0
    )

    for copy in fu:
        copy.wait_recv()
        copy.wait_send()

    def beside(i):
        for side, x in ((0, 5 + i), (1, 24 + i)):
            scale = jnp.where(x_in(x), 1.0, 0.0)
            for k in range(2):
                UA[k, x, 8:88] = XU[side, k, i] * scale
    loop(0, 3, beside)

    both = jnp.concatenate([widen, beyond], 1)
    wide = dot(eb1[6:18, 8:56].reshape(576, 128), both)
    for k in range(2):
        PR[k] = wide[:, 128 * k : 128 * k + 128].reshape(12, 48, 128)

    def up0(i):
        for j in range(2):
            for k in range(2):
                v = PR[k, 2 * i + j]
                pro[2 * j + k, pl.ds(0, 48, stride=2)] = v
                pro[2 * j + k, pl.ds(1, 48, stride=2)] = v
        for lo in range(8, 88, CH):
            s = slice(lo, lo + CH)
            values = []
            for j in range(2):
                for n in range(2):
                    x = 4 + 4 * i + 2 * j + n
                    for k in range(2):
                        values.append(((k, x, s), UA[k, x, s] + H[k, x, s] * pro[2 * j + k, s]))
            for index, value in values:
                UA[index] = value
    loop(0, 6, up0, 2)
    smooth(UA, UB, 6, 26, None, 1.0 / THETA)
    smooth(UB, UA, 7, 25, *fine[0])

    alpha, beta = fine[1]

    def finish(i):
        for lo in range(16, 80, CH):
            values = []
            for k in range(2):
                x = 8 + 2 * i + k
                s = slice(lo, lo + CH)
                u, us = own_sum(UA, x, lo)
                d = alpha * DU[0, x, s] + beta * (C[0, x, s] - u + Q[0, x, s] * us)
                values.append((u + d) / H[0, x, s])
            for k in range(2):
                out[2 * i + k, lo - 16 : lo - 16 + CH] = values[k]
    stores = []
    for part in range(4):
        loop(2 * part, 2 * part + 2, finish)
        planes = pl.ds(4 * part, 4)
        stores.append(pltpu.make_async_copy(out.at[planes], out_hbm.at[planes], s_out.at[part]))
        stores[-1].start()
    for copy in stores:
        copy.wait()

    for copy in started:
        copy.wait_send()


def shards(image, labels):
    def level0():
        return pltpu.VMEM((2, X0, Y0, 128), F32)

    def vmem(*shape):
        return pltpu.VMEM(shape, F32)

    def sems(*shape):
        return pltpu.SemaphoreType.DMA(shape)

    scratch = [vmem(16, 64, 128), pltpu.VMEM((16, 64, 128), jnp.int32), vmem(16, 64, 128)]
    scratch += [vmem(X0, Y0, 128), vmem(X0, Y0, 128)] + [level0() for _ in range(8)] + [
        vmem(X0, 80, 128), vmem(2, 80, 128),
        vmem(2, 2, 64, 128), vmem(2, 3, 2, 80, 128), vmem(3, 64, 128), vmem(2, 8, 32, 128), vmem(8, 40, 128),
        vmem(8, 32, 128), vmem(9, 32, 128), vmem(8, 48, 128), vmem(8, 32, 128), vmem(8, 32, 128),
        vmem(5, X1, Y1, 128), vmem(2, X1, Y1, 128), vmem(5, 32, 128), vmem(2, 5, 32, 128), vmem(5, 3, 48, 128), vmem(6, X1, 48, 128),
        vmem(X1, Y1, 128), vmem(X1, 48, 128), vmem(X1, Y1, 128), vmem(X1, Y1, 128), vmem(X1, Y1, 128),
        vmem(5, X2, Y2, 128), vmem(5, 4, 32, 128), vmem(5, 16, 128), vmem(2, 5, 16, 128), vmem(5, 4, 32, 128), vmem(6, X2, 32, 128),
        vmem(X2, Y2, 128), vmem(X2, 32, 128), vmem(X2, Y2, 128), vmem(X2, Y2, 128), vmem(X2, Y2, 128),
        vmem(4, 16, 128), vmem(4, 96, 128), vmem(2, 12, 48, 128),
        sems(8), sems(8), sems(8), sems(8), sems(2, 2), sems(2, 2), sems(2, 8), sems(2, 8),
        sems(2, 2), sems(2, 2), sems(2, 8), sems(2, 8), sems(2, 8), sems(2, 8),
        sems(2, 2), sems(2, 2), sems(2, 11), sems(2, 11), sems(2, 11), sems(2, 11),
        sems(2), sems(4), vmem(2, 2, 3, 80, 128), sems(2), sems(2),
    ]
    return pl.pallas_call(
        kernel,
        out_shape=jax.ShapeDtypeStruct(image.shape, F32),
        in_specs=[pl.BlockSpec(memory_space=pl.ANY)] * 2,
        out_specs=pl.BlockSpec(memory_space=pl.ANY),
        scratch_shapes=scratch,
        compiler_params=pltpu.CompilerParams(
            collective_id=0, has_side_effects=True, vmem_limit_bytes=56 * 1024 * 1024
        ),
    )(image, labels)


def solution(mesh):
    placed = (P("gx", "gy", "gz"), P("gx", "gy", "gz"))
    return jax.shard_map(
        shards, mesh=mesh, in_specs=placed, out_specs=P("gx", "gy", "gz"), check_vma=False
    )
```
